256 devices in a mesh: row: 32 (over z_hi, x, core), col: 8 (over y, z_lo).
Axes of the slice: x: 4, y: 4, z: 8 (z_hi: 4, z_lo: 2; z = z_hi * 2 + z_lo), core: 2. Of those that a mesh axis runs over, the one named last changes fastest.
Arguments:
- row_features: bfloat16 [512, 256], P(('row', 'col')), may hold values from -6 to 6
- col_features: bfloat16 [2048, 256], P(('col', 'row')), may hold values from -6 to 6
- row_proj: bfloat16 [256, 64], replicated, may hold values from -0.375 to 0.375
- col_proj: bfloat16 [256, 64], replicated, may hold values from -0.375 to 0.375
- pair_weight: bfloat16 [2, 3, 3, 64, 64], replicated, may hold values from -0.1875 to 0.1875
- pair_bias: float32 [64], replicated, may hold values from -4 to 4
- conv_weight: bfloat16 [3, 3, 64, 64], replicated, may hold values from -0.25 to 0.25
- dilations: int32 [2], replicated, may hold values from 1 to 8, as said below
- cotangent: bfloat16 [64, 512, 2048], P(None, 'row', 'col'), may hold values from -6 to 6
Outputs:
- pair_out: bfloat16 [64, 512, 2048], P(None, 'row', 'col')
- grad_row_features: float32 [512, 256], P(('row', 'col'))
- grad_col_features: float32 [2048, 256], P(('col', 'row'))
- grad_row_proj: float32 [256, 64], replicated
- grad_col_proj: float32 [256, 64], replicated
- grad_pair_weight: float32 [2, 3, 3, 64, 64], replicated
- grad_pair_bias: float32 [64], replicated
- grad_conv_weight: float32 [3, 3, 64, 64], replicated
The draws below stay inside these ranges and needn't reach their ends.
Inputs may be any that keep to these rules, and one draw needn't show every extreme that they name: One of the two dilations equals 8.
All inputs are finite; a program needn't handle non-finite values.
Results may differ from the reference program's by a relative error of at most 0.0054.
Values may be sent and summed in bfloat16 or wider, within the bound.
A program may use at most 64 MiB of HBM per device.

```python
import jax
import jax.numpy as jnp
from jax import lax

CHANNELS = 256
PAIR_CHANNELS = 64
MAX_DILATION = 8
ROW_DEV = 16
ROW_BINS = 512
COL_BINS = 2048


def draw_dilations(key, part):
    rate_key, order_key = jax.random.split(jax.random.fold_in(key, 11))
    free_rate = jax.random.randint(rate_key, (), 1, MAX_DILATION + 1).astype(jnp.int32)
    order_bit = jax.random.randint(order_key, (), 0, 2).astype(jnp.int32)
    largest = jnp.full((), MAX_DILATION, jnp.int32)
    forward = jnp.stack([largest, free_rate])
    backward = jnp.stack([free_rate, largest])
    return jnp.where(order_bit == 1, backward, forward).astype(jnp.int32)


def steps_of(own_key, extent, pieces, least, high):
    def one(axis_at, blocks):
        heights = jax.random.uniform(jax.random.fold_in(jax.random.fold_in(own_key, 6), axis_at), (blocks,), jnp.float32, least / len(pieces), high / len(pieces))
        return jnp.repeat(jnp.exp(heights), extent[axis_at] // blocks).reshape((-1,) + (1,) * (len(extent) - axis_at - 1))

    gain = one(*pieces[0])
    for cut in pieces[1:]:
        gain = gain * one(*cut)
    return gain


def noise(rng, shape, spread, bound, cuts=(), kind=jnp.bfloat16):
    loudness = steps_of(rng, shape, cuts, -0.22, 0.18) if cuts else 1.0
    drawn = jax.random.normal(rng, shape, jnp.float32) * spread * loudness
    return jnp.minimum(jnp.maximum(drawn, -bound), bound).astype(kind)


def setup_inputs(seed: int = 0) -> dict:
    arg_keys = jax.random.split(jax.random.key(seed), 10)
    row_features = noise(arg_keys[0], (ROW_BINS, CHANNELS), 1.0, 6.0, ((0, 256),))
    col_features = noise(arg_keys[1], (COL_BINS, CHANNELS), 1.0, 6.0, ((0, 256),))
    row_proj = noise(arg_keys[2], (CHANNELS, PAIR_CHANNELS), CHANNELS ** -0.5, 0.375)
    col_proj = noise(arg_keys[3], (CHANNELS, PAIR_CHANNELS), CHANNELS ** -0.5, 0.375)
    pair_weight = noise(arg_keys[4], (2, 3, 3, PAIR_CHANNELS, PAIR_CHANNELS), (18 * PAIR_CHANNELS) ** -0.5, 0.1875)
    pair_bias = noise(arg_keys[5], (PAIR_CHANNELS,), 1.0, 4.0, (), jnp.float32)
    conv_weight = noise(arg_keys[6], (3, 3, PAIR_CHANNELS, PAIR_CHANNELS), (9 * PAIR_CHANNELS) ** -0.5, 0.25)
    dilations = draw_dilations(jax.random.fold_in(arg_keys[9], 71), 0)
    cotangent = noise(arg_keys[8], (PAIR_CHANNELS, ROW_BINS, COL_BINS), 1.0, 6.0, ((1, 32), (2, 8)))
    return dict(row_features=row_features, col_features=col_features, row_proj=row_proj, col_proj=col_proj, pair_weight=pair_weight, pair_bias=pair_bias, conv_weight=conv_weight, dilations=dilations, cotangent=cotangent)


def line_terms(padded, weights, dilation, count, offset):
    shifted = jnp.stack([lax.dynamic_slice_in_dim(padded, (offset + (tap_idx - 1) * dilation).astype(jnp.int32), count, 0) for tap_idx in range(3)])
    return jnp.einsum("kip,kqpo->qio", shifted.astype(jnp.float32), weights.astype(jnp.float32), precision=lax.Precision.HIGHEST)


def line_valid(first_cell, count, cell_limit, dilation):
    cells = first_cell + jnp.arange(count, dtype=jnp.int32)
    columns = [((cells + (tap_idx - 1) * dilation >= 0) & (cells + (tap_idx - 1) * dilation < cell_limit)) for tap_idx in range(3)]
    return jnp.stack(columns, axis=1).astype(jnp.float32)


def inside_mask(first_cell, count, cell_limit):
    cells = first_cell + jnp.arange(count, dtype=jnp.int32)
    return ((cells >= 0) & (cells < cell_limit)).astype(jnp.float32)


def pair_field(row_terms, col_terms, row_valid, col_valid, bias):
    from_rows = jnp.einsum("jq,qic->cij", col_valid, row_terms, precision=lax.Precision.HIGHEST)
    from_cols = jnp.einsum("ik,kjc->cij", row_valid, col_terms, precision=lax.Precision.HIGHEST)
    return from_rows + from_cols + bias[:, None, None]


def window_at(padded, row_index, col_index, rows, cols):
    anchor = jnp.zeros((), jnp.int32)
    return lax.dynamic_slice(padded, (anchor, row_index.astype(jnp.int32), col_index.astype(jnp.int32)), (padded.shape[0], rows, cols))


def conv_taps(padded, weight, dilation, rows, cols, margin):
    result = jnp.zeros((weight.shape[3], rows, cols), jnp.float32)
    for tap_row in range(3):
        for tap_col in range(3):
            window = window_at(padded, margin + (tap_row - 1) * dilation, margin + (tap_col - 1) * dilation, rows, cols)
            result = result + jnp.einsum("co,cij->oij", weight[tap_row, tap_col].astype(jnp.float32), window.astype(jnp.float32), precision=lax.Precision.HIGHEST)
    return result


def back_taps(padded, weight, dilation, rows, cols, margin):
    result = jnp.zeros((weight.shape[2], rows, cols), jnp.float32)
    for tap_row in range(3):
        for tap_col in range(3):
            window = window_at(padded, margin - (tap_row - 1) * dilation, margin - (tap_col - 1) * dilation, rows, cols)
            result = result + jnp.einsum("co,oij->cij", weight[tap_row, tap_col].astype(jnp.float32), window.astype(jnp.float32), precision=lax.Precision.HIGHEST)
    return result


def tap_grads(hidden_pad, grads, dilation, rows, cols, margin):
    stacked = []
    for tap_row in range(3):
        line_list = []
        for tap_col in range(3):
            window = window_at(hidden_pad, margin + (tap_row - 1) * dilation, margin + (tap_col - 1) * dilation, rows, cols)
            line_list.append(jnp.einsum("cij,oij->co", window.astype(jnp.float32), grads.astype(jnp.float32), precision=lax.Precision.HIGHEST))
        stacked.append(jnp.stack(line_list))
    return jnp.stack(stacked)


def reference(row_features, col_features, row_proj, col_proj, pair_weight, pair_bias, conv_weight, dilations, cotangent):
    first_rate = dilations[0]
    second_rate = dilations[1]
    margin = MAX_DILATION
    wide_pad = 2 * MAX_DILATION
    width = PAIR_CHANNELS
    rows_a = jnp.dot(row_features, row_proj, preferred_element_type=jnp.float32).astype(jnp.bfloat16)
    cols_b = jnp.dot(col_features, col_proj, preferred_element_type=jnp.float32).astype(jnp.bfloat16)
    a_pad = jnp.pad(rows_a, ((wide_pad, wide_pad), (0, 0)))
    b_pad = jnp.pad(cols_b, ((wide_pad, wide_pad), (0, 0)))
    row_terms = line_terms(a_pad, pair_weight[0], first_rate, ROW_BINS + 2 * margin, margin)
    col_terms = line_terms(b_pad, jnp.swapaxes(pair_weight[1], 0, 1), first_rate, COL_BINS + 2 * margin, margin)
    row_valid = line_valid(-margin, ROW_BINS + 2 * margin, ROW_BINS, first_rate)
    col_valid = line_valid(-margin, COL_BINS + 2 * margin, COL_BINS, first_rate)
    row_inside = inside_mask(-margin, ROW_BINS + 2 * margin, ROW_BINS)
    col_inside = inside_mask(-margin, COL_BINS + 2 * margin, COL_BINS)
    grad_pad = jnp.pad(cotangent, ((0, 0), (margin, margin), (margin, margin)))
    block_rows = ROW_DEV
    block_count = ROW_BINS // block_rows
    col_valid_own = col_valid[margin:margin + COL_BINS]

    def one_block(carry, block_index):
        conv_grad, bias_grad, col_sums = carry
        start_row = block_index * block_rows
        terms_here = lax.dynamic_slice_in_dim(row_terms, start_row, block_rows + 2 * margin, 1)
        valid_here = lax.dynamic_slice_in_dim(row_valid, start_row, block_rows + 2 * margin, 0)
        inside_here = lax.dynamic_slice_in_dim(row_inside, start_row, block_rows + 2 * margin, 0)
        pre_act = pair_field(terms_here, col_terms, valid_here, col_valid, pair_bias)
        hidden = (jax.nn.silu(pre_act) * inside_here[None, :, None] * col_inside[None, None, :]).astype(jnp.bfloat16)
        conv_mixed = conv_taps(hidden, conv_weight, second_rate, block_rows, COL_BINS, margin)
        hidden_own = hidden[:, margin:margin + block_rows, margin:margin + COL_BINS]
        output = (hidden_own.astype(jnp.float32) + conv_mixed).astype(jnp.bfloat16)
        grad_here = lax.dynamic_slice_in_dim(grad_pad, start_row, block_rows + 2 * margin, 1)
        grad_own = grad_here[:, margin:margin + block_rows, margin:margin + COL_BINS]
        d_hidden = grad_own.astype(jnp.float32) + back_taps(grad_here, conv_weight, second_rate, block_rows, COL_BINS, margin)
        conv_grad = conv_grad + tap_grads(hidden, grad_own, second_rate, block_rows, COL_BINS, margin)
        pre_own = pre_act[:, margin:margin + block_rows, margin:margin + COL_BINS]
        sigmoid_own = jax.nn.sigmoid(pre_own)
        d_wide = d_hidden * sigmoid_own * (1.0 + pre_own * (1.0 - sigmoid_own))
        bias_grad = bias_grad + jnp.sum(d_wide, axis=(1, 2))
        row_valid_own = valid_here[margin:margin + block_rows]
        row_part = jnp.einsum("jq,cij->qic", col_valid_own, d_wide, precision=lax.Precision.HIGHEST)
        col_sums = col_sums + jnp.einsum("ik,cij->kjc", row_valid_own, d_wide, precision=lax.Precision.HIGHEST)
        return (conv_grad, bias_grad, col_sums), (output, row_part)

    start_carry = (jnp.zeros((3, 3, width, width), jnp.float32), jnp.zeros((width,), jnp.float32), jnp.zeros((3, COL_BINS, width), jnp.float32))
    (conv_grad, bias_grad, col_sums), (outputs, row_parts) = lax.scan(one_block, start_carry, jnp.arange(block_count, dtype=jnp.int32))
    pair_out = jnp.moveaxis(outputs, 0, 1).reshape(width, ROW_BINS, COL_BINS)
    row_sums = jnp.moveaxis(row_parts, 0, 1).reshape(3, ROW_BINS, width)
    back_rows = jnp.einsum("qio,kqpo->kip", row_sums, pair_weight[0].astype(jnp.float32), precision=lax.Precision.HIGHEST)
    back_cols = jnp.einsum("kjo,kqpo->qjp", col_sums, pair_weight[1].astype(jnp.float32), precision=lax.Precision.HIGHEST)
    rows_back_pad = jnp.pad(back_rows, ((0, 0), (margin, margin), (0, 0)))
    cols_back_pad = jnp.pad(back_cols, ((0, 0), (margin, margin), (0, 0)))
    d_rows = sum(lax.dynamic_slice_in_dim(rows_back_pad[tap_idx], (margin - (tap_idx - 1) * first_rate).astype(jnp.int32), ROW_BINS, 0) for tap_idx in range(3))
    d_cols = sum(lax.dynamic_slice_in_dim(cols_back_pad[tap_idx], (margin - (tap_idx - 1) * first_rate).astype(jnp.int32), COL_BINS, 0) for tap_idx in range(3))
    d_rows = d_rows.astype(jnp.bfloat16)
    d_cols = d_cols.astype(jnp.bfloat16)
    grad_row_features = jnp.dot(d_rows, row_proj.T, preferred_element_type=jnp.float32)
    grad_col_features = jnp.dot(d_cols, col_proj.T, preferred_element_type=jnp.float32)
    grad_row_proj = jnp.dot(row_features.T, d_rows, preferred_element_type=jnp.float32)
    grad_col_proj = jnp.dot(col_features.T, d_cols, preferred_element_type=jnp.float32)
    row_shifted = jnp.stack([lax.dynamic_slice_in_dim(a_pad, (wide_pad + (tap_idx - 1) * first_rate).astype(jnp.int32), ROW_BINS, 0) for tap_idx in range(3)])
    col_shifted = jnp.stack([lax.dynamic_slice_in_dim(b_pad, (wide_pad + (tap_idx - 1) * first_rate).astype(jnp.int32), COL_BINS, 0) for tap_idx in range(3)])
    grad_row_pair = jnp.einsum("kip,qio->kqpo", row_shifted.astype(jnp.float32), row_sums, precision=lax.Precision.HIGHEST)
    grad_col_pair = jnp.einsum("qjp,kjo->kqpo", col_shifted.astype(jnp.float32), col_sums, precision=lax.Precision.HIGHEST)
    grad_pair_weight = jnp.stack([grad_row_pair, grad_col_pair])
    return (pair_out, grad_row_features, grad_col_features, grad_row_proj, grad_col_proj, grad_pair_weight, bias_grad, conv_grad)
```

```python
import functools

import jax
import jax.numpy as jnp
from jax import lax
from jax.experimental import pallas as pl
from jax.experimental.pallas import tpu as pltpu
from jax.sharding import PartitionSpec as P

MAX_DILATION = 8
MESH = pl.DeviceIdType.MESH
VMEM = pltpu.VMEM


def places():
    r = lax.axis_index("row")
    c = lax.axis_index("col")
    return r, c, r // 8, lax.rem(r // 2, 4), lax.rem(r, 2), c // 2, lax.rem(c, 2)


def device_at(z_hi, x, core, y, z_lo):
    return ((z_hi * 4 + x) * 2 + core, y * 2 + z_lo)


def signal(barrier, target):
    pl.semaphore_signal(barrier, inc=1, device_id=target, device_id_type=MESH)


def push(src, dst, send_sem, recv_sem, target):
    pltpu.make_async_remote_copy(
        src_ref=src,
        dst_ref=dst,
        send_sem=send_sem,
        recv_sem=recv_sem,
        device_id=target,
        device_id_type=MESH,
    ).start()


def await_bytes(ref, sem):
    pltpu.make_async_copy(ref, ref, sem).wait()


def gather_kernel(rf_ref, cf_ref, cot_ref, rows_ref, cols_ref, halo_ref, side_ref, pack, ssem, rsem):
    r, c, _, _, _, _, _ = places()
    up, down = lax.rem(r + 31, 32), lax.rem(r + 1, 32)
    left, right = lax.rem(c + 7, 8), lax.rem(c + 1, 8)
    barrier = pltpu.get_barrier_semaphore()

    @pl.loop(1, 32)
    def _(t):
        signal(barrier, (lax.rem(r + t, 32), c))

    @pl.loop(1, 8)
    def _(t):
        signal(barrier, (r, lax.rem(c + t, 8)))

    for r_to in (up, down):
        for c_to in (left, right):
            signal(barrier, (r_to, c_to))

    lane = lax.broadcasted_iota(jnp.int32, (64, 128), 1) // 8
    first = jnp.zeros((64, 128), jnp.float32)
    last = jnp.zeros((64, 128), jnp.float32)
    for i in range(16):
        head = cot_ref[i, :, 0:128].astype(jnp.float32)
        tail = cot_ref[i, :, 128:256].astype(jnp.float32)
        first = jnp.where(lane == i, pltpu.roll(head, 8 * i, 1) if i else head, first)
        last = jnp.where(lane == i, pltpu.roll(tail, (8 * i + 8) % 128, 1) if i < 15 else tail, last)
    pack[0] = first.astype(jnp.bfloat16)
    pack[1] = last.astype(jnp.bfloat16)
    rows_ref[1, c] = rf_ref[...]
    cols_ref[r + 2] = cf_ref[...]
    pl.semaphore_wait(barrier, 31 + 7 + 4)

    push(cot_ref.at[pl.ds(8, 8)], halo_ref.at[0], ssem.at[0], rsem.at[0], (down, c))
    push(cot_ref.at[pl.ds(0, 8)], halo_ref.at[1], ssem.at[1], rsem.at[1], (up, c))

    @pl.loop(1, 32)
    def _(t):
        push(cf_ref, cols_ref.at[r + 2], ssem.at[2], rsem.at[2], (lax.rem(r + t, 32), c))

    @pl.loop(1, 8)
    def _(t):
        push(rf_ref, rows_ref.at[1, c], ssem.at[3], rsem.at[3], (r, lax.rem(c + t, 8)))

    for slot, r_to in ((2, up), (1, r), (0, down)):
        push(pack.at[0], side_ref.at[1, slot], ssem.at[4], rsem.at[4], (r_to, left))
        push(pack.at[1], side_ref.at[0, slot], ssem.at[4], rsem.at[4], (r_to, right))

    await_bytes(rows_ref.at[1, pl.ds(0, 7)], rsem.at[3])
    push(rows_ref.at[1], rows_ref.at[0], ssem.at[5], rsem.at[5], (down, c))
    push(rows_ref.at[1], rows_ref.at[2], ssem.at[6], rsem.at[6], (up, c))
    await_bytes(cols_ref.at[pl.ds(2, 31)], rsem.at[2])
    push(cols_ref.at[pl.ds(2, 2)], cols_ref.at[pl.ds(34, 2)], ssem.at[7], rsem.at[7], (r, left))
    push(cols_ref.at[pl.ds(32, 2)], cols_ref.at[pl.ds(0, 2)], ssem.at[8], rsem.at[8], (r, right))

    await_bytes(halo_ref.at[0], rsem.at[0])
    await_bytes(halo_ref.at[1], rsem.at[1])
    await_bytes(side_ref, rsem.at[4])
    await_bytes(rows_ref.at[0], rsem.at[5])
    await_bytes(rows_ref.at[2], rsem.at[6])
    await_bytes(cols_ref.at[pl.ds(34, 2)], rsem.at[7])
    await_bytes(cols_ref.at[pl.ds(0, 2)], rsem.at[8])
    await_bytes(halo_ref.at[0], ssem.at[0])
    await_bytes(halo_ref.at[1], ssem.at[1])
    await_bytes(cols_ref.at[pl.ds(2, 31)], ssem.at[2])
    await_bytes(rows_ref.at[1, pl.ds(0, 7)], ssem.at[3])
    await_bytes(side_ref, ssem.at[4])
    await_bytes(rows_ref.at[0], ssem.at[5])
    await_bytes(rows_ref.at[2], ssem.at[6])
    await_bytes(cols_ref.at[pl.ds(34, 2)], ssem.at[7])
    await_bytes(cols_ref.at[pl.ds(0, 2)], ssem.at[8])


def gather_all(rf, cf, cot):
    vm = pl.BlockSpec(memory_space=VMEM)
    return pl.pallas_call(
        gather_kernel,
        out_shape=(
            jax.ShapeDtypeStruct((3, 8, 2, 256), jnp.float32),
            jax.ShapeDtypeStruct((36, 16, 128), jnp.bfloat16),
            jax.ShapeDtypeStruct((2, 8, 64, 256), jnp.bfloat16),
            jax.ShapeDtypeStruct((2, 3, 64, 128), jnp.bfloat16),
        ),
        in_specs=[vm] * 3,
        out_specs=(vm,) * 4,
        scratch_shapes=[
            VMEM((2, 64, 128), jnp.bfloat16),
            pltpu.SemaphoreType.DMA((9,)),
            pltpu.SemaphoreType.DMA((9,)),
        ],
        compiler_params=pltpu.CompilerParams(
            collective_id=1, has_side_effects=True, vmem_limit_bytes=40 << 20
        ),
        name="gather_all",
    )(rf, cf, cot)


def reduce_kernel(
    g_ref, c_ref, r_ref, out_ref, drow_ref, dcol_ref,
    g0, g1, gz, c0, c1, c2, r1, r2, red, halo, ssem, rsem,
):
    r, c, z_hi, x, core, y, z_lo = places()
    a = x * 4 + y
    z = z_hi * 2 + z_lo
    sibling = device_at(z_hi, x, 1 - core, y, z_lo)
    row_to = lax.rem(jnp.where(c < 4, r + 1, r + 31), 32)
    row_from = lax.rem(jnp.where(c < 4, r + 31, r + 1), 32)
    col_to = lax.rem(jnp.where(r < 16, c + 1, c + 7), 8)
    col_from = lax.rem(jnp.where(r < 16, c + 7, c + 1), 8)

    def plane(t):
        other = lax.rem(a + t, 16)
        return other, device_at(z_hi, other // 4, core, lax.rem(other, 4), z_lo)

    def along_z(t):
        other = lax.rem(z + t, 8)
        return device_at(other // 2, x, core, y, lax.rem(other, 2))

    barrier = pltpu.get_barrier_semaphore()
    signal(barrier, sibling)

    @pl.loop(1, 16)
    def _(t):
        signal(barrier, plane(t)[1])

    @pl.loop(1, 8)
    def _(t):
        signal(barrier, along_z(t))

    signal(barrier, (row_from, c))
    signal(barrier, (r, col_from))
    pl.semaphore_wait(barrier, 1 + 15 + 7 + 2)

    push(g_ref.at[1 - core], g0, ssem.at[0], rsem.at[0], sibling)
    push(c_ref.at[1 - core], c0, ssem.at[1], rsem.at[1], sibling)
    await_bytes(g0, rsem.at[0])
    red[...] = g_ref[core] + g0[...]

    @pl.loop(1, 16)
    def _(t):
        other, target = plane(t)
        push(red.at[other], g1.at[t], ssem.at[2], rsem.at[2], target)

    await_bytes(c0, rsem.at[1])
    c0[...] = c0[...] + c_ref[core]
    for t in range(1, 4):
        x_to = lax.rem(x + t, 4)
        push(c0.at[x_to], c1.at[t], ssem.at[3], rsem.at[3], device_at(z_hi, x_to, core, y, z_lo))
        y_to = lax.rem(y + t, 4)
        push(r_ref.at[y_to], r1.at[t], ssem.at[4], rsem.at[4], device_at(z_hi, x, core, y_to, z_lo))
    await_bytes(c1.at[pl.ds(1, 3)], rsem.at[3])
    await_bytes(r1.at[pl.ds(1, 3)], rsem.at[4])
    c1[0] = c0[x] + c1[1] + c1[2] + c1[3]
    r1[0] = r_ref[y] + r1[1] + r1[2] + r1[3]
    await_bytes(g1.at[pl.ds(1, 15)], rsem.at[2])
    gz[z] = red[a] + jnp.sum(g1[1:16], axis=0)

    @pl.loop(1, 8)
    def _(t):
        push(gz.at[z], gz.at[z], ssem.at[5], rsem.at[5], along_z(t))

    for t in range(1, 4):
        z_to = lax.rem(z_hi + t, 4)
        push(c1.at[0, z_to], c2.at[t], ssem.at[6], rsem.at[6], device_at(z_to, x, core, y, z_lo))
    push(r1.at[0, 1 - z_lo], r2.at[1], ssem.at[7], rsem.at[7], device_at(z_hi, x, core, y, 1 - z_lo))
    await_bytes(c2.at[pl.ds(1, 3)], rsem.at[6])
    await_bytes(r2.at[1], rsem.at[7])
    c2[0] = c1[0, z_hi] + c2[1] + c2[2] + c2[3]
    r2[0] = r1[0, z_lo] + r2[1]
    push(r2.at[0], r2.at[2], ssem.at[8], rsem.at[8], (row_to, c))
    push(c2.at[0], halo, ssem.at[9], rsem.at[9], (r, col_to))
    await_bytes(gz.at[pl.ds(0, 7)], rsem.at[5])
    out_ref[core, a] = jnp.sum(gz[...], axis=0)

    @pl.loop(1, 16)
    def _(t):
        push(out_ref.at[core, a], out_ref.at[core, a], ssem.at[10], rsem.at[10], plane(t)[1])

    await_bytes(r2.at[2], rsem.at[8])
    await_bytes(halo, rsem.at[9])
    drow_ref[...] = r2[0, :, 0:64] + r2[2, :, 64:128]
    dcol_ref[...] = c2[0, :, 0:64] + halo[:, 64:128]
    await_bytes(out_ref.at[core, pl.ds(0, 15)], rsem.at[10])
    push(out_ref.at[core], out_ref.at[core], ssem.at[11], rsem.at[11], sibling)
    await_bytes(out_ref.at[0], rsem.at[11])

    await_bytes(g0, ssem.at[0])
    await_bytes(c0, ssem.at[1])
    await_bytes(g1.at[pl.ds(1, 15)], ssem.at[2])
    await_bytes(c1.at[pl.ds(1, 3)], ssem.at[3])
    await_bytes(r1.at[pl.ds(1, 3)], ssem.at[4])
    await_bytes(gz.at[pl.ds(0, 7)], ssem.at[5])
    await_bytes(c2.at[pl.ds(1, 3)], ssem.at[6])
    await_bytes(r2.at[1], ssem.at[7])
    await_bytes(r2.at[2], ssem.at[8])
    await_bytes(halo, ssem.at[9])
    await_bytes(out_ref.at[core, pl.ds(0, 15)], ssem.at[10])
    await_bytes(out_ref.at[0], ssem.at[11])


def reduce_all(g, c, r):
    vm = pl.BlockSpec(memory_space=VMEM)
    f32 = jnp.float32
    return pl.pallas_call(
        reduce_kernel,
        out_shape=(
            jax.ShapeDtypeStruct((2, 16, 40, 128), f32),
            jax.ShapeDtypeStruct((2, 64), f32),
            jax.ShapeDtypeStruct((8, 64), f32),
        ),
        in_specs=[vm] * 3,
        out_specs=(vm,) * 3,
        scratch_shapes=[
            VMEM((16, 40, 128), f32),
            VMEM((16, 40, 128), f32),
            VMEM((8, 40, 128), f32),
            VMEM((4, 4, 8, 128), f32),
            VMEM((4, 4, 8, 128), f32),
            VMEM((4, 8, 128), f32),
            VMEM((4, 2, 2, 128), f32),
            VMEM((3, 2, 128), f32),
            VMEM((16, 40, 128), f32),
            VMEM((8, 128), f32),
            pltpu.SemaphoreType.DMA((12,)),
            pltpu.SemaphoreType.DMA((12,)),
        ],
        compiler_params=pltpu.CompilerParams(
            collective_id=2, has_side_effects=True, vmem_limit_bytes=40 << 20
        ),
        name="reduce_all",
    )(g, c, r)


def project(features, weight):
    return jnp.dot(features, weight, preferred_element_type=jnp.float32).astype(jnp.bfloat16)


def line_terms(padded, weights, dilation, count, offset):
    shifted = jnp.stack(
        [
            lax.dynamic_slice_in_dim(padded, offset + (tap_idx - 1) * dilation, count, 0)
            for tap_idx in range(3)
        ]
    )
    return jnp.einsum("kip,kqpo->qio", shifted, weights, preferred_element_type=jnp.float32)


def line_valid(first_cell, count, cell_limit, dilation):
    cells = first_cell + jnp.arange(count, dtype=jnp.int32)
    columns = [
        (cells + (tap_idx - 1) * dilation >= 0) & (cells + (tap_idx - 1) * dilation < cell_limit)
        for tap_idx in range(3)
    ]
    return jnp.stack(columns, axis=1).astype(jnp.float32)


def inside_mask(first_cell, count, cell_limit):
    cells = first_cell + jnp.arange(count, dtype=jnp.int32)
    return ((cells >= 0) & (cells < cell_limit)).astype(jnp.float32)


def pair_field(row_terms, col_terms, row_valid, col_valid, bias):
    from_rows = jnp.einsum("jq,qic->cij", col_valid, row_terms, precision=lax.Precision.HIGHEST)
    from_cols = jnp.einsum("ik,kjc->cij", row_valid, col_terms, precision=lax.Precision.HIGHEST)
    return from_rows + from_cols + bias[:, None, None]


def window_at(padded, row_index, col_index, rows, cols):
    anchor = jnp.zeros((), jnp.int32)
    return lax.dynamic_slice(padded, (anchor, row_index, col_index), (padded.shape[0], rows, cols))


def conv_taps(padded, weight, dilation, rows, cols, margin):
    result = jnp.zeros((weight.shape[3], rows, cols), jnp.float32)
    for tap_row in range(3):
        for tap_col in range(3):
            window = window_at(
                padded,
                margin + (tap_row - 1) * dilation,
                margin + (tap_col - 1) * dilation,
                rows,
                cols,
            )
            result = result + jnp.einsum(
                "co,cij->oij", weight[tap_row, tap_col], window, preferred_element_type=jnp.float32
            )
    return result


def back_taps(padded, weight, dilation, rows, cols, margin):
    result = jnp.zeros((weight.shape[2], rows, cols), jnp.float32)
    for tap_row in range(3):
        for tap_col in range(3):
            window = window_at(
                padded,
                margin - (tap_row - 1) * dilation,
                margin - (tap_col - 1) * dilation,
                rows,
                cols,
            )
            result = result + jnp.einsum(
                "co,oij->cij", weight[tap_row, tap_col], window, preferred_element_type=jnp.float32
            )
    return result


def tap_grads(hidden_pad, grads, dilation, rows, cols, margin):
    stacked = []
    for tap_row in range(3):
        line_list = []
        for tap_col in range(3):
            window = window_at(
                hidden_pad,
                margin + (tap_row - 1) * dilation,
                margin + (tap_col - 1) * dilation,
                rows,
                cols,
            )
            line_list.append(
                jnp.einsum("cij,oij->co", window, grads, preferred_element_type=jnp.float32)
            )
        stacked.append(jnp.stack(line_list))
    return jnp.stack(stacked)


def live_cells(first_cell, count, cell_limit):
    cells = first_cell + lax.broadcasted_iota(jnp.int32, (count, 256), 0)
    return (cells >= 0) & (cells < cell_limit)


def placed(value, offset, count):
    zeros = jnp.zeros((count, value.shape[1]), value.dtype)
    return lax.dynamic_update_slice_in_dim(zeros, value, offset, 0)


def shards(
    row_features,
    col_features,
    row_proj,
    col_proj,
    pair_weight,
    pair_bias,
    conv_weight,
    dilations,
    cotangent,
):
    first_rate = dilations[0]
    second_rate = dilations[1]
    margin = MAX_DILATION
    row_count = lax.axis_size("row")
    col_count = lax.axis_size("col")
    row_place = lax.axis_index("row")
    col_place = lax.axis_index("col")
    rows_here = cotangent.shape[1]
    cols_here = cotangent.shape[2]
    row_start = row_place * rows_here
    col_start = col_place * cols_here
    row_limit = rows_here * row_count
    col_limit = cols_here * col_count
    pad_reach = 2 * margin
    cot_t = jnp.swapaxes(cotangent, 0, 1)
    cf = jnp.concatenate([col_features[:, :128], col_features[:, 128:]], axis=0)
    row_f, col_f, halo, side = gather_all(row_features.astype(jnp.float32), cf, cot_t)
    row_f = row_f.reshape(48, 256)
    row_f = jnp.where(live_cells(row_start - pad_reach, 48, row_limit), row_f, 0.0).astype(jnp.bfloat16)
    col_f = jnp.concatenate([col_f[:, :8], col_f[:, 8:]], axis=2).reshape(288, 256)
    col_f = jnp.where(live_cells(col_start - pad_reach, 288, col_limit), col_f, 0)
    a_pad = project(row_f, row_proj)
    b_pad = project(col_f, col_proj)
    row_terms = line_terms(
        a_pad, pair_weight[0], first_rate, rows_here + 2 * margin, pad_reach - margin
    )
    col_terms = line_terms(
        b_pad,
        jnp.swapaxes(pair_weight[1], 0, 1),
        first_rate,
        cols_here + 2 * margin,
        pad_reach - margin,
    )
    row_valid = line_valid(row_start - margin, rows_here + 2 * margin, row_limit, first_rate)
    col_valid = line_valid(col_start - margin, cols_here + 2 * margin, col_limit, first_rate)
    pre_act = pair_field(row_terms, col_terms, row_valid, col_valid, pair_bias)
    row_inside = inside_mask(row_start - margin, rows_here + 2 * margin, row_limit)
    col_inside = inside_mask(col_start - margin, cols_here + 2 * margin, col_limit)
    hidden = (jax.nn.silu(pre_act) * row_inside[None, :, None] * col_inside[None, None, :]).astype(
        jnp.bfloat16
    )
    pre_own = pre_act[:, margin : margin + rows_here, margin : margin + cols_here]
    hidden_own = hidden[:, margin : margin + rows_here, margin : margin + cols_here]
    conv_mixed = conv_taps(hidden, conv_weight, second_rate, rows_here, cols_here, margin)
    pair_out = (hidden_own.astype(jnp.float32) + conv_mixed).astype(jnp.bfloat16)
    side = side.reshape(2, 3, 64, 16, 8)
    side = jnp.concatenate([side[:, 0, :, 8:], side[:, 1], side[:, 2, :, :8]], axis=2)
    halo = jnp.moveaxis(halo, 2, 1)
    grad_pad = jnp.concatenate([halo[0], cotangent, halo[1]], axis=1)
    grad_pad = jnp.concatenate([side[0], grad_pad, side[1]], axis=2)
    grad_pad = jnp.where(row_inside[None, :, None] * col_inside[None, None, :] > 0, grad_pad, 0)
    d_hidden = cotangent.astype(jnp.float32) + back_taps(
        grad_pad, conv_weight, second_rate, rows_here, cols_here, margin
    )
    conv_grad = tap_grads(hidden, cotangent, second_rate, rows_here, cols_here, margin)
    sigmoid_own = jax.nn.sigmoid(pre_own)
    d_pre = d_hidden * sigmoid_own * (1.0 + pre_own * (1.0 - sigmoid_own))
    bias_grad = jnp.sum(d_pre, axis=(1, 2))
    row_valid_own = line_valid(row_start, rows_here, row_limit, first_rate)
    col_valid_own = line_valid(col_start, cols_here, col_limit, first_rate)
    row_part = jnp.einsum("jq,cij->qic", col_valid_own, d_pre, precision=lax.Precision.HIGHEST)
    col_part = jnp.einsum("ik,cij->kjc", row_valid_own, d_pre, precision=lax.Precision.HIGHEST)
    high = lax.Precision.HIGHEST
    pair_wide = pair_weight.astype(jnp.float32)
    back_rows = jnp.einsum("qio,kqpo->kip", row_part, pair_wide[0], precision=high)
    back_cols = jnp.einsum("kjo,kqpo->qjp", col_part, pair_wide[1], precision=high)
    d_rows = sum(placed(back_rows[k], margin + (k - 1) * first_rate, rows_here + 2 * margin) for k in range(3))
    d_cols = sum(placed(back_cols[k], margin + (k - 1) * first_rate, cols_here + 2 * margin) for k in range(3))
    d_rows = jnp.where(row_inside[:, None] > 0, d_rows, 0.0)
    d_cols = jnp.where(col_inside[:, None] > 0, d_cols, 0.0)
    row_mid = row_f[margin : margin + 32].astype(jnp.float32)
    col_mid = col_f[margin : margin + 272].astype(jnp.float32)
    grad_row_proj = jnp.einsum("ic,ip->cp", row_mid, d_rows, precision=high)
    grad_col_proj = jnp.einsum("ic,ip->cp", col_mid, d_cols, precision=high)
    row_shifted = jnp.stack(
        [lax.dynamic_slice_in_dim(a_pad, pad_reach + (k - 1) * first_rate, rows_here, 0) for k in range(3)]
    ).astype(jnp.float32)
    col_shifted = jnp.stack(
        [lax.dynamic_slice_in_dim(b_pad, pad_reach + (k - 1) * first_rate, cols_here, 0) for k in range(3)]
    ).astype(jnp.float32)
    grad_row_pair = jnp.einsum("kip,qio->kqpo", row_shifted, row_part, precision=high)
    grad_col_pair = jnp.einsum("qjp,kjo->kqpo", col_shifted, col_part, precision=high)
    flat = [
        grad_row_proj.reshape(-1),
        grad_col_proj.reshape(-1),
        grad_row_pair.reshape(-1),
        grad_col_pair.reshape(-1),
        conv_grad.reshape(-1),
        bias_grad,
    ]
    packed = jnp.concatenate(flat)
    packed = jnp.pad(packed, (0, 163840 - packed.shape[0])).reshape(2, 16, 40, 128)
    main_c = d_cols[8:264].reshape(32, 8, 64)
    zero = jnp.zeros((30, 8, 64), jnp.float32)
    halo_c = jnp.concatenate([d_cols[None, 264:272], zero, d_cols[None, 0:8]])
    pieces_c = jnp.concatenate([main_c, halo_c], axis=2).reshape(4, 4, 2, 8, 128)
    pieces_c = jnp.transpose(pieces_c, (2, 1, 0, 3, 4))
    main_r = d_rows[8:24].reshape(8, 2, 64)
    halo_r = jnp.concatenate([d_rows[24:32], d_rows[0:8]]).reshape(8, 2, 64)
    pieces_r = jnp.concatenate([main_r, halo_r], axis=2).reshape(4, 2, 2, 128)
    total, own_rows, own_cols = reduce_all(packed, pieces_c, pieces_r)
    d_rows = own_rows.astype(jnp.bfloat16)
    d_cols = own_cols.astype(jnp.bfloat16)
    grad_row_features = jnp.dot(d_rows, row_proj.T, preferred_element_type=jnp.float32)
    grad_col_features = jnp.dot(d_cols, col_proj.T, preferred_element_type=jnp.float32)
    total = total.reshape(-1)
    return (
        pair_out,
        grad_row_features,
        grad_col_features,
        total[:16384].reshape(256, 64),
        total[16384:32768].reshape(256, 64),
        total[32768:106496].reshape(2, 3, 3, 64, 64),
        total[143360:143424],
        total[106496:143360].reshape(3, 3, 64, 64),
    )


def solution(mesh):
    return jax.shard_map(
        shards,
        mesh=mesh,
        in_specs=(
            P(("row", "col"), None),
            P(("col", "row"), None),
            P(),
            P(),
            P(),
            P(),
            P(),
            P(),
            P(None, "row", "col"),
        ),
        out_specs=(
            P(None, "row", "col"),
            P(("row", "col"), None),
            P(("col", "row"), None),
            P(),
            P(),
            P(),
            P(),
            P(),
        ),
        check_vma=False,
    )
```

```python
import functools

import jax
import jax.numpy as jnp
from jax import lax
from jax.experimental import pallas as pl
from jax.experimental.pallas import tpu as pltpu
from jax.sharding import PartitionSpec as P

MAX_DILATION = 8
MESH = pl.DeviceIdType.MESH
VMEM = pltpu.VMEM


def places():
    r = lax.axis_index("row")
    c = lax.axis_index("col")
    return r, c, r // 8, lax.rem(r // 2, 4), lax.rem(r, 2), c // 2, lax.rem(c, 2)


def device_at(z_hi, x, core, y, z_lo):
    return ((z_hi * 4 + x) * 2 + core, y * 2 + z_lo)


def signal(barrier, target):
    pl.semaphore_signal(barrier, inc=1, device_id=target, device_id_type=MESH)


def push(src, dst, send_sem, recv_sem, target):
    pltpu.make_async_remote_copy(
        src_ref=src,
        dst_ref=dst,
        send_sem=send_sem,
        recv_sem=recv_sem,
        device_id=target,
        device_id_type=MESH,
    ).start()


def await_bytes(ref, sem):
    pltpu.make_async_copy(ref, ref, sem).wait()


def gather_kernel(rf_ref, cf_ref, cot_ref, rows_ref, cols_ref, halo_ref, side_ref, pack, ssem, rsem):
    r, c, _, _, _, _, _ = places()
    up, down = lax.rem(r + 31, 32), lax.rem(r + 1, 32)
    left, right = lax.rem(c + 7, 8), lax.rem(c + 1, 8)
    barrier = pltpu.get_barrier_semaphore()

    @pl.loop(1, 32)
    def _(t):
        signal(barrier, (lax.rem(r + t, 32), c))

    @pl.loop(1, 8)
    def _(t):
        signal(barrier, (r, lax.rem(c + t, 8)))

    for r_to in (up, down):
        for c_to in (left, right):
            signal(barrier, (r_to, c_to))

    lane = lax.broadcasted_iota(jnp.int32, (64, 128), 1) // 8
    first = jnp.zeros((64, 128), jnp.float32)
    last = jnp.zeros((64, 128), jnp.float32)
    for i in range(16):
        head = cot_ref[i, :, 0:128].astype(jnp.float32)
        tail = cot_ref[i, :, 128:256].astype(jnp.float32)
        first = jnp.where(lane == i, pltpu.roll(head, 8 * i, 1) if i else head, first)
        last = jnp.where(lane == i, pltpu.roll(tail, (8 * i + 8) % 128, 1) if i < 15 else tail, last)
    pack[0] = first.astype(jnp.bfloat16)
    pack[1] = last.astype(jnp.bfloat16)
    rows_ref[1, c] = rf_ref[...]
    cols_ref[r + 2] = cf_ref[...]
    pl.semaphore_wait(barrier, 31 + 7 + 4)

    push(cot_ref.at[pl.ds(8, 8)], halo_ref.at[0], ssem.at[0], rsem.at[0], (down, c))
    push(cot_ref.at[pl.ds(0, 8)], halo_ref.at[1], ssem.at[1], rsem.at[1], (up, c))

    @pl.loop(1, 32)
    def _(t):
        push(cf_ref, cols_ref.at[r + 2], ssem.at[2], rsem.at[2], (lax.rem(r + t, 32), c))

    @pl.loop(1, 8)
    def _(t):
        push(rf_ref, rows_ref.at[1, c], ssem.at[3], rsem.at[3], (r, lax.rem(c + t, 8)))

    for slot, r_to in ((2, up), (1, r), (0, down)):
        push(pack.at[0], side_ref.at[1, slot], ssem.at[4], rsem.at[4], (r_to, left))
        push(pack.at[1], side_ref.at[0, slot], ssem.at[4], rsem.at[4], (r_to, right))

    await_bytes(rows_ref.at[1, pl.ds(0, 7)], rsem.at[3])
    push(rows_ref.at[1], rows_ref.at[0], ssem.at[5], rsem.at[5], (down, c))
    push(rows_ref.at[1], rows_ref.at[2], ssem.at[6], rsem.at[6], (up, c))
    await_bytes(cols_ref.at[pl.ds(2, 31)], rsem.at[2])
    push(cols_ref.at[pl.ds(2, 2)], cols_ref.at[pl.ds(34, 2)], ssem.at[7], rsem.at[7], (r, left))
    push(cols_ref.at[pl.ds(32, 2)], cols_ref.at[pl.ds(0, 2)], ssem.at[8], rsem.at[8], (r, right))

    await_bytes(halo_ref.at[0], rsem.at[0])
    await_bytes(halo_ref.at[1], rsem.at[1])
    await_bytes(side_ref, rsem.at[4])
    await_bytes(rows_ref.at[0], rsem.at[5])
    await_bytes(rows_ref.at[2], rsem.at[6])
    await_bytes(cols_ref.at[pl.ds(34, 2)], rsem.at[7])
    await_bytes(cols_ref.at[pl.ds(0, 2)], rsem.at[8])
    await_bytes(halo_ref.at[0], ssem.at[0])
    await_bytes(halo_ref.at[1], ssem.at[1])
    await_bytes(cols_ref.at[pl.ds(2, 31)], ssem.at[2])
    await_bytes(rows_ref.at[1, pl.ds(0, 7)], ssem.at[3])
    await_bytes(side_ref, ssem.at[4])
    await_bytes(rows_ref.at[0], ssem.at[5])
    await_bytes(rows_ref.at[2], ssem.at[6])
    await_bytes(cols_ref.at[pl.ds(34, 2)], ssem.at[7])
    await_bytes(cols_ref.at[pl.ds(0, 2)], ssem.at[8])


def gather_all(rf, cf, cot):
    vm = pl.BlockSpec(memory_space=VMEM)
    return pl.pallas_call(
        gather_kernel,
        out_shape=(
            jax.ShapeDtypeStruct((3, 8, 2, 256), jnp.float32),
            jax.ShapeDtypeStruct((36, 16, 128), jnp.bfloat16),
            jax.ShapeDtypeStruct((2, 8, 64, 256), jnp.bfloat16),
            jax.ShapeDtypeStruct((2, 3, 64, 128), jnp.bfloat16),
        ),
        in_specs=[vm] * 3,
        out_specs=(vm,) * 4,
        scratch_shapes=[
            VMEM((2, 64, 128), jnp.bfloat16),
            pltpu.SemaphoreType.DMA((9,)),
            pltpu.SemaphoreType.DMA((9,)),
        ],
        compiler_params=pltpu.CompilerParams(
            collective_id=1, has_side_effects=True, vmem_limit_bytes=40 << 20
        ),
        name="gather_all",
    )(rf, cf, cot)


def reduce_kernel(
    g_ref, c_ref, r_ref, out_ref, drow_ref, dcol_ref,
    g0, g1, gz, c0, c1, c2, r1, r2, red, halo, ssem, rsem,
):
    r, c, z_hi, x, core, y, z_lo = places()
    a = x * 4 + y
    z = z_hi * 2 + z_lo
    sibling = device_at(z_hi, x, 1 - core, y, z_lo)
    row_to = lax.rem(jnp.where(c < 4, r + 1, r + 31), 32)
    row_from = lax.rem(jnp.where(c < 4, r + 31, r + 1), 32)
    col_to = lax.rem(jnp.where(r < 16, c + 1, c + 7), 8)
    col_from = lax.rem(jnp.where(r < 16, c + 7, c + 1), 8)

    def plane(t):
        other = lax.rem(a + t, 16)
        return other, device_at(z_hi, other // 4, core, lax.rem(other, 4), z_lo)

    def along_z(t):
        other = lax.rem(z + t, 8)
        return device_at(other // 2, x, core, y, lax.rem(other, 2))

    barrier = pltpu.get_barrier_semaphore()
    signal(barrier, sibling)

    @pl.loop(1, 16)
    def _(t):
        signal(barrier, plane(t)[1])

    @pl.loop(1, 8)
    def _(t):
        signal(barrier, along_z(t))

    signal(barrier, (row_from, c))
    signal(barrier, (r, col_from))
    pl.semaphore_wait(barrier, 1 + 15 + 7 + 2)

    push(g_ref.at[1 - core], g0, ssem.at[0], rsem.at[0], sibling)
    push(c_ref.at[1 - core], c0, ssem.at[1], rsem.at[1], sibling)
    await_bytes(g0, rsem.at[0])
    red[...] = g_ref[core] + g0[...]

    @pl.loop(1, 16)
    def _(t):
        other, target = plane(t)
        push(red.at[other], g1.at[t], ssem.at[2], rsem.at[2], target)

    await_bytes(c0, rsem.at[1])
    c0[...] = c0[...] + c_ref[core]
    for t in range(1, 4):
        x_to = lax.rem(x + t, 4)
        push(c0.at[x_to], c1.at[t], ssem.at[3], rsem.at[3], device_at(z_hi, x_to, core, y, z_lo))
        y_to = lax.rem(y + t, 4)
        push(r_ref.at[y_to], r1.at[t], ssem.at[4], rsem.at[4], device_at(z_hi, x, core, y_to, z_lo))
    await_bytes(c1.at[pl.ds(1, 3)], rsem.at[3])
    await_bytes(r1.at[pl.ds(1, 3)], rsem.at[4])
    c1[0] = c0[x] + c1[1] + c1[2] + c1[3]
    r1[0] = r_ref[y] + r1[1] + r1[2] + r1[3]
    await_bytes(g1.at[pl.ds(1, 15)], rsem.at[2])
    gz[z] = red[a] + jnp.sum(g1[1:16], axis=0)

    @pl.loop(1, 8)
    def _(t):
        push(gz.at[z], gz.at[z], ssem.at[5], rsem.at[5], along_z(t))

    for t in range(1, 4):
        z_to = lax.rem(z_hi + t, 4)
        push(c1.at[0, z_to], c2.at[t], ssem.at[6], rsem.at[6], device_at(z_to, x, core, y, z_lo))
    push(r1.at[0, 1 - z_lo], r2.at[1], ssem.at[7], rsem.at[7], device_at(z_hi, x, core, y, 1 - z_lo))
    await_bytes(c2.at[pl.ds(1, 3)], rsem.at[6])
    await_bytes(r2.at[1], rsem.at[7])
    c2[0] = c1[0, z_hi] + c2[1] + c2[2] + c2[3]
    r2[0] = r1[0, z_lo] + r2[1]
    push(r2.at[0], r2.at[2], ssem.at[8], rsem.at[8], (row_to, c))
    push(c2.at[0], halo, ssem.at[9], rsem.at[9], (r, col_to))
    await_bytes(gz.at[pl.ds(0, 7)], rsem.at[5])
    out_ref[core, a] = jnp.sum(gz[...], axis=0)

    @pl.loop(1, 16)
    def _(t):
        push(out_ref.at[core, a], out_ref.at[core, a], ssem.at[10], rsem.at[10], plane(t)[1])

    await_bytes(r2.at[2], rsem.at[8])
    await_bytes(halo, rsem.at[9])
    drow_ref[...] = r2[0, :, 0:64] + r2[2, :, 64:128]
    dcol_ref[...] = c2[0, :, 0:64] + halo[:, 64:128]
    await_bytes(out_ref.at[core, pl.ds(0, 15)], rsem.at[10])
    push(out_ref.at[core], out_ref.at[core], ssem.at[11], rsem.at[11], sibling)
    await_bytes(out_ref.at[0], rsem.at[11])

    await_bytes(g0, ssem.at[0])
    await_bytes(c0, ssem.at[1])
    await_bytes(g1.at[pl.ds(1, 15)], ssem.at[2])
    await_bytes(c1.at[pl.ds(1, 3)], ssem.at[3])
    await_bytes(r1.at[pl.ds(1, 3)], ssem.at[4])
    await_bytes(gz.at[pl.ds(0, 7)], ssem.at[5])
    await_bytes(c2.at[pl.ds(1, 3)], ssem.at[6])
    await_bytes(r2.at[1], ssem.at[7])
    await_bytes(r2.at[2], ssem.at[8])
    await_bytes(halo, ssem.at[9])
    await_bytes(out_ref.at[core, pl.ds(0, 15)], ssem.at[10])
    await_bytes(out_ref.at[0], ssem.at[11])


def reduce_all(g, c, r):
    vm = pl.BlockSpec(memory_space=VMEM)
    f32 = jnp.float32
    return pl.pallas_call(
        reduce_kernel,
        out_shape=(
            jax.ShapeDtypeStruct((2, 16, 5, 8, 128), f32),
            jax.ShapeDtypeStruct((2, 64), f32),
            jax.ShapeDtypeStruct((8, 64), f32),
        ),
        in_specs=[vm] * 3,
        out_specs=(vm,) * 3,
        scratch_shapes=[
            VMEM((16, 5, 8, 128), f32),
            VMEM((16, 5, 8, 128), f32),
            VMEM((8, 5, 8, 128), f32),
            VMEM((4, 4, 8, 128), f32),
            VMEM((4, 4, 8, 128), f32),
            VMEM((4, 8, 128), f32),
            VMEM((4, 2, 2, 128), f32),
            VMEM((3, 2, 128), f32),
            VMEM((16, 5, 8, 128), f32),
            VMEM((8, 128), f32),
            pltpu.SemaphoreType.DMA((12,)),
            pltpu.SemaphoreType.DMA((12,)),
        ],
        compiler_params=pltpu.CompilerParams(
            collective_id=2, has_side_effects=True, vmem_limit_bytes=40 << 20
        ),
        name="reduce_all",
    )(g, c, r)


FAR = -1e9
F32 = jnp.float32
BF16 = jnp.bfloat16


def times(a, b):
    return jnp.dot(a, b, preferred_element_type=F32)


def times_t(a, b):
    return lax.dot_general(a, b, (((1,), (1,)), ((), ())), preferred_element_type=F32)


def halves(v):
    hi = v.astype(BF16)
    return hi, (v - hi.astype(F32)).astype(BF16)


def turned(v, back):
    n = v.shape[1]
    return pltpu.roll(v, lax.rem(n - back, n), 1)


def lanes(rows, n):
    return lax.broadcasted_iota(jnp.int32, (rows, n), 1)


def block_kernel(
    dil, rowf, colf, rproj, cproj, pw, bias, cw, cot, halo, side,
    out_ref, g_ref, c_ref, r_ref,
    fr, h3, c3, gs, vt, cs,
):
    d1 = dil[0]
    d2 = dil[1]
    r = lax.axis_index("row")
    c = lax.axis_index("col")
    row0 = r * 16
    col0 = c * 256

    fr[...] = jnp.zeros((128, 256), F32)
    for g in range(3):
        for n in range(8):
            fr[g * 16 + 2 * n : g * 16 + 2 * n + 2, :] = rowf[g, n]
    at = row0 - 16 + lax.broadcasted_iota(jnp.int32, (128, 256), 0)
    feat_r = jnp.where((at >= 0) & (at < 512), fr[...], 0.0).astype(BF16)
    wide = colf[...].astype(F32)
    feat_c = jnp.concatenate([wide[:, :8].reshape(288, 128), wide[:, 8:].reshape(288, 128)], axis=1)
    at = col0 - 16 + lax.broadcasted_iota(jnp.int32, (288, 256), 0)
    feat_c = jnp.where((at >= 0) & (at < 2048), feat_c, 0.0)
    feat_c = jnp.concatenate([feat_c, jnp.zeros((96, 256), F32)], axis=0).astype(BF16)
    a_t = times_t(rproj[...].T, feat_r).astype(BF16).astype(F32)
    b_t = times_t(cproj[...].T, feat_c).astype(BF16).astype(F32)

    def taps(v, offset):
        return jnp.concatenate([turned(v, offset + (k - 1) * d1) for k in range(3)], axis=0).astype(BF16)

    pw0 = jnp.concatenate(
        [jnp.concatenate([pw[0, k, q] for q in range(3)], axis=1) for k in range(3)], axis=0
    )
    pw1 = jnp.concatenate(
        [jnp.concatenate([pw[1, k, q] for k in range(3)], axis=1) for q in range(3)], axis=0
    )
    rt = times(pw0.T, taps(a_t, 8)) * 0.5
    ct = times(pw1.T, taps(b_t, 8)) * 0.5
    rt0, rt2 = rt[0:64], rt[128:192]
    rsum = rt0 + rt[64:128] + rt2
    bias_col = jnp.broadcast_to(bias[...] * 0.5, (8, 64)).T[:, 0:1]
    at = col0 - 8 + lanes(64, 384)
    base = ct[64:128] + bias_col + jnp.where((at >= 0) & (at < 2048), 0.0, FAR)
    sums = (base + ct[128:192], base + ct[0:64] + ct[128:192], base + ct[0:64])
    for case in range(3):
        for q in range(3):
            vt[case * 3 + q] = turned(sums[case], 8 + (q - 1) * d2)[:, 0:256]
    near, far = [], []
    for q in range(3):
        at = col0 + (q - 1) * d2 + lanes(1, 256)
        near.append(jnp.where(at - d1 < 0, 1.0, 0.0))
        far.append(jnp.where(at + d1 >= 2048, 1.0, 0.0))

    for e in range(32):
        i = row0 - 8 + e
        case = jnp.where(i - d1 < 0, 0, jnp.where(i + d1 >= 512, 2, 1))
        gate = jnp.where((i >= 0) & (i < 512), 0.0, FAR)
        all_e = rsum[:, e : e + 1] + gate
        rt0_e = rt0[:, e : e + 1]
        rt2_e = rt2[:, e : e + 1]
        for q in range(3):
            h = vt[case * 3 + q] + all_e - near[q] * rt0_e - far[q] * rt2_e
            t = jnp.tanh(h)
            h3[q * 64 : (q + 1) * 64, e * 256 : (e + 1) * 256] = (h + h * t).astype(BF16)
            if q == 1 and 8 <= e < 24:
                gs[:, (e - 8) * 256 : (e - 7) * 256] = 0.5 + 0.5 * t + h * (0.5 - 0.5 * t * t)

    lane = lanes(64, 128)
    for e in range(32):
        if e < 8:
            x0, x1, slot, n = halo[0, e, :, 0:128], halo[0, e, :, 128:256], 0, 8 + e
        elif e < 24:
            x0, x1, slot, n = cot[e - 8, :, 0:128], cot[e - 8, :, 128:256], 1, e - 8
        else:
            x0, x1, slot, n = halo[1, e - 24, :, 0:128], halo[1, e - 24, :, 128:256], 2, e - 24
        i = row0 - 8 + e
        ok = (i >= 0) & (i < 512)
        before = side[0, slot]
        after = side[1, slot]
        if slot != 1:
            keep = jnp.where(ok, 1.0, 0.0).astype(BF16)
            x0, x1 = x0 * keep, x1 * keep
        before = before * jnp.where(ok & (c > 0), 1.0, 0.0).astype(BF16)
        after = after * jnp.where(ok & (c < 7), 1.0, 0.0).astype(BF16)
        cols = slice(e * 256, e * 256 + 128)
        cols1 = slice(e * 256 + 128, e * 256 + 256)
        c3[64:128, cols] = x0
        c3[64:128, cols1] = x1
        r0 = pltpu.roll(x0, d2, 1)
        r1 = pltpu.roll(x1, d2, 1)
        rp = pltpu.roll(before, lax.rem(120 - 8 * n + d2 + 128, 128), 1)
        c3[128:192, cols] = jnp.where(lane < d2, rp, r0)
        c3[128:192, cols1] = jnp.where(lane < d2, r0, r1)
        l0 = pltpu.roll(x0, 128 - d2, 1)
        l1 = pltpu.roll(x1, 128 - d2, 1)
        rn = pltpu.roll(after, lax.rem(256 - 8 * n - d2, 128), 1)
        c3[0:64, cols] = jnp.where(lane >= 128 - d2, l1, l0)
        c3[0:64, cols1] = jnp.where(lane >= 128 - d2, rn, l1)

    wf = [cw[k].reshape(192, 64).T for k in range(3)]
    wb = [jnp.concatenate([cw[k, q] for q in range(3)], axis=1) for k in range(3)]
    live = [1.0 - near[1], None, 1.0 - far[1]]
    rs = [jnp.zeros((64, 128), F32) for _ in range(3)]
    gc = [jnp.zeros((64, 192), F32) for _ in range(3)]
    cs[...] = jnp.zeros((3, 64, 256), F32)
    for n in range(4):
        mixed = jnp.zeros((64, 1024), F32)
        back = jnp.zeros((64, 1024), F32)
        own = h3[64:128, 2048 + n * 1024 : 3072 + n * 1024]
        for k in range(3):
            ahead = pl.multiple_of((8 + (k - 1) * d2) * 256 + n * 1024, 256)
            behind = pl.multiple_of((8 - (k - 1) * d2) * 256 + n * 1024, 256)
            mixed = mixed + times(wf[k], h3[:, pl.ds(ahead, 1024)])
            grads = c3[:, pl.ds(behind, 1024)]
            back = back + times(wb[k], grads)
            gc[k] = gc[k] + times_t(own, grads)
        mixed = (own.astype(F32) + mixed).astype(BF16)
        for m in range(4):
            i = n * 4 + m
            span = slice(m * 256, (m + 1) * 256)
            out_ref[i] = mixed[:, span]
            d = (cot[i].astype(F32) + back[:, span]) * gs[:, i * 256 : (i + 1) * 256]
            cs[1] = cs[1] + d
            cs[0] = cs[0] + d * jnp.where(row0 + i - d1 >= 0, 1.0, 0.0)
            cs[2] = cs[2] + d * jnp.where(row0 + i + d1 < 512, 1.0, 0.0)
            for q in range(3):
                part = d if live[q] is None else d * live[q]
                rs[q] = jnp.where(lane == i, jnp.sum(part, axis=1, keepdims=True), rs[q])

    rs_hi, rs_lo = halves(jnp.concatenate(rs, axis=0))
    cs_all = cs[...].reshape(192, 256)
    cs_hi, cs_lo = halves(cs_all)
    br = times(pw0, rs_hi) + times(pw0, rs_lo)
    bc = times(pw1, cs_hi) + times(pw1, cs_lo)
    bc = jnp.concatenate([bc, jnp.zeros((192, 128), F32)], axis=1)
    dr = sum(pltpu.roll(br[k * 64 : (k + 1) * 64], 16 + (k - 1) * d1, 1) for k in range(3))
    dc = sum(pltpu.roll(bc[q * 64 : (q + 1) * 64], 16 + (q - 1) * d1, 1) for q in range(3))
    at = row0 - 16 + lane
    dr = jnp.where((at >= 0) & (at < 512), dr, 0.0)
    at = col0 - 16 + lanes(64, 384)
    dc = jnp.where((at >= 0) & (at < 2048), dc, 0.0)
    dr_hi, dr_lo = halves(dr)
    dc_hi, dc_lo = halves(dc)
    row_proj_g = (times(dr_hi, feat_r) + times(dr_lo, feat_r)).T
    col_proj_g = (times(dc_hi, feat_c) + times(dc_lo, feat_c)).T
    a_own = taps(a_t, 16)
    b_own = taps(b_t, 16)[:, 0:256]
    p0 = times_t(a_own, rs_hi) + times_t(a_own, rs_lo)
    p1 = times_t(b_own, cs_hi) + times_t(b_own, cs_lo)
    bias_g = jnp.broadcast_to(jnp.sum(cs[1], axis=1, keepdims=True), (64, 64)).T

    blocks = [row_proj_g[n * 64 : (n + 1) * 64] for n in range(4)]
    blocks += [col_proj_g[n * 64 : (n + 1) * 64] for n in range(4)]
    for k in range(3):
        for q in range(3):
            blocks.append(p0[k * 64 : (k + 1) * 64, q * 64 : (q + 1) * 64])
    for k in range(3):
        for q in range(3):
            blocks.append(p1[q * 64 : (q + 1) * 64, k * 64 : (k + 1) * 64])
    for k in range(3):
        for q in range(3):
            blocks.append(gc[k][:, q * 64 : (q + 1) * 64])
    blocks.append(bias_g)
    for b in range(18):
        g_ref[8 * b : 8 * b + 8] = jnp.concatenate([blocks[b], blocks[b + 18]], axis=1).reshape(8, 8, 128)
    g_ref[144:160] = jnp.zeros((16, 8, 128), F32)

    dr_p = dr.T
    dc_p = dc.T
    for n in range(32):
        z_hi, x, core = n // 8, (n // 2) % 4, n % 2
        if n == 0:
            extra = dc_p[272:280]
        elif n == 31:
            extra = dc_p[8:16]
        else:
            extra = jnp.zeros((8, 64), F32)
        c_ref[core * 16 + x * 4 + z_hi] = jnp.concatenate([dc_p[16 + 8 * n : 24 + 8 * n], extra], axis=1)
    for n in range(8):
        h = 32 + 2 * n if n < 4 else 2 * n
        r_ref[n] = jnp.concatenate([dr_p[16 + 2 * n : 18 + 2 * n], dr_p[h : h + 2]], axis=1)


def block(dil, *arrays):
    vm = pl.BlockSpec(memory_space=VMEM)
    return pl.pallas_call(
        block_kernel,
        out_shape=(
            jax.ShapeDtypeStruct((16, 64, 256), BF16),
            jax.ShapeDtypeStruct((160, 8, 128), F32),
            jax.ShapeDtypeStruct((32, 8, 128), F32),
            jax.ShapeDtypeStruct((8, 2, 128), F32),
        ),
        in_specs=[pl.BlockSpec(memory_space=pltpu.SMEM)] + [vm] * len(arrays),
        out_specs=(vm,) * 4,
        scratch_shapes=[
            VMEM((128, 256), F32),
            VMEM((192, 8192), BF16),
            VMEM((192, 8192), BF16),
            VMEM((64, 4096), F32),
            VMEM((9, 64, 256), F32),
            VMEM((3, 64, 256), F32),
        ],
        compiler_params=pltpu.CompilerParams(vmem_limit_bytes=40 << 20),
        name="block",
    )(dil, *arrays)


def shards(
    row_features,
    col_features,
    row_proj,
    col_proj,
    pair_weight,
    pair_bias,
    conv_weight,
    dilations,
    cotangent,
):
    cot_t = jnp.swapaxes(cotangent, 0, 1)
    cf = jnp.concatenate([col_features[:, :128], col_features[:, 128:]], axis=0)
    row_f, col_f, halo, side = gather_all(row_features.astype(F32), cf, cot_t)
    out_t, packed, pieces_c, pieces_r = block(
        dilations, row_f, col_f, row_proj, col_proj, pair_weight,
        pair_bias.reshape(1, 64), conv_weight, cot_t, halo, side,
    )
    total, own_rows, own_cols = reduce_all(
        packed.reshape(2, 16, 5, 8, 128),
        pieces_c.reshape(2, 4, 4, 8, 128),
        pieces_r.reshape(4, 2, 2, 128),
    )
    d_rows = own_rows.astype(BF16)
    d_cols = own_cols.astype(BF16)
    grad_row_features = times(d_rows, row_proj.T)
    grad_col_features = times(d_cols, col_proj.T)
    total = total.reshape(1280, 128)
    low, high = total[:, :64], total[:, 64:]
    pair = jnp.concatenate([low[512:1152], high[0:512]]).reshape(2, 3, 3, 64, 64)
    return (
        jnp.swapaxes(out_t, 0, 1),
        grad_row_features,
        grad_col_features,
        low[0:256],
        low[256:512],
        pair,
        high[1088],
        high[512:1088].reshape(3, 3, 64, 64),
    )


def solution(mesh):
    return jax.shard_map(
        shards,
        mesh=mesh,
        in_specs=(
            P(("row", "col"), None),
            P(("col", "row"), None),
            P(),
            P(),
            P(),
            P(),
            P(),
            P(),
            P(None, "row", "col"),
        ),
        out_specs=(
            P(None, "row", "col"),
            P(("row", "col"), None),
            P(("col", "row"), None),
            P(),
            P(),
            P(),
            P(),
            P(),
        ),
        check_vma=False,
    )
```

```python
import functools

import jax
import jax.numpy as jnp
from jax import lax
from jax.experimental import pallas as pl
from jax.experimental.pallas import tpu as pltpu
from jax.sharding import PartitionSpec as P

MAX_DILATION = 8
MESH = pl.DeviceIdType.MESH
VMEM = pltpu.VMEM


def places():
    r = lax.axis_index("row")
    c = lax.axis_index("col")
    return r, c, r // 8, lax.rem(r // 2, 4), lax.rem(r, 2), c // 2, lax.rem(c, 2)


def device_at(z_hi, x, core, y, z_lo):
    return ((z_hi * 4 + x) * 2 + core, y * 2 + z_lo)


def signal(barrier, target):
    pl.semaphore_signal(barrier, inc=1, device_id=target, device_id_type=MESH)


def push(src, dst, send_sem, recv_sem, target):
    pltpu.make_async_remote_copy(
        src_ref=src,
        dst_ref=dst,
        send_sem=send_sem,
        recv_sem=recv_sem,
        device_id=target,
        device_id_type=MESH,
    ).start()


def await_bytes(ref, sem):
    pltpu.make_async_copy(ref, ref, sem).wait()


FAR = -1e9
F32 = jnp.float32
BF16 = jnp.bfloat16


def times(a, b):
    return jnp.dot(a, b, preferred_element_type=F32)


def times_t(a, b):
    return lax.dot_general(a, b, (((1,), (1,)), ((), ())), preferred_element_type=F32)


def halves(v):
    hi = v.astype(BF16)
    return hi, (v - hi.astype(F32)).astype(BF16)


def turned(v, back):
    n = v.shape[1]
    return pltpu.roll(v, lax.rem(n - back, n), 1)


def lanes(rows, n):
    return lax.broadcasted_iota(jnp.int32, (rows, n), 1)


def main_kernel(
    dil, rf, cf, rproj, cproj, pw, bias, cw, cot,
    out_ref, sum_ref, drow_ref, dcol_ref,
    rows, cols, halo, side, pack, rf_wide, cf_tall,
    fr, h3, c3, gs, vt, cs,
    g, g0, red, g1, gz, pc, c0, c1, c2, c_halo, pr, r1, r2,
    ssem, rsem, ssem2, rsem2,
):
    d1 = dil[0]
    d2 = dil[1]
    r, c, z_hi, x, core, y, z_lo = places()
    row0 = r * 16
    col0 = c * 256
    up, down = lax.rem(r + 31, 32), lax.rem(r + 1, 32)
    left, right = lax.rem(c + 7, 8), lax.rem(c + 1, 8)
    a = x * 4 + y
    z = z_hi * 2 + z_lo
    sibling = device_at(z_hi, x, 1 - core, y, z_lo)

    def plane(t):
        other = lax.rem(a + t, 16)
        return other, device_at(z_hi, other // 4, core, lax.rem(other, 4), z_lo)

    def along_z(t):
        other = lax.rem(z + t, 8)
        return device_at(other // 2, x, core, y, lax.rem(other, 2))

    barrier = pltpu.get_barrier_semaphore()

    @pl.loop(1, 32)
    def _(t):
        signal(barrier, (lax.rem(r + t, 32), c))

    @pl.loop(1, 8)
    def _(t):
        signal(barrier, (r, lax.rem(c + t, 8)))

    for r_to in (up, down):
        for c_to in (left, right):
            signal(barrier, (r_to, c_to))
    for dx in range(1, 4):
        for dy in range(1, 4):
            signal(barrier, device_at(z_hi, lax.rem(x + dx, 4), core, lax.rem(y + dy, 4), z_lo))
    for dz in range(1, 4):
        signal(barrier, device_at(lax.rem(z_hi + dz, 4), x, core, y, 1 - z_lo))

    own_rf = rf[...].astype(F32)
    rf_wide[...] = own_rf
    rows[1, c] = own_rf
    own_cf = cf[...].astype(F32)
    own_cf = jnp.concatenate([own_cf[:, 0:128], own_cf[:, 128:256]], axis=0).astype(BF16)
    cf_tall[...] = own_cf
    cols[r + 2] = own_cf
    group = lanes(64, 128) // 8
    first = jnp.zeros((64, 128), jnp.float32)
    last = jnp.zeros((64, 128), jnp.float32)
    for i in range(16):
        head = cot[i, :, 0:128].astype(jnp.float32)
        tail = cot[i, :, 128:256].astype(jnp.float32)
        first = jnp.where(group == i, pltpu.roll(head, 8 * i, 1) if i else head, first)
        last = jnp.where(group == i, pltpu.roll(tail, (8 * i + 8) % 128, 1) if i < 15 else tail, last)
    pack[0] = first.astype(jnp.bfloat16)
    pack[1] = last.astype(jnp.bfloat16)
    pl.semaphore_wait(barrier, 31 + 7 + 4 + 9 + 3)

    @pl.loop(1, 32)
    def _(t):
        push(cf_tall, cols.at[r + 2], ssem.at[2], rsem.at[2], (lax.rem(r + t, 32), c))

    @pl.loop(1, 8)
    def _(t):
        push(rf_wide, rows.at[1, c], ssem.at[3], rsem.at[3], (r, lax.rem(c + t, 8)))

    for slot, r_to in ((2, up), (1, r), (0, down)):
        push(pack.at[0], side.at[1, slot], ssem.at[4], rsem.at[4], (r_to, left))
        push(pack.at[1], side.at[0, slot], ssem.at[4], rsem.at[4], (r_to, right))
    push(cot.at[pl.ds(8, 8)], halo.at[0], ssem.at[0], rsem.at[0], (down, c))
    push(cot.at[pl.ds(0, 8)], halo.at[1], ssem.at[1], rsem.at[1], (up, c))

    pw0 = jnp.concatenate(
        [jnp.concatenate([pw[0, k, q] for q in range(3)], axis=1) for k in range(3)], axis=0
    )
    pw1 = jnp.concatenate(
        [jnp.concatenate([pw[1, k, q] for k in range(3)], axis=1) for q in range(3)], axis=0
    )
    wf = [cw[k].reshape(192, 64).T for k in range(3)]
    wb = [jnp.concatenate([cw[k, q] for q in range(3)], axis=1) for k in range(3)]
    lane = lanes(64, 128)

    def taps(v, offset):
        return jnp.concatenate([turned(v, offset + (k - 1) * d1) for k in range(3)], axis=0).astype(BF16)

    def cotangent_row(e):
        if e < 8:
            x0, x1, slot, n = halo[0, e, :, 0:128], halo[0, e, :, 128:256], 0, 8 + e
        elif e < 24:
            x0, x1, slot, n = cot[e - 8, :, 0:128], cot[e - 8, :, 128:256], 1, e - 8
        else:
            x0, x1, slot, n = halo[1, e - 24, :, 0:128], halo[1, e - 24, :, 128:256], 2, e - 24
        i = row0 - 8 + e
        ok = (i >= 0) & (i < 512)
        before = side[0, slot]
        after = side[1, slot]
        if slot != 1:
            keep = jnp.where(ok, 1.0, 0.0).astype(BF16)
            x0, x1 = x0 * keep, x1 * keep
        before = before * jnp.where(ok & (c > 0), 1.0, 0.0).astype(BF16)
        after = after * jnp.where(ok & (c < 7), 1.0, 0.0).astype(BF16)
        low, high = slice(0, 128), slice(128, 256)
        c3[e, 64:128, low] = x0
        c3[e, 64:128, high] = x1
        r0 = pltpu.roll(x0, d2, 1)
        r1 = pltpu.roll(x1, d2, 1)
        rp = pltpu.roll(before, lax.rem(120 - 8 * n + d2 + 128, 128), 1)
        c3[e, 128:192, low] = jnp.where(lane < d2, rp, r0)
        c3[e, 128:192, high] = jnp.where(lane < d2, r0, r1)
        l0 = pltpu.roll(x0, 128 - d2, 1)
        l1 = pltpu.roll(x1, 128 - d2, 1)
        rn = pltpu.roll(after, lax.rem(256 - 8 * n - d2, 128), 1)
        c3[e, 0:64, low] = jnp.where(lane >= 128 - d2, l1, l0)
        c3[e, 0:64, high] = jnp.where(lane >= 128 - d2, rn, l1)

    await_bytes(rows.at[1, pl.ds(0, 7)], rsem.at[3])
    push(rows.at[1], rows.at[0], ssem.at[5], rsem.at[5], (down, c))
    push(rows.at[1], rows.at[2], ssem.at[6], rsem.at[6], (up, c))
    await_bytes(side, rsem.at[4])
    for e in range(8, 24):
        cotangent_row(e)
    await_bytes(cols.at[pl.ds(2, 31)], rsem.at[2])
    push(cols.at[pl.ds(2, 2)], cols.at[pl.ds(34, 2)], ssem.at[7], rsem.at[7], (r, left))
    push(cols.at[pl.ds(32, 2)], cols.at[pl.ds(0, 2)], ssem.at[8], rsem.at[8], (r, right))

    await_bytes(rows.at[0], rsem.at[5])
    await_bytes(rows.at[2], rsem.at[6])
    fr[...] = jnp.zeros((128, 256), F32)
    for m in range(3):
        for n in range(8):
            fr[m * 16 + 2 * n : m * 16 + 2 * n + 2, :] = rows[m, n]
    at = row0 - 16 + lax.broadcasted_iota(jnp.int32, (128, 256), 0)
    feat_r = jnp.where((at >= 0) & (at < 512), fr[...], 0.0).astype(BF16)
    a_t = times_t(rproj[...], feat_r).astype(BF16).astype(F32)
    rt = times(pw0.T, taps(a_t, 8)) * 0.5
    rt0, rt2 = rt[0:64], rt[128:192]
    rsum = rt0 + rt[64:128] + rt2
    bias_col = jnp.broadcast_to(bias[...] * 0.5, (8, 64)).T[:, 0:1]
    await_bytes(cols.at[pl.ds(34, 2)], rsem.at[7])
    await_bytes(cols.at[pl.ds(0, 2)], rsem.at[8])
    wide = cols[...].astype(F32)
    feat_c = jnp.concatenate([wide[:, :8].reshape(288, 128), wide[:, 8:].reshape(288, 128)], axis=1)
    at = col0 - 16 + lax.broadcasted_iota(jnp.int32, (288, 256), 0)
    feat_c = jnp.where((at >= 0) & (at < 2048), feat_c, 0.0)
    feat_c = jnp.concatenate([feat_c, jnp.zeros((96, 256), F32)], axis=0).astype(BF16)
    b_t = times_t(cproj[...], feat_c).astype(BF16).astype(F32)
    ct = times(pw1.T, taps(b_t, 8)) * 0.5
    at = col0 - 8 + lanes(64, 384)
    base = ct[64:128] + bias_col + jnp.where((at >= 0) & (at < 2048), 0.0, FAR)
    sums = (base + ct[128:192], base + ct[0:64] + ct[128:192], base + ct[0:64])
    for case in range(3):
        for q in range(3):
            vt[case * 3 + q] = turned(sums[case], 8 + (q - 1) * d2)[:, 0:256]
    near, far = [], []
    for q in range(3):
        at = col0 + (q - 1) * d2 + lanes(1, 256)
        near.append(jnp.where(at - d1 < 0, 1.0, 0.0))
        far.append(jnp.where(at + d1 >= 2048, 1.0, 0.0))

    for e in range(32):
        i = row0 - 8 + e
        case = jnp.where(i - d1 < 0, 0, jnp.where(i + d1 >= 512, 2, 1))
        gate = jnp.where((i >= 0) & (i < 512), 0.0, FAR)
        all_e = rsum[:, e : e + 1] + gate
        rt0_e = rt0[:, e : e + 1]
        rt2_e = rt2[:, e : e + 1]
        for q in range(3):
            h = vt[case * 3 + q] + all_e - near[q] * rt0_e - far[q] * rt2_e
            t = jnp.tanh(h)
            h3[e, q * 64 : (q + 1) * 64, :] = (h + h * t).astype(BF16)
            if q == 1 and 8 <= e < 24:
                gs[:, (e - 8) * 256 : (e - 7) * 256] = 0.5 + 0.5 * t + h * (0.5 - 0.5 * t * t)

    for i in range(16):
        mixed = h3[8 + i, 64:128, :].astype(F32)
        for k in range(3):
            mixed = mixed + times(wf[k], h3[8 + i + (k - 1) * d2])
        out_ref[i] = mixed.astype(BF16)

    await_bytes(halo.at[0], rsem.at[0])
    await_bytes(halo.at[1], rsem.at[1])
    for e in range(8):
        cotangent_row(e)
        cotangent_row(24 + e)
    live = [1.0 - near[1], None, 1.0 - far[1]]
    rs = [jnp.zeros((64, 128), F32) for _ in range(3)]
    gc = [jnp.zeros((64, 192), F32) for _ in range(3)]
    cs[...] = jnp.zeros((3, 64, 256), F32)
    for i in range(16):
        own = h3[8 + i, 64:128, :]
        d = cot[i].astype(F32)
        for k in range(3):
            grads = c3[8 + i - (k - 1) * d2]
            d = d + times(wb[k], grads)
            gc[k] = gc[k] + times_t(own, grads)
        d = d * gs[:, i * 256 : (i + 1) * 256]
        cs[1] = cs[1] + d
        cs[0] = cs[0] + d * jnp.where(row0 + i - d1 >= 0, 1.0, 0.0)
        cs[2] = cs[2] + d * jnp.where(row0 + i + d1 < 512, 1.0, 0.0)
        for q in range(3):
            part = d if live[q] is None else d * live[q]
            rs[q] = jnp.where(lane == i, jnp.sum(part, axis=1, keepdims=True), rs[q])

    rs_hi, rs_lo = halves(jnp.concatenate(rs, axis=0))
    cs_hi, cs_lo = halves(cs[...].reshape(192, 256))
    br = times(pw0, rs_hi) + times(pw0, rs_lo)
    bc = times(pw1, cs_hi) + times(pw1, cs_lo)
    bc = jnp.concatenate([bc, jnp.zeros((192, 128), F32)], axis=1)
    dr = sum(pltpu.roll(br[k * 64 : (k + 1) * 64], 16 + (k - 1) * d1, 1) for k in range(3))
    dc = sum(pltpu.roll(bc[q * 64 : (q + 1) * 64], 16 + (q - 1) * d1, 1) for q in range(3))
    at = row0 - 16 + lane
    dr = jnp.where((at >= 0) & (at < 512), dr, 0.0)
    at = col0 - 16 + lanes(64, 384)
    dc = jnp.where((at >= 0) & (at < 2048), dc, 0.0)
    dr_hi, dr_lo = halves(dr)
    dc_hi, dc_lo = halves(dc)
    row_proj_g = times(dr_hi, feat_r) + times(dr_lo, feat_r)
    col_proj_g = times(dc_hi, feat_c) + times(dc_lo, feat_c)
    a_own = taps(a_t, 16)
    b_own = taps(b_t, 16)[:, 0:256]
    p0 = times_t(a_own, rs_hi) + times_t(a_own, rs_lo)
    p1 = times_t(b_own, cs_hi) + times_t(b_own, cs_lo)
    bias_g = jnp.broadcast_to(jnp.sum(cs[1], axis=1, keepdims=True), (64, 64)).T

    strips = [p0[k * 64 : (k + 1) * 64] for k in range(3)]
    strips += [p1[q * 64 : (q + 1) * 64] for q in range(3)] + gc
    pairs = [row_proj_g[:, 0:128], row_proj_g[:, 128:256], col_proj_g[:, 0:128], col_proj_g[:, 128:256]]
    pairs += [strip[:, 0:128] for strip in strips]
    rest = [strip[:, 128:192] for strip in strips] + [bias_g]
    pairs += [jnp.concatenate([rest[2 * n], rest[2 * n + 1]], axis=1) for n in range(5)]
    for b in range(18):
        for j in range(4):
            tile = 4 * b + j
            g[tile // 36, (tile // 3) % 12, tile % 3] = pairs[b][16 * j : 16 * j + 16]

    dr_p = dr.T
    dc_p = dc.T
    for n in range(32):
        if n == 0:
            extra = dc_p[272:280]
        elif n == 31:
            extra = dc_p[8:16]
        else:
            extra = jnp.zeros((8, 64), F32)
        pc[n % 2, (n // 2) % 4, n // 8] = jnp.concatenate([dc_p[16 + 8 * n : 24 + 8 * n], extra], axis=1)
    for n in range(8):
        h = 32 + 2 * n if n < 4 else 2 * n
        pr[n // 2, n % 2] = jnp.concatenate([dr_p[16 + 2 * n : 18 + 2 * n], dr_p[h : h + 2]], axis=1)

    row_to = jnp.where(c < 4, down, up)
    col_to = jnp.where(r < 16, right, left)
    push(g.at[1 - core], g0, ssem2.at[0], rsem2.at[0], sibling)
    push(pc.at[1 - core], c0, ssem2.at[1], rsem2.at[1], sibling)
    for t in range(1, 4):
        y_to = lax.rem(y + t, 4)
        push(pr.at[y_to], r1.at[t], ssem2.at[4], rsem2.at[4], device_at(z_hi, x, core, y_to, z_lo))
    await_bytes(g0, rsem2.at[0])
    red[...] = (g[core] + g0[...]).astype(BF16)

    @pl.loop(1, 16)
    def _(t):
        other, target = plane(t)

        @pl.when(other < 12)
        def _():
            push(red.at[other], g1.at[t], ssem2.at[2], rsem2.at[2], target)

    await_bytes(c0, rsem2.at[1])
    c0[...] = c0[...] + pc[core]
    for t in range(1, 4):
        x_to = lax.rem(x + t, 4)
        push(c0.at[x_to], c1.at[t], ssem2.at[3], rsem2.at[3], device_at(z_hi, x_to, core, y, z_lo))
    await_bytes(r1.at[pl.ds(1, 3)], rsem2.at[4])
    r1[0] = pr[y] + r1[1] + r1[2] + r1[3]

    @pl.when(a < 12)
    def _():
        await_bytes(g1.at[pl.ds(1, 15)], rsem2.at[2])
        mine = g[core, a] + g0[a]
        for t in range(1, 16):
            mine = mine + g1[t].astype(F32)
        gz[z] = mine.astype(BF16)

        @pl.loop(1, 8)
        def _(t):
            push(gz.at[z], gz.at[z], ssem2.at[5], rsem2.at[5], along_z(t))

    await_bytes(c1.at[pl.ds(1, 3)], rsem2.at[3])
    c1[0] = c0[x] + c1[1] + c1[2] + c1[3]
    for t in range(1, 4):
        z_to = lax.rem(z_hi + t, 4)
        push(c1.at[0, z_to], c2.at[t], ssem2.at[6], rsem2.at[6], device_at(z_to, x, core, y, z_lo))
    push(r1.at[0, 1 - z_lo], r2.at[1], ssem2.at[7], rsem2.at[7], device_at(z_hi, x, core, y, 1 - z_lo))

    @pl.when(a < 12)
    def _():
        await_bytes(gz.at[pl.ds(0, 7)], rsem2.at[5])
        whole = gz[0].astype(F32)
        for t in range(1, 8):
            whole = whole + gz[t].astype(F32)
        sum_ref[core, a] = whole.astype(BF16)

        @pl.loop(1, 16)
        def _(t):
            push(sum_ref.at[core, a], sum_ref.at[core, a], ssem2.at[10], rsem2.at[10], plane(t)[1])

    await_bytes(c2.at[pl.ds(1, 3)], rsem2.at[6])
    await_bytes(r2.at[1], rsem2.at[7])
    c2[0] = c1[0, z_hi] + c2[1] + c2[2] + c2[3]
    r2[0] = r1[0, z_lo] + r2[1]
    push(r2.at[0], r2.at[2], ssem2.at[8], rsem2.at[8], (row_to, c))
    push(c2.at[0], c_halo, ssem2.at[9], rsem2.at[9], (r, col_to))
    await_bytes(r2.at[2], rsem2.at[8])
    await_bytes(c_halo, rsem2.at[9])
    drow_ref[...] = r2[0, :, 0:64] + r2[2, :, 64:128]
    dcol_ref[...] = c2[0, :, 0:64] + c_halo[:, 64:128]

    @pl.when(a < 12)
    def _():
        await_bytes(sum_ref.at[core, pl.ds(0, 11)], rsem2.at[10])

    @pl.when(a >= 12)
    def _():
        await_bytes(sum_ref.at[core], rsem2.at[10])

    push(sum_ref.at[core], sum_ref.at[core], ssem2.at[11], rsem2.at[11], sibling)
    await_bytes(sum_ref.at[0], rsem2.at[11])

    await_bytes(halo.at[0], ssem.at[0])
    await_bytes(halo.at[1], ssem.at[1])
    await_bytes(cols.at[pl.ds(2, 31)], ssem.at[2])
    await_bytes(rows.at[1, pl.ds(0, 7)], ssem.at[3])
    await_bytes(side, ssem.at[4])
    await_bytes(rows.at[0], ssem.at[5])
    await_bytes(rows.at[2], ssem.at[6])
    await_bytes(cols.at[pl.ds(34, 2)], ssem.at[7])
    await_bytes(cols.at[pl.ds(0, 2)], ssem.at[8])
    await_bytes(g0, ssem2.at[0])
    await_bytes(c0, ssem2.at[1])
    await_bytes(c1.at[pl.ds(1, 3)], ssem2.at[3])
    await_bytes(r1.at[pl.ds(1, 3)], ssem2.at[4])
    await_bytes(c2.at[pl.ds(1, 3)], ssem2.at[6])
    await_bytes(r2.at[1], ssem2.at[7])
    await_bytes(r2.at[2], ssem2.at[8])
    await_bytes(c_halo, ssem2.at[9])
    await_bytes(sum_ref.at[0], ssem2.at[11])

    @pl.when(a < 12)
    def _():
        await_bytes(g1.at[pl.ds(0, 11)], ssem2.at[2])
        await_bytes(gz.at[pl.ds(0, 7)], ssem2.at[5])
        await_bytes(g1.at[pl.ds(1, 15)], ssem2.at[10])

    @pl.when(a >= 12)
    def _():
        await_bytes(g1.at[pl.ds(0, 12)], ssem2.at[2])


def main(dil, *arrays):
    vm = pl.BlockSpec(memory_space=VMEM)
    return pl.pallas_call(
        main_kernel,
        out_shape=(
            jax.ShapeDtypeStruct((16, 64, 256), BF16),
            jax.ShapeDtypeStruct((2, 12, 3, 16, 128), BF16),
            jax.ShapeDtypeStruct((2, 64), F32),
            jax.ShapeDtypeStruct((8, 64), F32),
        ),
        in_specs=[pl.BlockSpec(memory_space=pltpu.SMEM)] + [vm] * len(arrays),
        out_specs=(vm,) * 4,
        scratch_shapes=[
            VMEM((3, 8, 2, 256), F32),
            VMEM((36, 16, 128), BF16),
            VMEM((2, 8, 64, 256), BF16),
            VMEM((2, 3, 64, 128), BF16),
            VMEM((2, 64, 128), BF16),
            VMEM((2, 256), F32),
            VMEM((16, 128), BF16),
            VMEM((128, 256), F32),
            VMEM((32, 192, 256), BF16),
            VMEM((32, 192, 256), BF16),
            VMEM((64, 4096), F32),
            VMEM((9, 64, 256), F32),
            VMEM((3, 64, 256), F32),
            VMEM((2, 12, 3, 16, 128), F32),
            VMEM((12, 3, 16, 128), F32),
            VMEM((12, 3, 16, 128), BF16),
            VMEM((16, 3, 16, 128), BF16),
            VMEM((8, 3, 16, 128), BF16),
            VMEM((2, 4, 4, 8, 128), F32),
            VMEM((4, 4, 8, 128), F32),
            VMEM((4, 4, 8, 128), F32),
            VMEM((4, 8, 128), F32),
            VMEM((8, 128), F32),
            VMEM((4, 2, 2, 128), F32),
            VMEM((4, 2, 2, 128), F32),
            VMEM((3, 2, 128), F32),
            pltpu.SemaphoreType.DMA((9,)),
            pltpu.SemaphoreType.DMA((9,)),
            pltpu.SemaphoreType.DMA((12,)),
            pltpu.SemaphoreType.DMA((12,)),
        ],
        compiler_params=pltpu.CompilerParams(
            collective_id=1, has_side_effects=True, vmem_limit_bytes=48 << 20
        ),
        name="main",
    )(dil, *arrays)


def finish_kernel(sums, drow, dcol, rproj, cproj, rp_ref, cp_ref, pair_ref, conv_ref, bias_ref, rf_ref, cf_ref):
    def pair_at(b):
        parts = []
        for j in range(4):
            tile = 4 * b + j
            parts.append(sums[tile // 36, (tile // 3) % 12, tile % 3].astype(F32))
        return jnp.concatenate(parts, axis=0)

    rp_ref[:, 0:128] = pair_at(0)
    rp_ref[:, 128:256] = pair_at(1)
    cp_ref[:, 0:128] = pair_at(2)
    cp_ref[:, 128:256] = pair_at(3)
    strips = [pair_at(4 + n) for n in range(9)]
    rest = []
    for n in range(5):
        both = pair_at(13 + n)
        rest += [both[:, 0:64], both[:, 64:128]]
    for k in range(3):
        for q in range(3):
            near = slice(q * 64, q * 64 + 64)
            pair_ref[k * 3 + q] = strips[k][:, near] if q < 2 else rest[k]
            pair_ref[9 + q * 3 + k] = strips[3 + k][:, near] if q < 2 else rest[3 + k]
            conv_ref[k * 3 + q] = strips[6 + k][:, near] if q < 2 else rest[6 + k]
    bias_ref[...] = rest[9][0:1]
    rf_ref[...] = times(drow[...].astype(BF16), rproj[...])
    cf_ref[...] = times(dcol[...].astype(BF16), cproj[...])


def finish(*arrays):
    vm = pl.BlockSpec(memory_space=VMEM)
    shapes = ((64, 256), (64, 256), (18, 64, 64), (9, 64, 64), (1, 64), (2, 256), (8, 256))
    return pl.pallas_call(
        finish_kernel,
        out_shape=tuple(jax.ShapeDtypeStruct(s, F32) for s in shapes),
        in_specs=[vm] * len(arrays),
        out_specs=(vm,) * len(shapes),
        compiler_params=pltpu.CompilerParams(vmem_limit_bytes=24 << 20),
        name="finish",
    )(*arrays)


def shards(
    row_features,
    col_features,
    row_proj,
    col_proj,
    pair_weight,
    pair_bias,
    conv_weight,
    dilations,
    cotangent,
):
    cot_t = jnp.swapaxes(cotangent, 0, 1)
    row_w, col_w = row_proj.T, col_proj.T
    out_t, sums, own_rows, own_cols = main(
        dilations, row_features, col_features, row_w, col_w, pair_weight,
        pair_bias.reshape(1, 64), conv_weight, cot_t,
    )
    row_g, col_g, pair, conv, bias, row_f, col_f = finish(sums, own_rows, own_cols, row_w, col_w)
    return (
        jnp.swapaxes(out_t, 0, 1),
        row_f,
        col_f,
        row_g.T,
        col_g.T,
        pair.reshape(2, 3, 3, 64, 64),
        bias.reshape(64),
        conv.reshape(3, 3, 64, 64),
    )


def solution(mesh):
    return jax.shard_map(
        shards,
        mesh=mesh,
        in_specs=(
            P(("row", "col"), None),
            P(("col", "row"), None),
            P(),
            P(),
            P(),
            P(),
            P(),
            P(),
            P(None, "row", "col"),
        ),
        out_specs=(
            P(None, "row", "col"),
            P(("row", "col"), None),
            P(("col", "row"), None),
            P(),
            P(),
            P(),
            P(),
            P(),
        ),
        check_vma=False,
    )
```

```python
import functools

import jax
import jax.numpy as jnp
from jax import lax
from jax.experimental import pallas as pl
from jax.experimental.pallas import tpu as pltpu
from jax.sharding import PartitionSpec as P

MAX_DILATION = 8
MESH = pl.DeviceIdType.MESH
VMEM = pltpu.VMEM


def places():
    r = lax.axis_index("row")
    c = lax.axis_index("col")
    return r, c, r // 8, lax.rem(r // 2, 4), lax.rem(r, 2), c // 2, lax.rem(c, 2)


def device_at(z_hi, x, core, y, z_lo):
    return ((z_hi * 4 + x) * 2 + core, y * 2 + z_lo)


def signal(barrier, target):
    pl.semaphore_signal(barrier, inc=1, device_id=target, device_id_type=MESH)


def push(src, dst, send_sem, recv_sem, target):
    pltpu.make_async_remote_copy(
        src_ref=src,
        dst_ref=dst,
        send_sem=send_sem,
        recv_sem=recv_sem,
        device_id=target,
        device_id_type=MESH,
    ).start()


def await_bytes(ref, sem):
    pltpu.make_async_copy(ref, ref, sem).wait()


FAR = -1e9
F32 = jnp.float32
BF16 = jnp.bfloat16


def times(a, b):
    return jnp.dot(a, b, preferred_element_type=F32)


def times_t(a, b):
    return lax.dot_general(a, b, (((1,), (1,)), ((), ())), preferred_element_type=F32)


def halves(v):
    hi = v.astype(BF16)
    return hi, (v - hi.astype(F32)).astype(BF16)


def turned(v, back):
    n = v.shape[1]
    return pltpu.roll(v, lax.rem(n - back, n), 1)


def lanes(rows, n):
    return lax.broadcasted_iota(jnp.int32, (rows, n), 1)


def main_kernel(
    dil, rf, cf, rproj, cproj, pw, bias, cw, cot,
    out_ref, sum_ref, drow_ref, dcol_ref,
    rows, cols, halo, side, pack, rf_wide, cf_tall,
    fr, h3, c3, gs, vt, st, cs,
    g, g0, red, g1, gz, pc, c0, c1, c2, c_halo, pr, r1, r2,
    ssem, rsem, ssem2, rsem2,
):
    d1 = dil[0]
    d2 = dil[1]
    r, c, z_hi, x, core, y, z_lo = places()
    row0 = r * 16
    col0 = c * 256
    up, down = lax.rem(r + 31, 32), lax.rem(r + 1, 32)
    left, right = lax.rem(c + 7, 8), lax.rem(c + 1, 8)
    a = x * 4 + y
    z = z_hi * 2 + z_lo
    sibling = device_at(z_hi, x, 1 - core, y, z_lo)

    def plane(t):
        other = lax.rem(a + t, 16)
        return other, device_at(z_hi, other // 4, core, lax.rem(other, 4), z_lo)

    def along_z(t):
        other = lax.rem(z + t, 8)
        return device_at(other // 2, x, core, y, lax.rem(other, 2))

    barrier = pltpu.get_barrier_semaphore()

    @pl.loop(1, 32)
    def _(t):
        signal(barrier, (lax.rem(r + t, 32), c))

    @pl.loop(1, 8)
    def _(t):
        signal(barrier, (r, lax.rem(c + t, 8)))

    for r_to in (up, down):
        for c_to in (left, right):
            signal(barrier, (r_to, c_to))
    for dx in range(1, 4):
        for dy in range(1, 4):
            signal(barrier, device_at(z_hi, lax.rem(x + dx, 4), core, lax.rem(y + dy, 4), z_lo))
    for dz in range(1, 4):
        signal(barrier, device_at(lax.rem(z_hi + dz, 4), x, core, y, 1 - z_lo))

    own_rf = rf[...].astype(F32)
    rf_wide[...] = own_rf
    rows[1, c] = own_rf
    own_cf = cf[...].astype(F32)
    own_cf = jnp.concatenate([own_cf[:, 0:128], own_cf[:, 128:256]], axis=0).astype(BF16)
    cf_tall[...] = own_cf
    cols[r + 2] = own_cf
    group = lanes(64, 128) // 8
    first = jnp.zeros((64, 128), jnp.float32)
    last = jnp.zeros((64, 128), jnp.float32)
    for i in range(16):
        head = cot[i, :, 0:128].astype(jnp.float32)
        tail = cot[i, :, 128:256].astype(jnp.float32)
        first = jnp.where(group == i, pltpu.roll(head, 8 * i, 1) if i else head, first)
        last = jnp.where(group == i, pltpu.roll(tail, (8 * i + 8) % 128, 1) if i < 15 else tail, last)
    pack[0] = first.astype(jnp.bfloat16)
    pack[1] = last.astype(jnp.bfloat16)
    pl.semaphore_wait(barrier, 31 + 7 + 4 + 9 + 3)

    @pl.loop(1, 32)
    def _(t):
        push(cf_tall, cols.at[r + 2], ssem.at[2], rsem.at[2], (lax.rem(r + t, 32), c))

    @pl.loop(1, 8)
    def _(t):
        push(rf_wide, rows.at[1, c], ssem.at[3], rsem.at[3], (r, lax.rem(c + t, 8)))

    for slot, r_to in ((2, up), (1, r), (0, down)):
        push(pack.at[0], side.at[1, slot], ssem.at[4], rsem.at[4], (r_to, left))
        push(pack.at[1], side.at[0, slot], ssem.at[4], rsem.at[4], (r_to, right))
    push(cot.at[pl.ds(8, 8)], halo.at[0], ssem.at[0], rsem.at[0], (down, c))
    push(cot.at[pl.ds(0, 8)], halo.at[1], ssem.at[1], rsem.at[1], (up, c))

    pw0 = jnp.concatenate(
        [jnp.concatenate([pw[0, k, q] for q in range(3)], axis=1) for k in range(3)], axis=0
    )
    pw1 = jnp.concatenate(
        [jnp.concatenate([pw[1, k, q] for k in range(3)], axis=1) for q in range(3)], axis=0
    )
    wf = [cw[k].reshape(192, 64).T for k in range(3)]
    wb = [jnp.concatenate([cw[k, q] for q in range(3)], axis=1) for k in range(3)]
    lane = lanes(64, 128)

    def taps(v, offset):
        return jnp.concatenate([turned(v, offset + (k - 1) * d1) for k in range(3)], axis=0).astype(BF16)

    def cotangent_row(e):
        if e < 8:
            x0, x1, slot, n = halo[0, e, :, 0:128], halo[0, e, :, 128:256], 0, 8 + e
        elif e < 24:
            x0, x1, slot, n = cot[e - 8, :, 0:128], cot[e - 8, :, 128:256], 1, e - 8
        else:
            x0, x1, slot, n = halo[1, e - 24, :, 0:128], halo[1, e - 24, :, 128:256], 2, e - 24
        i = row0 - 8 + e
        ok = (i >= 0) & (i < 512)
        before = side[0, slot]
        after = side[1, slot]
        if slot != 1:
            keep = jnp.where(ok, 1.0, 0.0).astype(BF16)
            x0, x1 = x0 * keep, x1 * keep
        before = before * jnp.where(ok & (c > 0), 1.0, 0.0).astype(BF16)
        after = after * jnp.where(ok & (c < 7), 1.0, 0.0).astype(BF16)
        low, high = slice(0, 128), slice(128, 256)
        c3[e, 64:128, low] = x0
        c3[e, 64:128, high] = x1
        r0 = pltpu.roll(x0, d2, 1)
        r1 = pltpu.roll(x1, d2, 1)
        rp = pltpu.roll(before, lax.rem(120 - 8 * n + d2 + 128, 128), 1)
        c3[e, 128:192, low] = jnp.where(lane < d2, rp, r0)
        c3[e, 128:192, high] = jnp.where(lane < d2, r0, r1)
        l0 = pltpu.roll(x0, 128 - d2, 1)
        l1 = pltpu.roll(x1, 128 - d2, 1)
        rn = pltpu.roll(after, lax.rem(256 - 8 * n - d2, 128), 1)
        c3[e, 0:64, low] = jnp.where(lane >= 128 - d2, l1, l0)
        c3[e, 0:64, high] = jnp.where(lane >= 128 - d2, rn, l1)

    await_bytes(rows.at[1, pl.ds(0, 7)], rsem.at[3])
    push(rows.at[1], rows.at[0], ssem.at[5], rsem.at[5], (down, c))
    push(rows.at[1], rows.at[2], ssem.at[6], rsem.at[6], (up, c))
    await_bytes(side, rsem.at[4])
    for e in range(8, 24):
        cotangent_row(e)
    await_bytes(cols.at[pl.ds(2, 31)], rsem.at[2])
    push(cols.at[pl.ds(2, 2)], cols.at[pl.ds(34, 2)], ssem.at[7], rsem.at[7], (r, left))
    push(cols.at[pl.ds(32, 2)], cols.at[pl.ds(0, 2)], ssem.at[8], rsem.at[8], (r, right))

    await_bytes(rows.at[0], rsem.at[5])
    await_bytes(rows.at[2], rsem.at[6])
    fr[...] = jnp.zeros((128, 256), F32)
    for m in range(3):
        for n in range(8):
            fr[m * 16 + 2 * n : m * 16 + 2 * n + 2, :] = rows[m, n]
    at = row0 - 16 + lax.broadcasted_iota(jnp.int32, (128, 256), 0)
    feat_r = jnp.where((at >= 0) & (at < 512), fr[...], 0.0).astype(BF16)
    a_t = times_t(rproj[...], feat_r).astype(BF16).astype(F32)
    rt = times(pw0.T, taps(a_t, 8)) * 0.5
    rt0, rt2 = rt[0:64], rt[128:192]
    rsum = rt0 + rt[64:128] + rt2
    bias_col = jnp.broadcast_to(bias[...] * 0.5, (8, 64)).T[:, 0:1]
    await_bytes(cols.at[pl.ds(34, 2)], rsem.at[7])
    await_bytes(cols.at[pl.ds(0, 2)], rsem.at[8])
    wide = cols[...].astype(F32)
    feat_c = jnp.concatenate([wide[:, :8].reshape(288, 128), wide[:, 8:].reshape(288, 128)], axis=1)
    at = col0 - 16 + lax.broadcasted_iota(jnp.int32, (288, 256), 0)
    feat_c = jnp.where((at >= 0) & (at < 2048), feat_c, 0.0)
    feat_c = jnp.concatenate([feat_c, jnp.zeros((96, 256), F32)], axis=0).astype(BF16)
    b_t = times_t(cproj[...], feat_c).astype(BF16).astype(F32)
    ct = times(pw1.T, taps(b_t, 8)) * 0.5
    at = col0 - 8 + lanes(64, 384)
    base = ct[64:128] + bias_col + jnp.where((at >= 0) & (at < 2048), 0.0, FAR)
    sums = (base + ct[128:192], base + ct[0:64] + ct[128:192], base + ct[0:64])
    for case in range(3):
        st[case] = sums[case]
        vt[case * 3 + 1] = turned(sums[case], 8)[:, 0:256]
    near, far = [], []
    for q in range(3):
        at = col0 + (q - 1) * d2 + lanes(1, 256)
        near.append(jnp.where(at - d1 < 0, 1.0, 0.0))
        far.append(jnp.where(at + d1 >= 2048, 1.0, 0.0))

    def hidden_row(e, taps_here):
        i = row0 - 8 + e
        case = jnp.where(i - d1 < 0, 0, jnp.where(i + d1 >= 512, 2, 1))
        gate = jnp.where((i >= 0) & (i < 512), 0.0, FAR)
        all_e = rsum[:, e : e + 1] + gate
        rt0_e = rt0[:, e : e + 1]
        rt2_e = rt2[:, e : e + 1]
        for q in taps_here:
            h = vt[case * 3 + q] + all_e - near[q] * rt0_e - far[q] * rt2_e
            t = jnp.tanh(h)
            h3[e, q * 64 : (q + 1) * 64, :] = (h + h * t).astype(BF16)
            if q == 1 and 8 <= e < 24:
                gs[:, (e - 8) * 256 : (e - 7) * 256] = 0.5 + 0.5 * t + h * (0.5 - 0.5 * t * t)

    for e in range(8, 24):
        hidden_row(e, (1,))

    await_bytes(halo.at[0], rsem.at[0])
    await_bytes(halo.at[1], rsem.at[1])
    for e in range(8):
        cotangent_row(e)
        cotangent_row(24 + e)
    live = [1.0 - near[1], None, 1.0 - far[1]]
    rs = [jnp.zeros((64, 128), F32) for _ in range(3)]
    gc = [jnp.zeros((64, 192), F32) for _ in range(3)]
    cs[...] = jnp.zeros((3, 64, 256), F32)
    for i in range(16):
        own = h3[8 + i, 64:128, :]
        d = cot[i].astype(F32)
        for k in range(3):
            grads = c3[8 + i - (k - 1) * d2]
            d = d + times(wb[k], grads)
            gc[k] = gc[k] + times_t(own, grads)
        d = d * gs[:, i * 256 : (i + 1) * 256]
        cs[1] = cs[1] + d
        cs[0] = cs[0] + d * jnp.where(row0 + i - d1 >= 0, 1.0, 0.0)
        cs[2] = cs[2] + d * jnp.where(row0 + i + d1 < 512, 1.0, 0.0)
        for q in range(3):
            part = d if live[q] is None else d * live[q]
            rs[q] = jnp.where(lane == i, jnp.sum(part, axis=1, keepdims=True), rs[q])

    rs_hi, rs_lo = halves(jnp.concatenate(rs, axis=0))
    cs_hi, cs_lo = halves(cs[...].reshape(192, 256))
    br = times(pw0, rs_hi) + times(pw0, rs_lo)
    bc = times(pw1, cs_hi) + times(pw1, cs_lo)
    bc = jnp.concatenate([bc, jnp.zeros((192, 128), F32)], axis=1)
    dr = sum(pltpu.roll(br[k * 64 : (k + 1) * 64], 16 + (k - 1) * d1, 1) for k in range(3))
    dc = sum(pltpu.roll(bc[q * 64 : (q + 1) * 64], 16 + (q - 1) * d1, 1) for q in range(3))
    at = row0 - 16 + lane
    dr = jnp.where((at >= 0) & (at < 512), dr, 0.0)
    at = col0 - 16 + lanes(64, 384)
    dc = jnp.where((at >= 0) & (at < 2048), dc, 0.0)
    dr_hi, dr_lo = halves(dr)
    dc_hi, dc_lo = halves(dc)
    row_proj_g = times(dr_hi, feat_r) + times(dr_lo, feat_r)
    col_proj_g = times(dc_hi, feat_c) + times(dc_lo, feat_c)
    a_own = taps(a_t, 16)
    b_own = taps(b_t, 16)[:, 0:256]
    p0 = times_t(a_own, rs_hi) + times_t(a_own, rs_lo)
    p1 = times_t(b_own, cs_hi) + times_t(b_own, cs_lo)
    bias_g = jnp.broadcast_to(jnp.sum(cs[1], axis=1, keepdims=True), (64, 64)).T

    strips = [p0[k * 64 : (k + 1) * 64] for k in range(3)]
    strips += [p1[q * 64 : (q + 1) * 64] for q in range(3)] + gc
    pairs = [row_proj_g[:, 0:128], row_proj_g[:, 128:256], col_proj_g[:, 0:128], col_proj_g[:, 128:256]]
    pairs += [strip[:, 0:128] for strip in strips]
    rest = [strip[:, 128:192] for strip in strips] + [bias_g]
    pairs += [jnp.concatenate([rest[2 * n], rest[2 * n + 1]], axis=1) for n in range(5)]
    for b in range(18):
        for j in range(4):
            tile = 4 * b + j
            g[tile // 36, (tile // 3) % 12, tile % 3] = pairs[b][16 * j : 16 * j + 16]

    dr_p = dr.T
    dc_p = dc.T
    for n in range(32):
        if n == 0:
            extra = dc_p[272:280]
        elif n == 31:
            extra = dc_p[8:16]
        else:
            extra = jnp.zeros((8, 64), F32)
        pc[n % 2, (n // 2) % 4, n // 8] = jnp.concatenate([dc_p[16 + 8 * n : 24 + 8 * n], extra], axis=1)
    for n in range(8):
        h = 32 + 2 * n if n < 4 else 2 * n
        pr[n // 2, n % 2] = jnp.concatenate([dr_p[16 + 2 * n : 18 + 2 * n], dr_p[h : h + 2]], axis=1)

    row_to = jnp.where(c < 4, down, up)
    col_to = jnp.where(r < 16, right, left)
    push(g.at[1 - core], g0, ssem2.at[0], rsem2.at[0], sibling)
    push(pc.at[1 - core], c0, ssem2.at[1], rsem2.at[1], sibling)
    for t in range(1, 4):
        y_to = lax.rem(y + t, 4)
        push(pr.at[y_to], r1.at[t], ssem2.at[4], rsem2.at[4], device_at(z_hi, x, core, y_to, z_lo))
    await_bytes(g0, rsem2.at[0])
    red[...] = (g[core] + g0[...]).astype(BF16)

    @pl.loop(1, 16)
    def _(t):
        other, target = plane(t)

        @pl.when(other < 12)
        def _():
            push(red.at[other], g1.at[t], ssem2.at[2], rsem2.at[2], target)

    await_bytes(c0, rsem2.at[1])
    c0[...] = c0[...] + pc[core]
    for t in range(1, 4):
        x_to = lax.rem(x + t, 4)
        push(c0.at[x_to], c1.at[t], ssem2.at[3], rsem2.at[3], device_at(z_hi, x_to, core, y, z_lo))
    for case in range(3):
        for q in (0, 2):
            vt[case * 3 + q] = turned(st[case], 8 + (q - 1) * d2)[:, 0:256]
    for e in range(32):
        hidden_row(e, (0, 2) if 8 <= e < 24 else (0, 1, 2))

    await_bytes(r1.at[pl.ds(1, 3)], rsem2.at[4])
    r1[0] = pr[y] + r1[1] + r1[2] + r1[3]

    @pl.when(a < 12)
    def _():
        await_bytes(g1.at[pl.ds(1, 15)], rsem2.at[2])
        mine = g[core, a] + g0[a]
        for t in range(1, 16):
            mine = mine + g1[t].astype(F32)
        gz[z] = mine.astype(BF16)

        @pl.loop(1, 8)
        def _(t):
            push(gz.at[z], gz.at[z], ssem2.at[5], rsem2.at[5], along_z(t))

    await_bytes(c1.at[pl.ds(1, 3)], rsem2.at[3])
    c1[0] = c0[x] + c1[1] + c1[2] + c1[3]
    for t in range(1, 4):
        z_to = lax.rem(z_hi + t, 4)
        push(c1.at[0, z_to], c2.at[t], ssem2.at[6], rsem2.at[6], device_at(z_to, x, core, y, z_lo))
    push(r1.at[0, 1 - z_lo], r2.at[1], ssem2.at[7], rsem2.at[7], device_at(z_hi, x, core, y, 1 - z_lo))

    for i in range(16):
        mixed = h3[8 + i, 64:128, :].astype(F32)
        for k in range(3):
            mixed = mixed + times(wf[k], h3[8 + i + (k - 1) * d2])
        out_ref[i] = mixed.astype(BF16)

    @pl.when(a < 12)
    def _():
        await_bytes(gz.at[pl.ds(0, 7)], rsem2.at[5])
        whole = gz[0].astype(F32)
        for t in range(1, 8):
            whole = whole + gz[t].astype(F32)
        sum_ref[core, a] = whole.astype(BF16)

        @pl.loop(1, 16)
        def _(t):
            push(sum_ref.at[core, a], sum_ref.at[core, a], ssem2.at[10], rsem2.at[10], plane(t)[1])

    await_bytes(c2.at[pl.ds(1, 3)], rsem2.at[6])
    await_bytes(r2.at[1], rsem2.at[7])
    c2[0] = c1[0, z_hi] + c2[1] + c2[2] + c2[3]
    r2[0] = r1[0, z_lo] + r2[1]
    push(r2.at[0], r2.at[2], ssem2.at[8], rsem2.at[8], (row_to, c))
    push(c2.at[0], c_halo, ssem2.at[9], rsem2.at[9], (r, col_to))
    await_bytes(r2.at[2], rsem2.at[8])
    await_bytes(c_halo, rsem2.at[9])
    drow_ref[...] = r2[0, :, 0:64] + r2[2, :, 64:128]
    dcol_ref[...] = c2[0, :, 0:64] + c_halo[:, 64:128]

    @pl.when(a < 12)
    def _():
        await_bytes(sum_ref.at[core, pl.ds(0, 11)], rsem2.at[10])

    @pl.when(a >= 12)
    def _():
        await_bytes(sum_ref.at[core], rsem2.at[10])

    push(sum_ref.at[core], sum_ref.at[core], ssem2.at[11], rsem2.at[11], sibling)
    await_bytes(sum_ref.at[0], rsem2.at[11])

    await_bytes(halo.at[0], ssem.at[0])
    await_bytes(halo.at[1], ssem.at[1])
    await_bytes(cols.at[pl.ds(2, 31)], ssem.at[2])
    await_bytes(rows.at[1, pl.ds(0, 7)], ssem.at[3])
    await_bytes(side, ssem.at[4])
    await_bytes(rows.at[0], ssem.at[5])
    await_bytes(rows.at[2], ssem.at[6])
    await_bytes(cols.at[pl.ds(34, 2)], ssem.at[7])
    await_bytes(cols.at[pl.ds(0, 2)], ssem.at[8])
    await_bytes(g0, ssem2.at[0])
    await_bytes(c0, ssem2.at[1])
    await_bytes(c1.at[pl.ds(1, 3)], ssem2.at[3])
    await_bytes(r1.at[pl.ds(1, 3)], ssem2.at[4])
    await_bytes(c2.at[pl.ds(1, 3)], ssem2.at[6])
    await_bytes(r2.at[1], ssem2.at[7])
    await_bytes(r2.at[2], ssem2.at[8])
    await_bytes(c_halo, ssem2.at[9])
    await_bytes(sum_ref.at[0], ssem2.at[11])

    @pl.when(a < 12)
    def _():
        await_bytes(g1.at[pl.ds(0, 11)], ssem2.at[2])
        await_bytes(gz.at[pl.ds(0, 7)], ssem2.at[5])
        await_bytes(g1.at[pl.ds(1, 15)], ssem2.at[10])

    @pl.when(a >= 12)
    def _():
        await_bytes(g1.at[pl.ds(0, 12)], ssem2.at[2])


def main(dil, *arrays):
    vm = pl.BlockSpec(memory_space=VMEM)
    return pl.pallas_call(
        main_kernel,
        out_shape=(
            jax.ShapeDtypeStruct((16, 64, 256), BF16),
            jax.ShapeDtypeStruct((2, 12, 3, 16, 128), BF16),
            jax.ShapeDtypeStruct((2, 64), F32),
            jax.ShapeDtypeStruct((8, 64), F32),
        ),
        in_specs=[pl.BlockSpec(memory_space=pltpu.SMEM)] + [vm] * len(arrays),
        out_specs=(vm,) * 4,
        scratch_shapes=[
            VMEM((3, 8, 2, 256), F32),
            VMEM((36, 16, 128), BF16),
            VMEM((2, 8, 64, 256), BF16),
            VMEM((2, 3, 64, 128), BF16),
            VMEM((2, 64, 128), BF16),
            VMEM((2, 256), F32),
            VMEM((16, 128), BF16),
            VMEM((128, 256), F32),
            VMEM((32, 192, 256), BF16),
            VMEM((32, 192, 256), BF16),
            VMEM((64, 4096), F32),
            VMEM((9, 64, 256), F32),
            VMEM((3, 64, 384), F32),
            VMEM((3, 64, 256), F32),
            VMEM((2, 12, 3, 16, 128), F32),
            VMEM((12, 3, 16, 128), F32),
            VMEM((12, 3, 16, 128), BF16),
            VMEM((16, 3, 16, 128), BF16),
            VMEM((8, 3, 16, 128), BF16),
            VMEM((2, 4, 4, 8, 128), F32),
            VMEM((4, 4, 8, 128), F32),
            VMEM((4, 4, 8, 128), F32),
            VMEM((4, 8, 128), F32),
            VMEM((8, 128), F32),
            VMEM((4, 2, 2, 128), F32),
            VMEM((4, 2, 2, 128), F32),
            VMEM((3, 2, 128), F32),
            pltpu.SemaphoreType.DMA((9,)),
            pltpu.SemaphoreType.DMA((9,)),
            pltpu.SemaphoreType.DMA((12,)),
            pltpu.SemaphoreType.DMA((12,)),
        ],
        compiler_params=pltpu.CompilerParams(
            collective_id=1, has_side_effects=True, vmem_limit_bytes=48 << 20
        ),
        name="main",
    )(dil, *arrays)


def finish_kernel(sums, drow, dcol, rproj, cproj, rp_ref, cp_ref, pair_ref, conv_ref, bias_ref, rf_ref, cf_ref):
    def pair_at(b):
        parts = []
        for j in range(4):
            tile = 4 * b + j
            parts.append(sums[tile // 36, (tile // 3) % 12, tile % 3].astype(F32))
        return jnp.concatenate(parts, axis=0)

    rp_ref[:, 0:128] = pair_at(0)
    rp_ref[:, 128:256] = pair_at(1)
    cp_ref[:, 0:128] = pair_at(2)
    cp_ref[:, 128:256] = pair_at(3)
    strips = [pair_at(4 + n) for n in range(9)]
    rest = []
    for n in range(5):
        both = pair_at(13 + n)
        rest += [both[:, 0:64], both[:, 64:128]]
    for k in range(3):
        for q in range(3):
            near = slice(q * 64, q * 64 + 64)
            pair_ref[k * 3 + q] = strips[k][:, near] if q < 2 else rest[k]
            pair_ref[9 + q * 3 + k] = strips[3 + k][:, near] if q < 2 else rest[3 + k]
            conv_ref[k * 3 + q] = strips[6 + k][:, near] if q < 2 else rest[6 + k]
    bias_ref[...] = rest[9][0:1]
    rf_ref[...] = times(drow[...].astype(BF16), rproj[...])
    cf_ref[...] = times(dcol[...].astype(BF16), cproj[...])


def finish(*arrays):
    vm = pl.BlockSpec(memory_space=VMEM)
    shapes = ((64, 256), (64, 256), (18, 64, 64), (9, 64, 64), (1, 64), (2, 256), (8, 256))
    return pl.pallas_call(
        finish_kernel,
        out_shape=tuple(jax.ShapeDtypeStruct(s, F32) for s in shapes),
        in_specs=[vm] * len(arrays),
        out_specs=(vm,) * len(shapes),
        compiler_params=pltpu.CompilerParams(vmem_limit_bytes=24 << 20),
        name="finish",
    )(*arrays)


def shards(
    row_features,
    col_features,
    row_proj,
    col_proj,
    pair_weight,
    pair_bias,
    conv_weight,
    dilations,
    cotangent,
):
    cot_t = jnp.swapaxes(cotangent, 0, 1)
    row_w, col_w = row_proj.T, col_proj.T
    out_t, sums, own_rows, own_cols = main(
        dilations, row_features, col_features, row_w, col_w, pair_weight,
        pair_bias.reshape(1, 64), conv_weight, cot_t,
    )
    row_g, col_g, pair, conv, bias, row_f, col_f = finish(sums, own_rows, own_cols, row_w, col_w)
    return (
        jnp.swapaxes(out_t, 0, 1),
        row_f,
        col_f,
        row_g.T,
        col_g.T,
        pair.reshape(2, 3, 3, 64, 64),
        bias.reshape(64),
        conv.reshape(3, 3, 64, 64),
    )


def solution(mesh):
    return jax.shard_map(
        shards,
        mesh=mesh,
        in_specs=(
            P(("row", "col"), None),
            P(("col", "row"), None),
            P(),
            P(),
            P(),
            P(),
            P(),
            P(),
            P(None, "row", "col"),
        ),
        out_specs=(
            P(None, "row", "col"),
            P(("row", "col"), None),
            P(("col", "row"), None),
            P(),
            P(),
            P(),
            P(),
            P(),
        ),
        check_vma=False,
    )
```

```python
import functools

import jax
import jax.numpy as jnp
from jax import lax
from jax.experimental import pallas as pl
from jax.experimental.pallas import tpu as pltpu
from jax.sharding import PartitionSpec as P

MAX_DILATION = 8
MESH = pl.DeviceIdType.MESH
VMEM = pltpu.VMEM


def places():
    r = lax.axis_index("row")
    c = lax.axis_index("col")
    return r, c, r // 8, lax.rem(r // 2, 4), lax.rem(r, 2), c // 2, lax.rem(c, 2)


def device_at(z_hi, x, core, y, z_lo):
    return ((z_hi * 4 + x) * 2 + core, y * 2 + z_lo)


def signal(barrier, target):
    pl.semaphore_signal(barrier, inc=1, device_id=target, device_id_type=MESH)


def push(src, dst, send_sem, recv_sem, target):
    pltpu.make_async_remote_copy(
        src_ref=src,
        dst_ref=dst,
        send_sem=send_sem,
        recv_sem=recv_sem,
        device_id=target,
        device_id_type=MESH,
    ).start()


def await_bytes(ref, sem):
    pltpu.make_async_copy(ref, ref, sem).wait()


FAR = -1e9
F32 = jnp.float32
BF16 = jnp.bfloat16


def times(a, b):
    return jnp.dot(a, b, preferred_element_type=F32)


def times_t(a, b):
    return lax.dot_general(a, b, (((1,), (1,)), ((), ())), preferred_element_type=F32)


def halves(v):
    hi = v.astype(BF16)
    return hi, (v - hi.astype(F32)).astype(BF16)


def turned(v, back):
    n = v.shape[1]
    return pltpu.roll(v, lax.rem(n - back, n), 1)


def lanes(rows, n):
    return lax.broadcasted_iota(jnp.int32, (rows, n), 1)


def main_kernel(
    dil, rf, cf, rproj, cproj, pw, bias, cw, cot,
    out_ref, sum_ref, drow_ref, dcol_ref,
    rows, cols, halo, side, pack, rf_wide, cf_tall,
    mix, fr, h3, c3, gs, vt, st, cs,
    g, g0, red, g1, gz, pc, c0, c1, c2, c_halo, pr, r1, r2,
    ssem, rsem, ssem2, rsem2,
):
    d1 = dil[0]
    d2 = dil[1]
    r, c, z_hi, x, core, y, z_lo = places()
    row0 = r * 16
    col0 = c * 256
    up, down = lax.rem(r + 31, 32), lax.rem(r + 1, 32)
    left, right = lax.rem(c + 7, 8), lax.rem(c + 1, 8)
    a = x * 4 + y
    z = z_hi * 2 + z_lo
    sibling = device_at(z_hi, x, 1 - core, y, z_lo)

    def plane(t):
        other = lax.rem(a + t, 16)
        return other, device_at(z_hi, other // 4, core, lax.rem(other, 4), z_lo)

    def along_z(t):
        other = lax.rem(z + t, 8)
        return device_at(other // 2, x, core, y, lax.rem(other, 2))

    barrier = pltpu.get_barrier_semaphore()

    @pl.loop(12, 43)
    def _(t):
        signal(barrier, (lax.rem(r + t + t // 32, 32), c))

    @pl.loop(1, 8)
    def _(t):
        signal(barrier, (r, lax.rem(c + t, 8)))

    for r_to in (up, down):
        for c_to in (left, right):
            signal(barrier, (r_to, c_to))
    for dx in range(1, 4):
        for dy in range(1, 4):
            signal(barrier, device_at(z_hi, lax.rem(x + dx, 4), core, lax.rem(y + dy, 4), z_lo))
    for dz in range(1, 4):
        signal(barrier, device_at(lax.rem(z_hi + dz, 4), x, core, y, 1 - z_lo))

    own_rf = rf[...].astype(F32)
    rf_wide[...] = own_rf
    rows[1, c] = own_rf
    own_cf = cf[...].astype(F32)
    own_cf = jnp.concatenate([own_cf[:, 0:128], own_cf[:, 128:256]], axis=0).astype(BF16)
    cf_tall[...] = own_cf
    cols[r + 2] = own_cf
    pl.semaphore_wait(barrier, 31 + 7 + 4 + 9 + 3)

    @pl.loop(12, 43)
    def _(t):
        push(cf_tall, cols.at[r + 2], ssem.at[2], rsem.at[2], (lax.rem(r + t + t // 32, 32), c))

    @pl.loop(1, 8)
    def _(t):
        push(rf_wide, rows.at[1, c], ssem.at[3], rsem.at[3], (r, lax.rem(c + t, 8)))

    group = lanes(64, 128) // 8
    first = jnp.zeros((64, 128), jnp.float32)
    last = jnp.zeros((64, 128), jnp.float32)
    for i in range(16):
        head = cot[i, :, 0:128].astype(jnp.float32)
        tail = cot[i, :, 128:256].astype(jnp.float32)
        first = jnp.where(group == i, pltpu.roll(head, 8 * i, 1) if i else head, first)
        last = jnp.where(group == i, pltpu.roll(tail, (8 * i + 8) % 128, 1) if i < 15 else tail, last)
    pack[0] = first.astype(jnp.bfloat16)
    pack[1] = last.astype(jnp.bfloat16)
    for slot, r_to in ((2, up), (1, r), (0, down)):
        push(pack.at[0], side.at[1, slot], ssem.at[4], rsem.at[4], (r_to, left))
        push(pack.at[1], side.at[0, slot], ssem.at[4], rsem.at[4], (r_to, right))
    push(cot.at[pl.ds(8, 8)], halo.at[0], ssem.at[0], rsem.at[0], (down, c))
    push(cot.at[pl.ds(0, 8)], halo.at[1], ssem.at[1], rsem.at[1], (up, c))

    pw0 = jnp.concatenate(
        [jnp.concatenate([pw[0, k, q] for q in range(3)], axis=1) for k in range(3)], axis=0
    )
    pw1 = jnp.concatenate(
        [jnp.concatenate([pw[1, k, q] for k in range(3)], axis=1) for q in range(3)], axis=0
    )
    wf = [cw[k].reshape(192, 64).T for k in range(3)]
    wb = [jnp.concatenate([cw[k, q] for q in range(3)], axis=1) for k in range(3)]
    lane = lanes(64, 128)

    def taps(v, offset):
        return jnp.concatenate([turned(v, offset + (k - 1) * d1) for k in range(3)], axis=0).astype(BF16)

    def cotangent_row(e):
        if e < 8:
            x0, x1, slot, n = halo[0, e, :, 0:128], halo[0, e, :, 128:256], 0, 8 + e
        elif e < 24:
            x0, x1, slot, n = cot[e - 8, :, 0:128], cot[e - 8, :, 128:256], 1, e - 8
        else:
            x0, x1, slot, n = halo[1, e - 24, :, 0:128], halo[1, e - 24, :, 128:256], 2, e - 24
        i = row0 - 8 + e
        ok = (i >= 0) & (i < 512)
        before = side[0, slot]
        after = side[1, slot]
        if slot != 1:
            keep = jnp.where(ok, 1.0, 0.0).astype(BF16)
            x0, x1 = x0 * keep, x1 * keep
        before = before * jnp.where(ok & (c > 0), 1.0, 0.0).astype(BF16)
        after = after * jnp.where(ok & (c < 7), 1.0, 0.0).astype(BF16)
        low, high = slice(0, 128), slice(128, 256)
        c3[e, 64:128, low] = x0
        c3[e, 64:128, high] = x1
        r0 = pltpu.roll(x0, d2, 1)
        r1 = pltpu.roll(x1, d2, 1)
        rp = pltpu.roll(before, lax.rem(120 - 8 * n + d2 + 128, 128), 1)
        c3[e, 128:192, low] = jnp.where(lane < d2, rp, r0)
        c3[e, 128:192, high] = jnp.where(lane < d2, r0, r1)
        l0 = pltpu.roll(x0, 128 - d2, 1)
        l1 = pltpu.roll(x1, 128 - d2, 1)
        rn = pltpu.roll(after, lax.rem(256 - 8 * n - d2, 128), 1)
        c3[e, 0:64, low] = jnp.where(lane >= 128 - d2, l1, l0)
        c3[e, 0:64, high] = jnp.where(lane >= 128 - d2, rn, l1)

    await_bytes(rows.at[1, pl.ds(0, 7)], rsem.at[3])
    push(rows.at[1], rows.at[0], ssem.at[5], rsem.at[5], (down, c))
    push(rows.at[1], rows.at[2], ssem.at[6], rsem.at[6], (up, c))
    await_bytes(side, rsem.at[4])
    for e in range(8, 24):
        cotangent_row(e)
    await_bytes(cols.at[pl.ds(2, 31)], rsem.at[2])
    push(cols.at[pl.ds(2, 2)], cols.at[pl.ds(34, 2)], ssem.at[7], rsem.at[7], (r, left))
    push(cols.at[pl.ds(32, 2)], cols.at[pl.ds(0, 2)], ssem.at[8], rsem.at[8], (r, right))

    await_bytes(rows.at[0], rsem.at[5])
    await_bytes(rows.at[2], rsem.at[6])
    fr[...] = jnp.zeros((128, 256), F32)
    for m in range(3):
        for n in range(8):
            fr[m * 16 + 2 * n : m * 16 + 2 * n + 2, :] = rows[m, n]
    at = row0 - 16 + lax.broadcasted_iota(jnp.int32, (128, 256), 0)
    feat_r = jnp.where((at >= 0) & (at < 512), fr[...], 0.0).astype(BF16)
    a_t = times_t(rproj[...], feat_r).astype(BF16).astype(F32)
    rt = times(pw0.T, taps(a_t, 8)) * 0.5
    rt0, rt2 = rt[0:64], rt[128:192]
    rsum = rt0 + rt[64:128] + rt2
    bias_col = jnp.broadcast_to(bias[...] * 0.5, (8, 64)).T[:, 0:1]
    await_bytes(cols.at[pl.ds(34, 2)], rsem.at[7])
    await_bytes(cols.at[pl.ds(0, 2)], rsem.at[8])
    wide = cols[...].astype(F32)
    feat_c = jnp.concatenate([wide[:, :8].reshape(288, 128), wide[:, 8:].reshape(288, 128)], axis=1)
    at = col0 - 16 + lax.broadcasted_iota(jnp.int32, (288, 256), 0)
    feat_c = jnp.where((at >= 0) & (at < 2048), feat_c, 0.0)
    feat_c = jnp.concatenate([feat_c, jnp.zeros((96, 256), F32)], axis=0).astype(BF16)
    b_t = times_t(cproj[...], feat_c).astype(BF16).astype(F32)
    ct = times(pw1.T, taps(b_t, 8)) * 0.5
    at = col0 - 8 + lanes(64, 384)
    base = ct[64:128] + bias_col + jnp.where((at >= 0) & (at < 2048), 0.0, FAR)
    sums = (base + ct[128:192], base + ct[0:64] + ct[128:192], base + ct[0:64])
    for case in range(3):
        st[case] = sums[case]
        vt[case * 3 + 1] = turned(sums[case], 8)[:, 0:256]
    near, far = [], []
    for q in range(3):
        at = col0 + (q - 1) * d2 + lanes(1, 256)
        near.append(jnp.where(at - d1 < 0, 1.0, 0.0))
        far.append(jnp.where(at + d1 >= 2048, 1.0, 0.0))

    def hidden_row(e, taps_here):
        i = row0 - 8 + e
        case = jnp.where(i - d1 < 0, 0, jnp.where(i + d1 >= 512, 2, 1))
        gate = jnp.where((i >= 0) & (i < 512), 0.0, FAR)
        all_e = rsum[:, e : e + 1] + gate
        rt0_e = rt0[:, e : e + 1]
        rt2_e = rt2[:, e : e + 1]
        for q in taps_here:
            h = vt[case * 3 + q] + all_e - near[q] * rt0_e - far[q] * rt2_e
            t = jnp.tanh(h)
            h3[e, q * 64 : (q + 1) * 64, :] = (h + h * t).astype(BF16)
            if q == 1 and 8 <= e < 24:
                gs[:, (e - 8) * 256 : (e - 7) * 256] = 0.5 + 0.5 * t + h * (0.5 - 0.5 * t * t)

    for e in range(8, 24):
        hidden_row(e, (1,))

    await_bytes(halo.at[0], rsem.at[0])
    await_bytes(halo.at[1], rsem.at[1])
    for e in range(8):
        cotangent_row(e)
        cotangent_row(24 + e)
    live = [1.0 - near[1], None, 1.0 - far[1]]
    rs = [jnp.zeros((64, 128), F32) for _ in range(3)]
    gc = [jnp.zeros((64, 192), F32) for _ in range(3)]
    cs[...] = jnp.zeros((3, 64, 256), F32)
    for i in range(16):
        own = h3[8 + i, 64:128, :]
        d = cot[i].astype(F32)
        for k in range(3):
            grads = c3[8 + i - (k - 1) * d2]
            d = d + times(wb[k], grads)
            gc[k] = gc[k] + times_t(own, grads)
        d = d * gs[:, i * 256 : (i + 1) * 256]
        cs[1] = cs[1] + d
        cs[0] = cs[0] + d * jnp.where(row0 + i - d1 >= 0, 1.0, 0.0)
        cs[2] = cs[2] + d * jnp.where(row0 + i + d1 < 512, 1.0, 0.0)
        for q in range(3):
            part = d if live[q] is None else d * live[q]
            rs[q] = jnp.where(lane == i, jnp.sum(part, axis=1, keepdims=True), rs[q])

    rs_hi, rs_lo = halves(jnp.concatenate(rs, axis=0))
    cs_hi, cs_lo = halves(cs[...].reshape(192, 256))
    br = times(pw0, rs_hi) + times(pw0, rs_lo)
    bc = times(pw1, cs_hi) + times(pw1, cs_lo)
    bc = jnp.concatenate([bc, jnp.zeros((192, 128), F32)], axis=1)
    dr = sum(pltpu.roll(br[k * 64 : (k + 1) * 64], 16 + (k - 1) * d1, 1) for k in range(3))
    dc = sum(pltpu.roll(bc[q * 64 : (q + 1) * 64], 16 + (q - 1) * d1, 1) for q in range(3))
    at = row0 - 16 + lane
    dr = jnp.where((at >= 0) & (at < 512), dr, 0.0)
    at = col0 - 16 + lanes(64, 384)
    dc = jnp.where((at >= 0) & (at < 2048), dc, 0.0)
    dr_hi, dr_lo = halves(dr)
    dc_hi, dc_lo = halves(dc)
    row_proj_g = times(dr_hi, feat_r) + times(dr_lo, feat_r)
    col_proj_g = times(dc_hi, feat_c) + times(dc_lo, feat_c)
    a_own = taps(a_t, 16)
    b_own = taps(b_t, 16)[:, 0:256]
    p0 = times_t(a_own, rs_hi) + times_t(a_own, rs_lo)
    p1 = times_t(b_own, cs_hi) + times_t(b_own, cs_lo)
    bias_g = jnp.broadcast_to(jnp.sum(cs[1], axis=1, keepdims=True), (64, 64)).T

    strips = [p0[k * 64 : (k + 1) * 64] for k in range(3)]
    strips += [p1[q * 64 : (q + 1) * 64] for q in range(3)] + gc
    pairs = [row_proj_g[:, 0:128], row_proj_g[:, 128:256], col_proj_g[:, 0:128], col_proj_g[:, 128:256]]
    pairs += [strip[:, 0:128] for strip in strips]
    rest = [strip[:, 128:192] for strip in strips] + [bias_g]
    pairs += [jnp.concatenate([rest[2 * n], rest[2 * n + 1]], axis=1) for n in range(5)]
    for b in range(18):
        for j in range(4):
            tile = 4 * b + j
            g[tile // 36, (tile // 3) % 12, tile % 3] = pairs[b][16 * j : 16 * j + 16]

    dr_p = dr.T
    dc_p = dc.T
    for n in range(32):
        if n == 0:
            extra = dc_p[272:280]
        elif n == 31:
            extra = dc_p[8:16]
        else:
            extra = jnp.zeros((8, 64), F32)
        pc[n % 2, (n // 2) % 4, n // 8] = jnp.concatenate([dc_p[16 + 8 * n : 24 + 8 * n], extra], axis=1)
    for n in range(8):
        h = 32 + 2 * n if n < 4 else 2 * n
        pr[n // 2, n % 2] = jnp.concatenate([dr_p[16 + 2 * n : 18 + 2 * n], dr_p[h : h + 2]], axis=1)

    row_to = jnp.where(c < 4, down, up)
    col_to = jnp.where(r < 16, right, left)
    push(g.at[1 - core], g0, ssem2.at[0], rsem2.at[0], sibling)
    push(pc.at[1 - core], c0, ssem2.at[1], rsem2.at[1], sibling)
    for t in range(1, 4):
        y_to = lax.rem(y + t, 4)
        push(pr.at[y_to], r1.at[t], ssem2.at[4], rsem2.at[4], device_at(z_hi, x, core, y_to, z_lo))
    await_bytes(g0, rsem2.at[0])
    red[...] = (g[core] + g0[...]).astype(BF16)

    @pl.loop(6, 21)
    def _(u):
        t = lax.rem(u + u // 16, 16)
        other, target = plane(t)

        @pl.when(other < 12)
        def _():
            push(red.at[other], g1.at[t], ssem2.at[2], rsem2.at[2], target)

    await_bytes(c0, rsem2.at[1])
    c0[...] = c0[...] + pc[core]
    for t in range(1, 4):
        x_to = lax.rem(x + t, 4)
        push(c0.at[x_to], c1.at[t], ssem2.at[3], rsem2.at[3], device_at(z_hi, x_to, core, y, z_lo))
    for case in range(3):
        for q in (0, 2):
            vt[case * 3 + q] = turned(st[case], 8 + (q - 1) * d2)[:, 0:256]
    for e in range(32):
        hidden_row(e, (0, 2) if 8 <= e < 24 else (0, 1, 2))

    await_bytes(r1.at[pl.ds(1, 3)], rsem2.at[4])
    r1[0] = pr[y] + r1[1] + r1[2] + r1[3]

    @pl.when(a < 12)
    def _():
        await_bytes(g1.at[pl.ds(1, 15)], rsem2.at[2])
        mine = g[core, a] + g0[a]
        for t in range(1, 16):
            mine = mine + g1[t].astype(F32)
        gz[z] = mine.astype(BF16)

        @pl.loop(3, 10)
        def _(u):
            t = lax.rem(u + u // 8, 8)
            push(gz.at[z], gz.at[z], ssem2.at[5], rsem2.at[5], along_z(t))

    await_bytes(c1.at[pl.ds(1, 3)], rsem2.at[3])
    c1[0] = c0[x] + c1[1] + c1[2] + c1[3]
    for t in range(1, 4):
        z_to = lax.rem(z_hi + t, 4)
        push(c1.at[0, z_to], c2.at[t], ssem2.at[6], rsem2.at[6], device_at(z_to, x, core, y, z_lo))
    push(r1.at[0, 1 - z_lo], r2.at[1], ssem2.at[7], rsem2.at[7], device_at(z_hi, x, core, y, 1 - z_lo))

    for i in range(16):
        mixed = h3[8 + i, 64:128, :].astype(F32)
        for k in range(3):
            mixed = mixed + times(wf[k], h3[8 + i + (k - 1) * d2])
        mix[i] = mixed.astype(BF16)
    out_ref[...] = jnp.swapaxes(mix[...], 0, 1)

    @pl.when(a < 12)
    def _():
        await_bytes(gz.at[pl.ds(0, 7)], rsem2.at[5])
        whole = gz[0].astype(F32)
        for t in range(1, 8):
            whole = whole + gz[t].astype(F32)
        sum_ref[core, a] = whole.astype(BF16)

        @pl.loop(6, 21)
        def _(u):
            t = lax.rem(u + u // 16, 16)
            push(sum_ref.at[core, a], sum_ref.at[core, a], ssem2.at[10], rsem2.at[10], plane(t)[1])

    await_bytes(c2.at[pl.ds(1, 3)], rsem2.at[6])
    await_bytes(r2.at[1], rsem2.at[7])
    c2[0] = c1[0, z_hi] + c2[1] + c2[2] + c2[3]
    r2[0] = r1[0, z_lo] + r2[1]
    push(r2.at[0], r2.at[2], ssem2.at[8], rsem2.at[8], (row_to, c))
    push(c2.at[0], c_halo, ssem2.at[9], rsem2.at[9], (r, col_to))
    await_bytes(r2.at[2], rsem2.at[8])
    await_bytes(c_halo, rsem2.at[9])
    drow_ref[...] = r2[0, :, 0:64] + r2[2, :, 64:128]
    dcol_ref[...] = c2[0, :, 0:64] + c_halo[:, 64:128]

    @pl.when(a < 12)
    def _():
        await_bytes(sum_ref.at[core, pl.ds(0, 11)], rsem2.at[10])

    @pl.when(a >= 12)
    def _():
        await_bytes(sum_ref.at[core], rsem2.at[10])

    push(sum_ref.at[core], sum_ref.at[core], ssem2.at[11], rsem2.at[11], sibling)
    await_bytes(sum_ref.at[0], rsem2.at[11])

    await_bytes(halo.at[0], ssem.at[0])
    await_bytes(halo.at[1], ssem.at[1])
    await_bytes(cols.at[pl.ds(2, 31)], ssem.at[2])
    await_bytes(rows.at[1, pl.ds(0, 7)], ssem.at[3])
    await_bytes(side, ssem.at[4])
    await_bytes(rows.at[0], ssem.at[5])
    await_bytes(rows.at[2], ssem.at[6])
    await_bytes(cols.at[pl.ds(34, 2)], ssem.at[7])
    await_bytes(cols.at[pl.ds(0, 2)], ssem.at[8])
    await_bytes(g0, ssem2.at[0])
    await_bytes(c0, ssem2.at[1])
    await_bytes(c1.at[pl.ds(1, 3)], ssem2.at[3])
    await_bytes(r1.at[pl.ds(1, 3)], ssem2.at[4])
    await_bytes(c2.at[pl.ds(1, 3)], ssem2.at[6])
    await_bytes(r2.at[1], ssem2.at[7])
    await_bytes(r2.at[2], ssem2.at[8])
    await_bytes(c_halo, ssem2.at[9])
    await_bytes(sum_ref.at[0], ssem2.at[11])

    @pl.when(a < 12)
    def _():
        await_bytes(g1.at[pl.ds(0, 11)], ssem2.at[2])
        await_bytes(gz.at[pl.ds(0, 7)], ssem2.at[5])
        await_bytes(g1.at[pl.ds(1, 15)], ssem2.at[10])

    @pl.when(a >= 12)
    def _():
        await_bytes(g1.at[pl.ds(0, 12)], ssem2.at[2])


def main(dil, *arrays):
    vm = pl.BlockSpec(memory_space=VMEM)
    return pl.pallas_call(
        main_kernel,
        out_shape=(
            jax.ShapeDtypeStruct((64, 16, 256), BF16),
            jax.ShapeDtypeStruct((2, 12, 3, 16, 128), BF16),
            jax.ShapeDtypeStruct((2, 64), F32),
            jax.ShapeDtypeStruct((8, 64), F32),
        ),
        in_specs=[pl.BlockSpec(memory_space=pltpu.SMEM)] + [vm] * len(arrays),
        out_specs=(vm,) * 4,
        scratch_shapes=[
            VMEM((3, 8, 2, 256), F32),
            VMEM((36, 16, 128), BF16),
            VMEM((2, 8, 64, 256), BF16),
            VMEM((2, 3, 64, 128), BF16),
            VMEM((2, 64, 128), BF16),
            VMEM((2, 256), F32),
            VMEM((16, 128), BF16),
            VMEM((16, 64, 256), BF16),
            VMEM((128, 256), F32),
            VMEM((32, 192, 256), BF16),
            VMEM((32, 192, 256), BF16),
            VMEM((64, 4096), F32),
            VMEM((9, 64, 256), F32),
            VMEM((3, 64, 384), F32),
            VMEM((3, 64, 256), F32),
            VMEM((2, 12, 3, 16, 128), F32),
            VMEM((12, 3, 16, 128), F32),
            VMEM((12, 3, 16, 128), BF16),
            VMEM((16, 3, 16, 128), BF16),
            VMEM((8, 3, 16, 128), BF16),
            VMEM((2, 4, 4, 8, 128), F32),
            VMEM((4, 4, 8, 128), F32),
            VMEM((4, 4, 8, 128), F32),
            VMEM((4, 8, 128), F32),
            VMEM((8, 128), F32),
            VMEM((4, 2, 2, 128), F32),
            VMEM((4, 2, 2, 128), F32),
            VMEM((3, 2, 128), F32),
            pltpu.SemaphoreType.DMA((9,)),
            pltpu.SemaphoreType.DMA((9,)),
            pltpu.SemaphoreType.DMA((12,)),
            pltpu.SemaphoreType.DMA((12,)),
        ],
        compiler_params=pltpu.CompilerParams(
            collective_id=1, has_side_effects=True, vmem_limit_bytes=48 << 20
        ),
        name="main",
    )(dil, *arrays)


def finish_kernel(sums, drow, dcol, rproj, cproj, rp_ref, cp_ref, pair_ref, conv_ref, bias_ref, rf_ref, cf_ref):
    def pair_at(b):
        parts = []
        for j in range(4):
            tile = 4 * b + j
            parts.append(sums[tile // 36, (tile // 3) % 12, tile % 3].astype(F32))
        return jnp.concatenate(parts, axis=0)

    rp_ref[:, 0:128] = pair_at(0)
    rp_ref[:, 128:256] = pair_at(1)
    cp_ref[:, 0:128] = pair_at(2)
    cp_ref[:, 128:256] = pair_at(3)
    strips = [pair_at(4 + n) for n in range(9)]
    rest = []
    for n in range(5):
        both = pair_at(13 + n)
        rest += [both[:, 0:64], both[:, 64:128]]
    for k in range(3):
        for q in range(3):
            near = slice(q * 64, q * 64 + 64)
            pair_ref[k * 3 + q] = strips[k][:, near] if q < 2 else rest[k]
            pair_ref[9 + q * 3 + k] = strips[3 + k][:, near] if q < 2 else rest[3 + k]
            conv_ref[k * 3 + q] = strips[6 + k][:, near] if q < 2 else rest[6 + k]
    bias_ref[...] = rest[9][0:1]
    rf_ref[...] = times(drow[...].astype(BF16), rproj[...])
    cf_ref[...] = times(dcol[...].astype(BF16), cproj[...])


def finish(*arrays):
    vm = pl.BlockSpec(memory_space=VMEM)
    shapes = ((64, 256), (64, 256), (18, 64, 64), (9, 64, 64), (1, 64), (2, 256), (8, 256))
    return pl.pallas_call(
        finish_kernel,
        out_shape=tuple(jax.ShapeDtypeStruct(s, F32) for s in shapes),
        in_specs=[vm] * len(arrays),
        out_specs=(vm,) * len(shapes),
        compiler_params=pltpu.CompilerParams(vmem_limit_bytes=24 << 20),
        name="finish",
    )(*arrays)


def shards(
    row_features,
    col_features,
    row_proj,
    col_proj,
    pair_weight,
    pair_bias,
    conv_weight,
    dilations,
    cotangent,
):
    cot_t = jnp.swapaxes(cotangent, 0, 1)
    row_w, col_w = row_proj.T, col_proj.T
    out_t, sums, own_rows, own_cols = main(
        dilations, row_features, col_features, row_w, col_w, pair_weight,
        pair_bias.reshape(1, 64), conv_weight, cot_t,
    )
    row_g, col_g, pair, conv, bias, row_f, col_f = finish(sums, own_rows, own_cols, row_w, col_w)
    return (
        out_t,
        row_f,
        col_f,
        row_g.T,
        col_g.T,
        pair.reshape(2, 3, 3, 64, 64),
        bias.reshape(64),
        conv.reshape(3, 3, 64, 64),
    )


def solution(mesh):
    return jax.shard_map(
        shards,
        mesh=mesh,
        in_specs=(
            P(("row", "col"), None),
            P(("col", "row"), None),
            P(),
            P(),
            P(),
            P(),
            P(),
            P(),
            P(None, "row", "col"),
        ),
        out_specs=(
            P(None, "row", "col"),
            P(("row", "col"), None),
            P(("col", "row"), None),
            P(),
            P(),
            P(),
            P(),
            P(),
        ),
        check_vma=False,
    )
```

```python
import functools

import jax
import jax.numpy as jnp
from jax import lax
from jax.experimental import pallas as pl
from jax.experimental.pallas import tpu as pltpu
from jax.sharding import PartitionSpec as P

MAX_DILATION = 8
MESH = pl.DeviceIdType.MESH
VMEM = pltpu.VMEM


def places():
    r = lax.axis_index("row")
    c = lax.axis_index("col")
    return r, c, r // 8, lax.rem(r // 2, 4), lax.rem(r, 2), c // 2, lax.rem(c, 2)


def device_at(z_hi, x, core, y, z_lo):
    return ((z_hi * 4 + x) * 2 + core, y * 2 + z_lo)


def signal(barrier, target):
    pl.semaphore_signal(barrier, inc=1, device_id=target, device_id_type=MESH)


def push(src, dst, send_sem, recv_sem, target):
    pltpu.make_async_remote_copy(
        src_ref=src,
        dst_ref=dst,
        send_sem=send_sem,
        recv_sem=recv_sem,
        device_id=target,
        device_id_type=MESH,
    ).start()


def await_bytes(ref, sem):
    pltpu.make_async_copy(ref, ref, sem).wait()


FAR = -1e9
F32 = jnp.float32
BF16 = jnp.bfloat16


def times(a, b):
    return jnp.dot(a, b, preferred_element_type=F32)


def times_t(a, b):
    return lax.dot_general(a, b, (((1,), (1,)), ((), ())), preferred_element_type=F32)


def halves(v):
    hi = v.astype(BF16)
    return hi, (v - hi.astype(F32)).astype(BF16)


def turned(v, back):
    n = v.shape[1]
    return pltpu.roll(v, lax.rem(n - back, n), 1)


def lanes(rows, n):
    return lax.broadcasted_iota(jnp.int32, (rows, n), 1)


def main_kernel(
    dil, rf, cf, rproj, cproj, pw, bias, cw, cot,
    out_ref, sum_ref, drow_ref, dcol_ref,
    rows, cols, halo, side, pack, rf_wide, cf_tall,
    mix, fr, h3, c3, gs, vt, st, cs,
    g, g0, red, g1, gz, pc, c0, c1, c2, c_halo, pr, r1, r2,
    ssem, rsem, ssem2, rsem2,
):
    d1 = dil[0]
    d2 = dil[1]
    r, c, z_hi, x, core, y, z_lo = places()
    row0 = r * 16
    col0 = c * 256
    up, down = lax.rem(r + 31, 32), lax.rem(r + 1, 32)
    left, right = lax.rem(c + 7, 8), lax.rem(c + 1, 8)
    a = x * 4 + y
    z = z_hi * 2 + z_lo
    sibling = device_at(z_hi, x, 1 - core, y, z_lo)

    def plane(t):
        other = lax.rem(a + t, 16)
        return other, device_at(z_hi, other // 4, core, lax.rem(other, 4), z_lo)

    def along_z(t):
        other = lax.rem(z + t, 8)
        return device_at(other // 2, x, core, y, lax.rem(other, 2))

    barrier = pltpu.get_barrier_semaphore()

    @pl.loop(12, 43)
    def _(t):
        signal(barrier, (lax.rem(r + t + t // 32, 32), c))

    @pl.loop(1, 8)
    def _(t):
        signal(barrier, (r, lax.rem(c + t, 8)))

    for r_to in (up, down):
        for c_to in (left, right):
            signal(barrier, (r_to, c_to))
    for dx in range(1, 4):
        for dy in range(1, 4):
            signal(barrier, device_at(z_hi, lax.rem(x + dx, 4), core, lax.rem(y + dy, 4), z_lo))
    for dz in range(1, 4):
        signal(barrier, device_at(lax.rem(z_hi + dz, 4), x, core, y, 1 - z_lo))

    own_rf = rf[...].astype(F32)
    rf_wide[...] = own_rf
    rows[1, c] = own_rf
    own_cf = cf[...].astype(F32)
    own_cf = jnp.concatenate([own_cf[:, 0:128], own_cf[:, 128:256]], axis=0).astype(BF16)
    cf_tall[...] = own_cf
    cols[r + 2] = own_cf
    pl.semaphore_wait(barrier, 31 + 7 + 4 + 9 + 3)

    @pl.loop(12, 43)
    def _(t):
        push(cf_tall, cols.at[r + 2], ssem.at[2], rsem.at[2], (lax.rem(r + t + t // 32, 32), c))

    @pl.loop(1, 8)
    def _(t):
        push(rf_wide, rows.at[1, c], ssem.at[3], rsem.at[3], (r, lax.rem(c + t, 8)))

    group = lanes(64, 128) // 8
    first = jnp.zeros((64, 128), jnp.float32)
    last = jnp.zeros((64, 128), jnp.float32)
    for i in range(16):
        head = cot[i, :, 0:128].astype(jnp.float32)
        tail = cot[i, :, 128:256].astype(jnp.float32)
        first = jnp.where(group == i, pltpu.roll(head, 8 * i, 1) if i else head, first)
        last = jnp.where(group == i, pltpu.roll(tail, (8 * i + 8) % 128, 1) if i < 15 else tail, last)
    pack[0] = first.astype(jnp.bfloat16)
    pack[1] = last.astype(jnp.bfloat16)
    for slot, r_to in ((2, up), (1, r), (0, down)):
        push(pack.at[0], side.at[1, slot], ssem.at[4], rsem.at[4], (r_to, left))
        push(pack.at[1], side.at[0, slot], ssem.at[4], rsem.at[4], (r_to, right))

    pw0 = jnp.concatenate(
        [jnp.concatenate([pw[0, k, q] for q in range(3)], axis=1) for k in range(3)], axis=0
    )
    pw1 = jnp.concatenate(
        [jnp.concatenate([pw[1, k, q] for k in range(3)], axis=1) for q in range(3)], axis=0
    )
    wf = [cw[k].reshape(192, 64).T for k in range(3)]
    wb = [jnp.concatenate([cw[k, q] for q in range(3)], axis=1) for k in range(3)]
    lane = lanes(64, 128)

    def taps(v, offset):
        return jnp.concatenate([turned(v, offset + (k - 1) * d1) for k in range(3)], axis=0).astype(BF16)

    def cotangent_row(e):
        if e < 8:
            x0, x1, slot, n = halo[0, e, :, 0:128], halo[0, e, :, 128:256], 0, 8 + e
        elif e < 24:
            x0, x1, slot, n = cot[e - 8, :, 0:128], cot[e - 8, :, 128:256], 1, e - 8
        else:
            x0, x1, slot, n = halo[1, e - 24, :, 0:128], halo[1, e - 24, :, 128:256], 2, e - 24
        i = row0 - 8 + e
        ok = (i >= 0) & (i < 512)
        before = side[0, slot]
        after = side[1, slot]
        if slot != 1:
            keep = jnp.where(ok, 1.0, 0.0).astype(BF16)
            x0, x1 = x0 * keep, x1 * keep
        before = before * jnp.where(ok & (c > 0), 1.0, 0.0).astype(BF16)
        after = after * jnp.where(ok & (c < 7), 1.0, 0.0).astype(BF16)
        low, high = slice(0, 128), slice(128, 256)
        c3[e, 64:128, low] = x0
        c3[e, 64:128, high] = x1
        r0 = pltpu.roll(x0, d2, 1)
        r1 = pltpu.roll(x1, d2, 1)
        rp = pltpu.roll(before, lax.rem(120 - 8 * n + d2 + 128, 128), 1)
        c3[e, 128:192, low] = jnp.where(lane < d2, rp, r0)
        c3[e, 128:192, high] = jnp.where(lane < d2, r0, r1)
        l0 = pltpu.roll(x0, 128 - d2, 1)
        l1 = pltpu.roll(x1, 128 - d2, 1)
        rn = pltpu.roll(after, lax.rem(256 - 8 * n - d2, 128), 1)
        c3[e, 0:64, low] = jnp.where(lane >= 128 - d2, l1, l0)
        c3[e, 0:64, high] = jnp.where(lane >= 128 - d2, rn, l1)

    await_bytes(rows.at[1, pl.ds(0, 7)], rsem.at[3])
    push(rows.at[1], rows.at[0], ssem.at[5], rsem.at[5], (down, c))
    push(rows.at[1], rows.at[2], ssem.at[6], rsem.at[6], (up, c))
    push(cot.at[pl.ds(8, 8)], halo.at[0], ssem.at[0], rsem.at[0], (down, c))
    push(cot.at[pl.ds(0, 8)], halo.at[1], ssem.at[1], rsem.at[1], (up, c))
    await_bytes(side, rsem.at[4])
    for e in range(8, 24):
        cotangent_row(e)
    await_bytes(cols.at[pl.ds(2, 31)], rsem.at[2])
    push(cols.at[pl.ds(2, 2)], cols.at[pl.ds(34, 2)], ssem.at[7], rsem.at[7], (r, left))
    push(cols.at[pl.ds(32, 2)], cols.at[pl.ds(0, 2)], ssem.at[8], rsem.at[8], (r, right))

    await_bytes(rows.at[0], rsem.at[5])
    await_bytes(rows.at[2], rsem.at[6])
    fr[...] = jnp.zeros((128, 256), F32)
    for m in range(3):
        for n in range(8):
            fr[m * 16 + 2 * n : m * 16 + 2 * n + 2, :] = rows[m, n]
    at = row0 - 16 + lax.broadcasted_iota(jnp.int32, (128, 256), 0)
    feat_r = jnp.where((at >= 0) & (at < 512), fr[...], 0.0).astype(BF16)
    a_t = times_t(rproj[...], feat_r).astype(BF16).astype(F32)
    rt = times(pw0.T, taps(a_t, 8)) * 0.5
    rt0, rt2 = rt[0:64], rt[128:192]
    rsum = rt0 + rt[64:128] + rt2
    bias_col = jnp.broadcast_to(bias[...] * 0.5, (8, 64)).T[:, 0:1]
    await_bytes(cols.at[pl.ds(34, 2)], rsem.at[7])
    await_bytes(cols.at[pl.ds(0, 2)], rsem.at[8])
    wide = cols[...].astype(F32)
    feat_c = jnp.concatenate([wide[:, :8].reshape(288, 128), wide[:, 8:].reshape(288, 128)], axis=1)
    at = col0 - 16 + lax.broadcasted_iota(jnp.int32, (288, 256), 0)
    feat_c = jnp.where((at >= 0) & (at < 2048), feat_c, 0.0)
    feat_c = jnp.concatenate([feat_c, jnp.zeros((96, 256), F32)], axis=0).astype(BF16)
    b_t = times_t(cproj[...], feat_c).astype(BF16).astype(F32)
    ct = times(pw1.T, taps(b_t, 8)) * 0.5
    at = col0 - 8 + lanes(64, 384)
    base = ct[64:128] + bias_col + jnp.where((at >= 0) & (at < 2048), 0.0, FAR)
    sums = (base + ct[128:192], base + ct[0:64] + ct[128:192], base + ct[0:64])
    for case in range(3):
        st[case] = sums[case]
        vt[case * 3 + 1] = turned(sums[case], 8)[:, 0:256]
    near, far = [], []
    for q in range(3):
        at = col0 + (q - 1) * d2 + lanes(1, 256)
        near.append(jnp.where(at - d1 < 0, 1.0, 0.0))
        far.append(jnp.where(at + d1 >= 2048, 1.0, 0.0))

    def hidden_row(e, taps_here):
        i = row0 - 8 + e
        case = jnp.where(i - d1 < 0, 0, jnp.where(i + d1 >= 512, 2, 1))
        gate = jnp.where((i >= 0) & (i < 512), 0.0, FAR)
        all_e = rsum[:, e : e + 1] + gate
        rt0_e = rt0[:, e : e + 1]
        rt2_e = rt2[:, e : e + 1]
        for q in taps_here:
            h = vt[case * 3 + q] + all_e - near[q] * rt0_e - far[q] * rt2_e
            t = jnp.tanh(h)
            h3[e, q * 64 : (q + 1) * 64, :] = (h + h * t).astype(BF16)
            if q == 1 and 8 <= e < 24:
                gs[:, (e - 8) * 256 : (e - 7) * 256] = 0.5 + 0.5 * t + h * (0.5 - 0.5 * t * t)

    for e in range(8, 24):
        hidden_row(e, (1,))

    await_bytes(halo.at[0], rsem.at[0])
    await_bytes(halo.at[1], rsem.at[1])
    for e in range(8):
        cotangent_row(e)
        cotangent_row(24 + e)
    live = [1.0 - near[1], None, 1.0 - far[1]]
    rs = [jnp.zeros((64, 128), F32) for _ in range(3)]
    gc = [jnp.zeros((192, 64), F32) for _ in range(3)]
    cs[...] = jnp.zeros((3, 64, 256), F32)
    for i in range(16):
        own = h3[8 + i, 64:128, :]
        d = cot[i].astype(F32)
        for k in range(3):
            grads = c3[8 + i - (k - 1) * d2]
            d = d + times(wb[k], grads)
            gc[k] = gc[k] + times_t(grads, own)
        d = d * gs[:, i * 256 : (i + 1) * 256]
        cs[1] = cs[1] + d
        cs[0] = cs[0] + d * jnp.where(row0 + i - d1 >= 0, 1.0, 0.0)
        cs[2] = cs[2] + d * jnp.where(row0 + i + d1 < 512, 1.0, 0.0)
        for q in range(3):
            part = d if live[q] is None else d * live[q]
            rs[q] = jnp.where(lane == i, jnp.sum(part, axis=1, keepdims=True), rs[q])

    rs_hi, rs_lo = halves(jnp.concatenate(rs, axis=0))
    cs_hi, cs_lo = halves(cs[...].reshape(192, 256))
    br = times(pw0, rs_hi) + times(pw0, rs_lo)
    bc = times(pw1, cs_hi) + times(pw1, cs_lo)
    bc = jnp.concatenate([bc, jnp.zeros((192, 128), F32)], axis=1)
    dr = sum(pltpu.roll(br[k * 64 : (k + 1) * 64], 16 + (k - 1) * d1, 1) for k in range(3))
    dc = sum(pltpu.roll(bc[q * 64 : (q + 1) * 64], 16 + (q - 1) * d1, 1) for q in range(3))
    at = row0 - 16 + lane
    dr = jnp.where((at >= 0) & (at < 512), dr, 0.0)
    at = col0 - 16 + lanes(64, 384)
    dc = jnp.where((at >= 0) & (at < 2048), dc, 0.0)
    dr_hi, dr_lo = halves(dr)
    dc_hi, dc_lo = halves(dc)
    row_proj_g = times(dr_hi, feat_r) + times(dr_lo, feat_r)
    col_proj_g = times(dc_hi, feat_c) + times(dc_lo, feat_c)
    a_own = taps(a_t, 16)
    b_own = taps(b_t, 16)[:, 0:256]
    p0 = times_t(a_own, rs_hi) + times_t(a_own, rs_lo)
    p1 = times_t(b_own, cs_hi) + times_t(b_own, cs_lo)
    bias_g = jnp.broadcast_to(jnp.sum(cs[1], axis=1, keepdims=True), (64, 64)).T

    strips = [p0[k * 64 : (k + 1) * 64] for k in range(3)]
    strips += [p1[q * 64 : (q + 1) * 64] for q in range(3)] + [part.T for part in gc]
    pairs = [row_proj_g[:, 0:128], row_proj_g[:, 128:256], col_proj_g[:, 0:128], col_proj_g[:, 128:256]]
    pairs += [strip[:, 0:128] for strip in strips]
    rest = [strip[:, 128:192] for strip in strips] + [bias_g]
    pairs += [jnp.concatenate([rest[2 * n], rest[2 * n + 1]], axis=1) for n in range(5)]
    for b in range(18):
        for j in range(4):
            tile = 4 * b + j
            g[tile // 36, (tile // 3) % 12, tile % 3] = pairs[b][16 * j : 16 * j + 16]

    dr_p = dr.T
    dc_p = dc.T
    for n in range(32):
        if n == 0:
            extra = dc_p[272:280]
        elif n == 31:
            extra = dc_p[8:16]
        else:
            extra = jnp.zeros((8, 64), F32)
        pc[n % 2, (n // 2) % 4, n // 8] = jnp.concatenate([dc_p[16 + 8 * n : 24 + 8 * n], extra], axis=1)
    for n in range(8):
        h = 32 + 2 * n if n < 4 else 2 * n
        pr[n // 2, n % 2] = jnp.concatenate([dr_p[16 + 2 * n : 18 + 2 * n], dr_p[h : h + 2]], axis=1)

    row_to = jnp.where(c < 4, down, up)
    col_to = jnp.where(r < 16, right, left)
    push(g.at[1 - core], g0, ssem2.at[0], rsem2.at[0], sibling)
    push(pc.at[1 - core], c0, ssem2.at[1], rsem2.at[1], sibling)
    for t in range(1, 4):
        y_to = lax.rem(y + t, 4)
        push(pr.at[y_to], r1.at[t], ssem2.at[4], rsem2.at[4], device_at(z_hi, x, core, y_to, z_lo))
    await_bytes(g0, rsem2.at[0])
    red[...] = (g[core] + g0[...]).astype(BF16)

    @pl.loop(6, 21)
    def _(u):
        t = lax.rem(u + u // 16, 16)
        other, target = plane(t)

        @pl.when(other < 12)
        def _():
            push(red.at[other], g1.at[t], ssem2.at[2], rsem2.at[2], target)

    await_bytes(c0, rsem2.at[1])
    c0[...] = c0[...] + pc[core]
    for t in range(1, 4):
        x_to = lax.rem(x + t, 4)
        push(c0.at[x_to], c1.at[t], ssem2.at[3], rsem2.at[3], device_at(z_hi, x_to, core, y, z_lo))
    for case in range(3):
        for q in (0, 2):
            vt[case * 3 + q] = turned(st[case], 8 + (q - 1) * d2)[:, 0:256]
    for e in range(32):
        hidden_row(e, (0, 2) if 8 <= e < 24 else (0, 1, 2))

    await_bytes(r1.at[pl.ds(1, 3)], rsem2.at[4])
    r1[0] = pr[y] + r1[1] + r1[2] + r1[3]

    @pl.when(a < 12)
    def _():
        await_bytes(g1.at[pl.ds(1, 15)], rsem2.at[2])
        mine = g[core, a] + g0[a]
        for t in range(1, 16):
            mine = mine + g1[t].astype(F32)
        gz[z] = mine.astype(BF16)

        @pl.loop(3, 10)
        def _(u):
            t = lax.rem(u + u // 8, 8)
            push(gz.at[z], gz.at[z], ssem2.at[5], rsem2.at[5], along_z(t))

    await_bytes(c1.at[pl.ds(1, 3)], rsem2.at[3])
    c1[0] = c0[x] + c1[1] + c1[2] + c1[3]
    for t in range(1, 4):
        z_to = lax.rem(z_hi + t, 4)
        push(c1.at[0, z_to], c2.at[t], ssem2.at[6], rsem2.at[6], device_at(z_to, x, core, y, z_lo))
    push(r1.at[0, 1 - z_lo], r2.at[1], ssem2.at[7], rsem2.at[7], device_at(z_hi, x, core, y, 1 - z_lo))

    for i in range(16):
        mixed = h3[8 + i, 64:128, :].astype(F32)
        for k in range(3):
            mixed = mixed + times(wf[k], h3[8 + i + (k - 1) * d2])
        mix[i] = mixed.astype(BF16)
    out_ref[...] = jnp.swapaxes(mix[...], 0, 1)

    @pl.when(a < 12)
    def _():
        await_bytes(gz.at[pl.ds(0, 7)], rsem2.at[5])
        whole = gz[0].astype(F32)
        for t in range(1, 8):
            whole = whole + gz[t].astype(F32)
        sum_ref[core, a] = whole.astype(BF16)

        @pl.loop(6, 21)
        def _(u):
            t = lax.rem(u + u // 16, 16)
            push(sum_ref.at[core, a], sum_ref.at[core, a], ssem2.at[10], rsem2.at[10], plane(t)[1])

    await_bytes(c2.at[pl.ds(1, 3)], rsem2.at[6])
    await_bytes(r2.at[1], rsem2.at[7])
    c2[0] = c1[0, z_hi] + c2[1] + c2[2] + c2[3]
    r2[0] = r1[0, z_lo] + r2[1]
    push(r2.at[0], r2.at[2], ssem2.at[8], rsem2.at[8], (row_to, c))
    push(c2.at[0], c_halo, ssem2.at[9], rsem2.at[9], (r, col_to))
    await_bytes(r2.at[2], rsem2.at[8])
    await_bytes(c_halo, rsem2.at[9])
    drow_ref[...] = r2[0, :, 0:64] + r2[2, :, 64:128]
    dcol_ref[...] = c2[0, :, 0:64] + c_halo[:, 64:128]

    @pl.when(a < 12)
    def _():
        await_bytes(sum_ref.at[core, pl.ds(0, 11)], rsem2.at[10])

    @pl.when(a >= 12)
    def _():
        await_bytes(sum_ref.at[core], rsem2.at[10])

    push(sum_ref.at[core], sum_ref.at[core], ssem2.at[11], rsem2.at[11], sibling)
    await_bytes(sum_ref.at[0], rsem2.at[11])

    await_bytes(halo.at[0], ssem.at[0])
    await_bytes(halo.at[1], ssem.at[1])
    await_bytes(cols.at[pl.ds(2, 31)], ssem.at[2])
    await_bytes(rows.at[1, pl.ds(0, 7)], ssem.at[3])
    await_bytes(side, ssem.at[4])
    await_bytes(rows.at[0], ssem.at[5])
    await_bytes(rows.at[2], ssem.at[6])
    await_bytes(cols.at[pl.ds(34, 2)], ssem.at[7])
    await_bytes(cols.at[pl.ds(0, 2)], ssem.at[8])
    await_bytes(g0, ssem2.at[0])
    await_bytes(c0, ssem2.at[1])
    await_bytes(c1.at[pl.ds(1, 3)], ssem2.at[3])
    await_bytes(r1.at[pl.ds(1, 3)], ssem2.at[4])
    await_bytes(c2.at[pl.ds(1, 3)], ssem2.at[6])
    await_bytes(r2.at[1], ssem2.at[7])
    await_bytes(r2.at[2], ssem2.at[8])
    await_bytes(c_halo, ssem2.at[9])
    await_bytes(sum_ref.at[0], ssem2.at[11])

    @pl.when(a < 12)
    def _():
        await_bytes(g1.at[pl.ds(0, 11)], ssem2.at[2])
        await_bytes(gz.at[pl.ds(0, 7)], ssem2.at[5])
        await_bytes(g1.at[pl.ds(1, 15)], ssem2.at[10])

    @pl.when(a >= 12)
    def _():
        await_bytes(g1.at[pl.ds(0, 12)], ssem2.at[2])


def main(dil, *arrays):
    vm = pl.BlockSpec(memory_space=VMEM)
    return pl.pallas_call(
        main_kernel,
        out_shape=(
            jax.ShapeDtypeStruct((64, 16, 256), BF16),
            jax.ShapeDtypeStruct((2, 12, 3, 16, 128), BF16),
            jax.ShapeDtypeStruct((2, 64), F32),
            jax.ShapeDtypeStruct((8, 64), F32),
        ),
        in_specs=[pl.BlockSpec(memory_space=pltpu.SMEM)] + [vm] * len(arrays),
        out_specs=(vm,) * 4,
        scratch_shapes=[
            VMEM((3, 8, 2, 256), F32),
            VMEM((36, 16, 128), BF16),
            VMEM((2, 8, 64, 256), BF16),
            VMEM((2, 3, 64, 128), BF16),
            VMEM((2, 64, 128), BF16),
            VMEM((2, 256), F32),
            VMEM((16, 128), BF16),
            VMEM((16, 64, 256), BF16),
            VMEM((128, 256), F32),
            VMEM((32, 192, 256), BF16),
            VMEM((32, 192, 256), BF16),
            VMEM((64, 4096), F32),
            VMEM((9, 64, 256), F32),
            VMEM((3, 64, 384), F32),
            VMEM((3, 64, 256), F32),
            VMEM((2, 12, 3, 16, 128), F32),
            VMEM((12, 3, 16, 128), F32),
            VMEM((12, 3, 16, 128), BF16),
            VMEM((16, 3, 16, 128), BF16),
            VMEM((8, 3, 16, 128), BF16),
            VMEM((2, 4, 4, 8, 128), F32),
            VMEM((4, 4, 8, 128), F32),
            VMEM((4, 4, 8, 128), F32),
            VMEM((4, 8, 128), F32),
            VMEM((8, 128), F32),
            VMEM((4, 2, 2, 128), F32),
            VMEM((4, 2, 2, 128), F32),
            VMEM((3, 2, 128), F32),
            pltpu.SemaphoreType.DMA((9,)),
            pltpu.SemaphoreType.DMA((9,)),
            pltpu.SemaphoreType.DMA((12,)),
            pltpu.SemaphoreType.DMA((12,)),
        ],
        compiler_params=pltpu.CompilerParams(
            collective_id=1, has_side_effects=True, vmem_limit_bytes=48 << 20
        ),
        name="main",
    )(dil, *arrays)


def finish_kernel(sums, drow, dcol, rproj, cproj, rp_ref, cp_ref, pair_ref, conv_ref, bias_ref, rf_ref, cf_ref):
    def pair_at(b):
        parts = []
        for j in range(4):
            tile = 4 * b + j
            parts.append(sums[tile // 36, (tile // 3) % 12, tile % 3].astype(F32))
        return jnp.concatenate(parts, axis=0)

    rp_ref[:, 0:128] = pair_at(0)
    rp_ref[:, 128:256] = pair_at(1)
    cp_ref[:, 0:128] = pair_at(2)
    cp_ref[:, 128:256] = pair_at(3)
    strips = [pair_at(4 + n) for n in range(9)]
    rest = []
    for n in range(5):
        both = pair_at(13 + n)
        rest += [both[:, 0:64], both[:, 64:128]]
    for k in range(3):
        for q in range(3):
            near = slice(q * 64, q * 64 + 64)
            pair_ref[k * 3 + q] = strips[k][:, near] if q < 2 else rest[k]
            pair_ref[9 + q * 3 + k] = strips[3 + k][:, near] if q < 2 else rest[3 + k]
            conv_ref[k * 3 + q] = strips[6 + k][:, near] if q < 2 else rest[6 + k]
    bias_ref[...] = rest[9][0:1]
    rf_ref[...] = times(drow[...].astype(BF16), rproj[...])
    cf_ref[...] = times(dcol[...].astype(BF16), cproj[...])


def finish(*arrays):
    vm = pl.BlockSpec(memory_space=VMEM)
    shapes = ((64, 256), (64, 256), (18, 64, 64), (9, 64, 64), (1, 64), (2, 256), (8, 256))
    return pl.pallas_call(
        finish_kernel,
        out_shape=tuple(jax.ShapeDtypeStruct(s, F32) for s in shapes),
        in_specs=[vm] * len(arrays),
        out_specs=(vm,) * len(shapes),
        compiler_params=pltpu.CompilerParams(vmem_limit_bytes=24 << 20),
        name="finish",
    )(*arrays)


def shards(
    row_features,
    col_features,
    row_proj,
    col_proj,
    pair_weight,
    pair_bias,
    conv_weight,
    dilations,
    cotangent,
):
    cot_t = jnp.swapaxes(cotangent, 0, 1)
    row_w, col_w = row_proj.T, col_proj.T
    out_t, sums, own_rows, own_cols = main(
        dilations, row_features, col_features, row_w, col_w, pair_weight,
        pair_bias.reshape(1, 64), conv_weight, cot_t,
    )
    row_g, col_g, pair, conv, bias, row_f, col_f = finish(sums, own_rows, own_cols, row_w, col_w)
    return (
        out_t,
        row_f,
        col_f,
        row_g.T,
        col_g.T,
        pair.reshape(2, 3, 3, 64, 64),
        bias.reshape(64),
        conv.reshape(3, 3, 64, 64),
    )


def solution(mesh):
    return jax.shard_map(
        shards,
        mesh=mesh,
        in_specs=(
            P(("row", "col"), None),
            P(("col", "row"), None),
            P(),
            P(),
            P(),
            P(),
            P(),
            P(),
            P(None, "row", "col"),
        ),
        out_specs=(
            P(None, "row", "col"),
            P(("row", "col"), None),
            P(("col", "row"), None),
            P(),
            P(),
            P(),
            P(),
            P(),
        ),
        check_vma=False,
    )
```

```python
import functools

import jax
import jax.numpy as jnp
from jax import lax
from jax.experimental import pallas as pl
from jax.experimental.pallas import tpu as pltpu
from jax.sharding import PartitionSpec as P

MAX_DILATION = 8
MESH = pl.DeviceIdType.MESH
VMEM = pltpu.VMEM


def places():
    r = lax.axis_index("row")
    c = lax.axis_index("col")
    return r, c, r // 8, lax.rem(r // 2, 4), lax.rem(r, 2), c // 2, lax.rem(c, 2)


def device_at(z_hi, x, core, y, z_lo):
    return ((z_hi * 4 + x) * 2 + core, y * 2 + z_lo)


def signal(barrier, target):
    pl.semaphore_signal(barrier, inc=1, device_id=target, device_id_type=MESH)


def push(src, dst, send_sem, recv_sem, target):
    pltpu.make_async_remote_copy(
        src_ref=src,
        dst_ref=dst,
        send_sem=send_sem,
        recv_sem=recv_sem,
        device_id=target,
        device_id_type=MESH,
    ).start()


def await_bytes(ref, sem):
    pltpu.make_async_copy(ref, ref, sem).wait()


FAR = -1e9
F32 = jnp.float32
BF16 = jnp.bfloat16


def times(a, b):
    return jnp.dot(a, b, preferred_element_type=F32)


def times_t(a, b):
    return lax.dot_general(a, b, (((1,), (1,)), ((), ())), preferred_element_type=F32)


def halves(v):
    hi = v.astype(BF16)
    return hi, (v - hi.astype(F32)).astype(BF16)


def turned(v, back):
    n = v.shape[1]
    return pltpu.roll(v, lax.rem(n - back, n), 1)


def lanes(rows, n):
    return lax.broadcasted_iota(jnp.int32, (rows, n), 1)


def main_kernel(
    dil, rf, cf, rproj, cproj, pw, bias, cw, cot,
    out_ref, sum_ref, drow_ref, dcol_ref,
    rows, cols, halo, side, pack, rf_wide, cf_tall,
    mix, fr, h3, c3, gs, vt, st, cs,
    g, g0, red, g1, gz, pc, c0, c1, c2, c_halo, pr, r1, r2,
    ssem, rsem, ssem2, rsem2,
):
    d1 = dil[0]
    d2 = dil[1]
    r, c, z_hi, x, core, y, z_lo = places()
    row0 = r * 16
    col0 = c * 256
    up, down = lax.rem(r + 31, 32), lax.rem(r + 1, 32)
    left, right = lax.rem(c + 7, 8), lax.rem(c + 1, 8)
    a = x * 4 + y
    z = z_hi * 2 + z_lo
    sibling = device_at(z_hi, x, 1 - core, y, z_lo)

    def plane(t):
        other = lax.rem(a + t, 16)
        return other, device_at(z_hi, other // 4, core, lax.rem(other, 4), z_lo)

    def along_z(t):
        other = lax.rem(z + t, 8)
        return device_at(other // 2, x, core, y, lax.rem(other, 2))

    barrier = pltpu.get_barrier_semaphore()

    @pl.loop(12, 43)
    def _(t):
        signal(barrier, (lax.rem(r + t + t // 32, 32), c))

    @pl.loop(1, 8)
    def _(t):
        signal(barrier, (r, lax.rem(c + t, 8)))

    for r_to in (up, down):
        for c_to in (left, right):
            signal(barrier, (r_to, c_to))
    for dx in range(1, 4):
        for dy in range(1, 4):
            signal(barrier, device_at(z_hi, lax.rem(x + dx, 4), core, lax.rem(y + dy, 4), z_lo))
    for dz in range(1, 4):
        signal(barrier, device_at(lax.rem(z_hi + dz, 4), x, core, y, 1 - z_lo))

    own_rf = rf[...].astype(F32)
    rf_wide[...] = own_rf
    rows[1, c] = own_rf
    own_cf = cf[...].astype(F32)
    own_cf = jnp.concatenate([own_cf[:, 0:128], own_cf[:, 128:256]], axis=0).astype(BF16)
    cf_tall[...] = own_cf
    cols[r + 2] = own_cf
    pl.semaphore_wait(barrier, 31 + 7 + 4 + 9 + 3)

    @pl.loop(12, 43)
    def _(t):
        push(cf_tall, cols.at[r + 2], ssem.at[2], rsem.at[2], (lax.rem(r + t + t // 32, 32), c))

    @pl.loop(1, 8)
    def _(t):
        push(rf_wide, rows.at[1, c], ssem.at[3], rsem.at[3], (r, lax.rem(c + t, 8)))

    group = lanes(64, 128) // 8
    first = jnp.zeros((64, 128), jnp.float32)
    last = jnp.zeros((64, 128), jnp.float32)
    for i in range(16):
        head = cot[i, :, 0:128].astype(jnp.float32)
        tail = cot[i, :, 128:256].astype(jnp.float32)
        first = jnp.where(group == i, pltpu.roll(head, 8 * i, 1) if i else head, first)
        last = jnp.where(group == i, pltpu.roll(tail, (8 * i + 8) % 128, 1) if i < 15 else tail, last)
    pack[0] = first.astype(jnp.bfloat16)
    pack[1] = last.astype(jnp.bfloat16)
    for slot, r_to in ((2, up), (1, r), (0, down)):
        push(pack.at[0], side.at[1, slot], ssem.at[4], rsem.at[4], (r_to, left))
        push(pack.at[1], side.at[0, slot], ssem.at[4], rsem.at[4], (r_to, right))

    pw0 = jnp.concatenate(
        [jnp.concatenate([pw[0, k, q] for q in range(3)], axis=1) for k in range(3)], axis=0
    )
    pw1 = jnp.concatenate(
        [jnp.concatenate([pw[1, k, q] for k in range(3)], axis=1) for q in range(3)], axis=0
    )
    wf = [cw[k].reshape(192, 64).T for k in range(3)]
    wb = [jnp.concatenate([cw[k, q] for q in range(3)], axis=1) for k in range(3)]
    lane = lanes(64, 128)

    def taps(v, offset):
        return jnp.concatenate([turned(v, offset + (k - 1) * d1) for k in range(3)], axis=0).astype(BF16)

    def cotangent_row(e):
        if e < 8:
            x0, x1, slot, n = halo[0, e, :, 0:128], halo[0, e, :, 128:256], 0, 8 + e
        elif e < 24:
            x0, x1, slot, n = cot[e - 8, :, 0:128], cot[e - 8, :, 128:256], 1, e - 8
        else:
            x0, x1, slot, n = halo[1, e - 24, :, 0:128], halo[1, e - 24, :, 128:256], 2, e - 24
        i = row0 - 8 + e
        ok = (i >= 0) & (i < 512)
        before = side[0, slot]
        after = side[1, slot]
        if slot != 1:
            keep = jnp.where(ok, 1.0, 0.0).astype(BF16)
            x0, x1 = x0 * keep, x1 * keep
        before = before * jnp.where(ok & (c > 0), 1.0, 0.0).astype(BF16)
        after = after * jnp.where(ok & (c < 7), 1.0, 0.0).astype(BF16)
        low, high = slice(0, 128), slice(128, 256)
        c3[e, 64:128, low] = x0
        c3[e, 64:128, high] = x1
        r0 = pltpu.roll(x0, d2, 1)
        r1 = pltpu.roll(x1, d2, 1)
        rp = pltpu.roll(before, lax.rem(120 - 8 * n + d2 + 128, 128), 1)
        c3[e, 128:192, low] = jnp.where(lane < d2, rp, r0)
        c3[e, 128:192, high] = jnp.where(lane < d2, r0, r1)
        l0 = pltpu.roll(x0, 128 - d2, 1)
        l1 = pltpu.roll(x1, 128 - d2, 1)
        rn = pltpu.roll(after, lax.rem(256 - 8 * n - d2, 128), 1)
        c3[e, 0:64, low] = jnp.where(lane >= 128 - d2, l1, l0)
        c3[e, 0:64, high] = jnp.where(lane >= 128 - d2, rn, l1)

    await_bytes(rows.at[1, pl.ds(0, 7)], rsem.at[3])
    push(rows.at[1], rows.at[0], ssem.at[5], rsem.at[5], (down, c))
    push(rows.at[1], rows.at[2], ssem.at[6], rsem.at[6], (up, c))
    push(cot.at[pl.ds(8, 8)], halo.at[0], ssem.at[0], rsem.at[0], (down, c))
    push(cot.at[pl.ds(0, 8)], halo.at[1], ssem.at[1], rsem.at[1], (up, c))
    await_bytes(side, rsem.at[4])
    for e in range(8, 24):
        cotangent_row(e)
    await_bytes(cols.at[pl.ds(2, 31)], rsem.at[2])
    push(cols.at[pl.ds(2, 2)], cols.at[pl.ds(34, 2)], ssem.at[7], rsem.at[7], (r, left))
    push(cols.at[pl.ds(32, 2)], cols.at[pl.ds(0, 2)], ssem.at[8], rsem.at[8], (r, right))

    await_bytes(rows.at[0], rsem.at[5])
    await_bytes(rows.at[2], rsem.at[6])
    fr[...] = jnp.zeros((128, 256), F32)
    for m in range(3):
        for n in range(8):
            fr[m * 16 + 2 * n : m * 16 + 2 * n + 2, :] = rows[m, n]
    at = row0 - 16 + lax.broadcasted_iota(jnp.int32, (128, 256), 0)
    feat_r = jnp.where((at >= 0) & (at < 512), fr[...], 0.0).astype(BF16)
    a_t = times_t(rproj[...], feat_r).astype(BF16).astype(F32)
    rt = times(pw0.T, taps(a_t, 8)) * 0.5
    rt0, rt2 = rt[0:64], rt[128:192]
    rsum = rt0 + rt[64:128] + rt2
    bias_col = jnp.broadcast_to(bias[...] * 0.5, (8, 64)).T[:, 0:1]
    await_bytes(cols.at[pl.ds(34, 2)], rsem.at[7])
    await_bytes(cols.at[pl.ds(0, 2)], rsem.at[8])
    wide = cols[...].astype(F32)
    feat_c = jnp.concatenate([wide[:, :8].reshape(288, 128), wide[:, 8:].reshape(288, 128)], axis=1)
    at = col0 - 16 + lax.broadcasted_iota(jnp.int32, (288, 256), 0)
    feat_c = jnp.where((at >= 0) & (at < 2048), feat_c, 0.0)
    feat_c = jnp.concatenate([feat_c, jnp.zeros((96, 256), F32)], axis=0).astype(BF16)
    b_t = times_t(cproj[...], feat_c).astype(BF16).astype(F32)
    ct = times(pw1.T, taps(b_t, 8)) * 0.5
    at = col0 - 8 + lanes(64, 384)
    base = ct[64:128] + bias_col + jnp.where((at >= 0) & (at < 2048), 0.0, FAR)
    sums = (base + ct[128:192], base + ct[0:64] + ct[128:192], base + ct[0:64])
    for case in range(3):
        st[case] = sums[case]
        vt[case * 3 + 1] = turned(sums[case], 8)[:, 0:256]
    near, far = [], []
    for q in range(3):
        at = col0 + (q - 1) * d2 + lanes(1, 256)
        near.append(jnp.where(at - d1 < 0, 1.0, 0.0))
        far.append(jnp.where(at + d1 >= 2048, 1.0, 0.0))

    def hidden_row(e, taps_here):
        i = row0 - 8 + e
        case = jnp.where(i - d1 < 0, 0, jnp.where(i + d1 >= 512, 2, 1))
        gate = jnp.where((i >= 0) & (i < 512), 0.0, FAR)
        all_e = rsum[:, e : e + 1] + gate
        rt0_e = rt0[:, e : e + 1]
        rt2_e = rt2[:, e : e + 1]
        for q in taps_here:
            h = vt[case * 3 + q] + all_e - near[q] * rt0_e - far[q] * rt2_e
            t = jnp.tanh(h)
            h3[e, q * 64 : (q + 1) * 64, :] = (h + h * t).astype(BF16)
            if q == 1 and 8 <= e < 24:
                gs[:, (e - 8) * 256 : (e - 7) * 256] = 0.5 + 0.5 * t + h * (0.5 - 0.5 * t * t)

    for e in range(8, 24):
        hidden_row(e, (1,))

    await_bytes(halo.at[0], rsem.at[0])
    await_bytes(halo.at[1], rsem.at[1])
    for e in range(8):
        cotangent_row(e)
        cotangent_row(24 + e)
    live = [1.0 - near[1], None, 1.0 - far[1]]
    rs = [jnp.zeros((64, 128), F32) for _ in range(3)]
    gc = [jnp.zeros((192, 64), F32) for _ in range(3)]
    cs[...] = jnp.zeros((3, 64, 256), F32)
    for i in range(16):
        own = h3[8 + i, 64:128, :]
        d = cot[i].astype(F32)
        for k in range(3):
            grads = c3[8 + i - (k - 1) * d2]
            d = d + times(wb[k], grads)
            gc[k] = gc[k] + times_t(grads, own)
        d = d * gs[:, i * 256 : (i + 1) * 256]
        cs[1] = cs[1] + d
        cs[0] = cs[0] + d * jnp.where(row0 + i - d1 >= 0, 1.0, 0.0)
        cs[2] = cs[2] + d * jnp.where(row0 + i + d1 < 512, 1.0, 0.0)
        for q in range(3):
            part = d if live[q] is None else d * live[q]
            rs[q] = jnp.where(lane == i, jnp.sum(part, axis=1, keepdims=True), rs[q])

    rs_hi, rs_lo = halves(jnp.concatenate(rs, axis=0))
    cs_hi, cs_lo = halves(cs[...].reshape(192, 256))
    br = times(pw0, rs_hi) + times(pw0, rs_lo)
    bc = times(pw1, cs_hi) + times(pw1, cs_lo)
    bc = jnp.concatenate([bc, jnp.zeros((192, 128), F32)], axis=1)
    dr = sum(pltpu.roll(br[k * 64 : (k + 1) * 64], 16 + (k - 1) * d1, 1) for k in range(3))
    dc = sum(pltpu.roll(bc[q * 64 : (q + 1) * 64], 16 + (q - 1) * d1, 1) for q in range(3))
    at = row0 - 16 + lane
    dr = jnp.where((at >= 0) & (at < 512), dr, 0.0)
    at = col0 - 16 + lanes(64, 384)
    dc = jnp.where((at >= 0) & (at < 2048), dc, 0.0)
    dr_hi, dr_lo = halves(dr)
    dc_hi, dc_lo = halves(dc)
    row_proj_g = times(dr_hi, feat_r) + times(dr_lo, feat_r)
    col_proj_g = times(dc_hi, feat_c) + times(dc_lo, feat_c)
    a_own = taps(a_t, 16)
    b_own = taps(b_t, 16)[:, 0:256]
    p0 = times_t(a_own, rs_hi) + times_t(a_own, rs_lo)
    p1 = times_t(b_own, cs_hi) + times_t(b_own, cs_lo)
    bias_g = jnp.broadcast_to(jnp.sum(cs[1], axis=1, keepdims=True), (64, 64)).T

    strips = [p0[k * 64 : (k + 1) * 64] for k in range(3)]
    strips += [p1[q * 64 : (q + 1) * 64] for q in range(3)] + [part.T for part in gc]
    pairs = [row_proj_g[:, 0:128], row_proj_g[:, 128:256], col_proj_g[:, 0:128], col_proj_g[:, 128:256]]
    pairs += [strip[:, 0:128] for strip in strips]
    rest = [strip[:, 128:192] for strip in strips] + [bias_g]
    pairs += [jnp.concatenate([rest[2 * n], rest[2 * n + 1]], axis=1) for n in range(5)]
    for b in range(18):
        for j in range(4):
            tile = 4 * b + j
            g[tile // 36, (tile // 3) % 12, tile % 3] = pairs[b][16 * j : 16 * j + 16]

    dr_p = dr.T
    dc_p = dc.T
    for n in range(32):
        if n == 0:
            extra = dc_p[272:280]
        elif n == 31:
            extra = dc_p[8:16]
        else:
            extra = jnp.zeros((8, 64), F32)
        pc[n % 2, (n // 2) % 4, n // 8] = jnp.concatenate([dc_p[16 + 8 * n : 24 + 8 * n], extra], axis=1)
    for n in range(8):
        h = 32 + 2 * n if n < 4 else 2 * n
        pr[n // 2, n % 2] = jnp.concatenate([dr_p[16 + 2 * n : 18 + 2 * n], dr_p[h : h + 2]], axis=1)

    row_to = jnp.where(c < 4, down, up)
    col_to = jnp.where(r < 16, right, left)
    push(g.at[1 - core], g0, ssem2.at[0], rsem2.at[0], sibling)
    push(pc.at[1 - core], c0, ssem2.at[1], rsem2.at[1], sibling)
    for t in range(1, 4):
        y_to = lax.rem(y + t, 4)
        push(pr.at[y_to], r1.at[t], ssem2.at[4], rsem2.at[4], device_at(z_hi, x, core, y_to, z_lo))
    await_bytes(g0, rsem2.at[0])
    red[...] = (g[core] + g0[...]).astype(BF16)

    @pl.loop(6, 21)
    def _(u):
        t = lax.rem(u + u // 16, 16)
        other, target = plane(t)

        @pl.when(other < 12)
        def _():
            push(red.at[other], g1.at[t], ssem2.at[2], rsem2.at[2], target)

    await_bytes(c0, rsem2.at[1])
    c0[...] = c0[...] + pc[core]
    for t in range(1, 4):
        x_to = lax.rem(x + t, 4)
        push(c0.at[x_to], c1.at[t], ssem2.at[3], rsem2.at[3], device_at(z_hi, x_to, core, y, z_lo))
    for case in range(3):
        for q in (0, 2):
            vt[case * 3 + q] = turned(st[case], 8 + (q - 1) * d2)[:, 0:256]
    for e in range(32):
        hidden_row(e, (0, 2) if 8 <= e < 24 else (0, 1, 2))

    await_bytes(r1.at[pl.ds(1, 3)], rsem2.at[4])
    r1[0] = pr[y] + r1[1] + r1[2] + r1[3]

    @pl.when(a < 12)
    def _():
        await_bytes(g1.at[pl.ds(1, 15)], rsem2.at[2])
        mine = g[core, a] + g0[a]
        for t in range(1, 16):
            mine = mine + g1[t].astype(F32)
        gz[z] = mine.astype(BF16)

        @pl.loop(3, 10)
        def _(u):
            t = lax.rem(u + u // 8, 8)
            push(gz.at[z], gz.at[z], ssem2.at[5], rsem2.at[5], along_z(t))

    await_bytes(c1.at[pl.ds(1, 3)], rsem2.at[3])
    c1[0] = c0[x] + c1[1] + c1[2] + c1[3]
    for t in range(1, 4):
        z_to = lax.rem(z_hi + t, 4)
        push(c1.at[0, z_to], c2.at[t], ssem2.at[6], rsem2.at[6], device_at(z_to, x, core, y, z_lo))
    push(r1.at[0, 1 - z_lo], r2.at[1], ssem2.at[7], rsem2.at[7], device_at(z_hi, x, core, y, 1 - z_lo))

    for i in range(16):
        mixed = h3[8 + i, 64:128, :].astype(F32)
        for k in range(3):
            mixed = mixed + times(wf[k], h3[8 + i + (k - 1) * d2])
        mix[i] = mixed.astype(BF16)

    @pl.when(a < 12)
    def _():
        await_bytes(gz.at[pl.ds(0, 7)], rsem2.at[5])
        whole = gz[0].astype(F32)
        for t in range(1, 8):
            whole = whole + gz[t].astype(F32)
        sum_ref[core, a] = whole.astype(BF16)

        @pl.loop(6, 21)
        def _(u):
            t = lax.rem(u + u // 16, 16)
            push(sum_ref.at[core, a], sum_ref.at[core, a], ssem2.at[10], rsem2.at[10], plane(t)[1])

    out_ref[...] = jnp.swapaxes(mix[...], 0, 1)
    await_bytes(c2.at[pl.ds(1, 3)], rsem2.at[6])
    await_bytes(r2.at[1], rsem2.at[7])
    c2[0] = c1[0, z_hi] + c2[1] + c2[2] + c2[3]
    r2[0] = r1[0, z_lo] + r2[1]
    push(r2.at[0], r2.at[2], ssem2.at[8], rsem2.at[8], (row_to, c))
    push(c2.at[0], c_halo, ssem2.at[9], rsem2.at[9], (r, col_to))
    await_bytes(r2.at[2], rsem2.at[8])
    await_bytes(c_halo, rsem2.at[9])
    drow_ref[...] = r2[0, :, 0:64] + r2[2, :, 64:128]
    dcol_ref[...] = c2[0, :, 0:64] + c_halo[:, 64:128]

    @pl.when(a < 12)
    def _():
        await_bytes(sum_ref.at[core, pl.ds(0, 11)], rsem2.at[10])

    @pl.when(a >= 12)
    def _():
        await_bytes(sum_ref.at[core], rsem2.at[10])

    push(sum_ref.at[core], sum_ref.at[core], ssem2.at[11], rsem2.at[11], sibling)
    await_bytes(sum_ref.at[0], rsem2.at[11])

    await_bytes(halo.at[0], ssem.at[0])
    await_bytes(halo.at[1], ssem.at[1])
    await_bytes(cols.at[pl.ds(2, 31)], ssem.at[2])
    await_bytes(rows.at[1, pl.ds(0, 7)], ssem.at[3])
    await_bytes(side, ssem.at[4])
    await_bytes(rows.at[0], ssem.at[5])
    await_bytes(rows.at[2], ssem.at[6])
    await_bytes(cols.at[pl.ds(34, 2)], ssem.at[7])
    await_bytes(cols.at[pl.ds(0, 2)], ssem.at[8])
    await_bytes(g0, ssem2.at[0])
    await_bytes(c0, ssem2.at[1])
    await_bytes(c1.at[pl.ds(1, 3)], ssem2.at[3])
    await_bytes(r1.at[pl.ds(1, 3)], ssem2.at[4])
    await_bytes(c2.at[pl.ds(1, 3)], ssem2.at[6])
    await_bytes(r2.at[1], ssem2.at[7])
    await_bytes(r2.at[2], ssem2.at[8])
    await_bytes(c_halo, ssem2.at[9])
    await_bytes(sum_ref.at[0], ssem2.at[11])

    @pl.when(a < 12)
    def _():
        await_bytes(g1.at[pl.ds(0, 11)], ssem2.at[2])
        await_bytes(gz.at[pl.ds(0, 7)], ssem2.at[5])
        await_bytes(g1.at[pl.ds(1, 15)], ssem2.at[10])

    @pl.when(a >= 12)
    def _():
        await_bytes(g1.at[pl.ds(0, 12)], ssem2.at[2])


def main(dil, *arrays):
    vm = pl.BlockSpec(memory_space=VMEM)
    return pl.pallas_call(
        main_kernel,
        out_shape=(
            jax.ShapeDtypeStruct((64, 16, 256), BF16),
            jax.ShapeDtypeStruct((2, 12, 3, 16, 128), BF16),
            jax.ShapeDtypeStruct((2, 64), F32),
            jax.ShapeDtypeStruct((8, 64), F32),
        ),
        in_specs=[pl.BlockSpec(memory_space=pltpu.SMEM)] + [vm] * len(arrays),
        out_specs=(vm,) * 4,
        scratch_shapes=[
            VMEM((3, 8, 2, 256), F32),
            VMEM((36, 16, 128), BF16),
            VMEM((2, 8, 64, 256), BF16),
            VMEM((2, 3, 64, 128), BF16),
            VMEM((2, 64, 128), BF16),
            VMEM((2, 256), F32),
            VMEM((16, 128), BF16),
            VMEM((16, 64, 256), BF16),
            VMEM((128, 256), F32),
            VMEM((32, 192, 256), BF16),
            VMEM((32, 192, 256), BF16),
            VMEM((64, 4096), F32),
            VMEM((9, 64, 256), F32),
            VMEM((3, 64, 384), F32),
            VMEM((3, 64, 256), F32),
            VMEM((2, 12, 3, 16, 128), F32),
            VMEM((12, 3, 16, 128), F32),
            VMEM((12, 3, 16, 128), BF16),
            VMEM((16, 3, 16, 128), BF16),
            VMEM((8, 3, 16, 128), BF16),
            VMEM((2, 4, 4, 8, 128), F32),
            VMEM((4, 4, 8, 128), F32),
            VMEM((4, 4, 8, 128), F32),
            VMEM((4, 8, 128), F32),
            VMEM((8, 128), F32),
            VMEM((4, 2, 2, 128), F32),
            VMEM((4, 2, 2, 128), F32),
            VMEM((3, 2, 128), F32),
            pltpu.SemaphoreType.DMA((9,)),
            pltpu.SemaphoreType.DMA((9,)),
            pltpu.SemaphoreType.DMA((12,)),
            pltpu.SemaphoreType.DMA((12,)),
        ],
        compiler_params=pltpu.CompilerParams(
            collective_id=1, has_side_effects=True, vmem_limit_bytes=48 << 20
        ),
        name="main",
    )(dil, *arrays)


def finish_kernel(sums, drow, dcol, rproj, cproj, rp_ref, cp_ref, pair_ref, conv_ref, bias_ref, rf_ref, cf_ref):
    def pair_at(b):
        parts = []
        for j in range(4):
            tile = 4 * b + j
            parts.append(sums[tile // 36, (tile // 3) % 12, tile % 3].astype(F32))
        return jnp.concatenate(parts, axis=0)

    rp_ref[:, 0:128] = pair_at(0)
    rp_ref[:, 128:256] = pair_at(1)
    cp_ref[:, 0:128] = pair_at(2)
    cp_ref[:, 128:256] = pair_at(3)
    strips = [pair_at(4 + n) for n in range(9)]
    rest = []
    for n in range(5):
        both = pair_at(13 + n)
        rest += [both[:, 0:64], both[:, 64:128]]
    for k in range(3):
        for q in range(3):
            near = slice(q * 64, q * 64 + 64)
            pair_ref[k * 3 + q] = strips[k][:, near] if q < 2 else rest[k]
            pair_ref[9 + q * 3 + k] = strips[3 + k][:, near] if q < 2 else rest[3 + k]
            conv_ref[k * 3 + q] = strips[6 + k][:, near] if q < 2 else rest[6 + k]
    bias_ref[...] = rest[9][0:1]
    rf_ref[...] = times(drow[...].astype(BF16), rproj[...])
    cf_ref[...] = times(dcol[...].astype(BF16), cproj[...])


def finish(*arrays):
    vm = pl.BlockSpec(memory_space=VMEM)
    shapes = ((64, 256), (64, 256), (18, 64, 64), (9, 64, 64), (1, 64), (2, 256), (8, 256))
    return pl.pallas_call(
        finish_kernel,
        out_shape=tuple(jax.ShapeDtypeStruct(s, F32) for s in shapes),
        in_specs=[vm] * len(arrays),
        out_specs=(vm,) * len(shapes),
        compiler_params=pltpu.CompilerParams(vmem_limit_bytes=24 << 20),
        name="finish",
    )(*arrays)


def shards(
    row_features,
    col_features,
    row_proj,
    col_proj,
    pair_weight,
    pair_bias,
    conv_weight,
    dilations,
    cotangent,
):
    cot_t = jnp.swapaxes(cotangent, 0, 1)
    row_w, col_w = row_proj.T, col_proj.T
    out_t, sums, own_rows, own_cols = main(
        dilations, row_features, col_features, row_w, col_w, pair_weight,
        pair_bias.reshape(1, 64), conv_weight, cot_t,
    )
    row_g, col_g, pair, conv, bias, row_f, col_f = finish(sums, own_rows, own_cols, row_w, col_w)
    return (
        out_t,
        row_f,
        col_f,
        row_g.T,
        col_g.T,
        pair.reshape(2, 3, 3, 64, 64),
        bias.reshape(64),
        conv.reshape(3, 3, 64, 64),
    )


def solution(mesh):
    return jax.shard_map(
        shards,
        mesh=mesh,
        in_specs=(
            P(("row", "col"), None),
            P(("col", "row"), None),
            P(),
            P(),
            P(),
            P(),
            P(),
            P(),
            P(None, "row", "col"),
        ),
        out_specs=(
            P(None, "row", "col"),
            P(("row", "col"), None),
            P(("col", "row"), None),
            P(),
            P(),
            P(),
            P(),
            P(),
        ),
        check_vma=False,
    )
```
